32 devices in a mesh: ctx: 4 (over z), fsdp: 8 (over y, x, core).
Axes of the slice: x: 2, y: 2, z: 4, core: 2. Of those that a mesh axis runs over, the one named last changes fastest.
Arguments:
- tokens: bfloat16 [8, 512, 1600], P('fsdp', 'ctx'), may hold values from -6 to 6
- cotangent: bfloat16 [8, 512, 1600], P('fsdp', 'ctx'), may hold values from -6 to 6
- doc_lengths: int32 [8, 3], P('fsdp'), may hold values from 1 to 385, 512 in all within a row
- meta_tokens: bfloat16 [128, 1600], P('fsdp'), may hold values from -6 to 6
- norm_gain: bfloat16 [1600], P('fsdp'), may hold values from 0.5 to 1.5
- w_query: bfloat16 [1600, 1600], P('fsdp'), may hold values from -0.15625 to 0.15625
- w_keyval: bfloat16 [1600, 640], P('fsdp'), may hold values from -0.15625 to 0.15625
- w_attn_out: bfloat16 [1600, 1600], P('fsdp'), may hold values from -0.15625 to 0.15625
- w_mixer_in: bfloat16 [1600, 6400], P('fsdp'), may hold values from -0.15625 to 0.15625
- conv_taps: bfloat16 [4, 3200], P(None, 'fsdp'), may hold values from -3 to 3
- conv_bias: bfloat16 [3200], P('fsdp'), may hold values from -3 to 3
- w_select: bfloat16 [3200, 132], P('fsdp'), may hold values from -0.109375 to 0.109375
- w_step: bfloat16 [100, 3200], P(None, 'fsdp'), may hold values from -0.625 to 0.625
- step_bias: bfloat16 [3200], P('fsdp'), may hold values from -1.5 to 0.5
- log_rates: bfloat16 [16, 3200], P(None, 'fsdp'), may hold values from -6 to -2.5
- skip_gain: bfloat16 [3200], P('fsdp'), may hold values from 0.5 to 1.5
- w_mixer_out: bfloat16 [3200, 1600], P('fsdp'), may hold values from -0.109375 to 0.109375
- attn_gain: bfloat16 [1600], P('fsdp'), may hold values from 0.5 to 1.5
- ssm_gain: bfloat16 [1600], P('fsdp'), may hold values from 0.5 to 1.5
- ffn_norm_gain: bfloat16 [1600], P('fsdp'), may hold values from 0.5 to 1.5
- w_gate_up: bfloat16 [1600, 11008], P('fsdp'), may hold values from -0.15625 to 0.15625
- w_down: bfloat16 [5504, 1600], P('fsdp'), may hold values from -0.078125 to 0.078125
Outputs:
- block_out: bfloat16 [8, 512, 1600], P('fsdp', 'ctx')
- grad_tokens: float32 [8, 512, 1600], P('fsdp', 'ctx')
- grad_meta_tokens: float32 [128, 1600], P('fsdp')
- grad_norm_gain: float32 [1600], P('fsdp')
- grad_w_query: float32 [1600, 1600], P('fsdp')
- grad_w_keyval: float32 [1600, 640], P('fsdp')
- grad_w_attn_out: float32 [1600, 1600], P('fsdp')
- grad_w_mixer_in: float32 [1600, 6400], P('fsdp')
- grad_conv_taps: float32 [4, 3200], P(None, 'fsdp')
- grad_conv_bias: float32 [3200], P('fsdp')
- grad_w_select: float32 [3200, 132], P('fsdp')
- grad_w_step: float32 [100, 3200], P(None, 'fsdp')
- grad_step_bias: float32 [3200], P('fsdp')
- grad_log_rates: float32 [16, 3200], P(None, 'fsdp')
- grad_skip_gain: float32 [3200], P('fsdp')
- grad_w_mixer_out: float32 [3200, 1600], P('fsdp')
- grad_attn_gain: float32 [1600], P('fsdp')
- grad_ssm_gain: float32 [1600], P('fsdp')
- grad_ffn_norm_gain: float32 [1600], P('fsdp')
- grad_w_gate_up: float32 [1600, 11008], P('fsdp')
- grad_w_down: float32 [5504, 1600], P('fsdp')
The draws below stay inside these ranges and needn't reach their ends.
Inputs may be any that keep to these rules, and one draw needn't show every extreme that they name: `doc_lengths`: each sequence's 3 lengths sum to 512; the longest is exactly 385.
All inputs are finite; a program needn't handle non-finite values.
Results may differ from the reference program's by a relative error of at most 0.025.
Values may be sent and summed in bfloat16 or wider, within the bound.
A program may use at most 640 MiB of HBM per device.

```python
import math
import jax
import jax.numpy as jnp
import numpy as np
from jax import lax

D = 1600
HEADS = 25
KV_HEADS = 5
HEAD = 64
META = 128
INNER = 3200
STATE = 16
CONV = 4
DT_RANK = 100
FF = 5504
TOK_DEV = 128
DOCS = 3
LENGTH = 512
SEQS = 8


def block_scale(own_key, shape, shards, least, largest):
    level, own = 1.0, jax.random.fold_in(own_key, 6)
    for dim, parts in shards:
        draws = jnp.exp(jax.random.uniform(jax.random.fold_in(own, dim), (parts,), jnp.float32, least / len(shards), largest / len(shards)))
        level = level * jnp.repeat(draws, shape[dim] // parts).reshape([-1 if axis == dim else 1 for axis in range(len(shape))])
    return level


def length_profile(number_of, total, most, slope):
    portions = [(1 << 20) // math.isqrt(rank ** slope) + 1 for rank in range(2, number_of + 1)]
    surplus, counts = total - most - (number_of - 1), [1] * (number_of - 1)
    while surplus > 0:
        movable = [i for i in range(number_of - 1) if counts[i] < most]
        whole, remaining = sum([portions[i] for i in movable]), surplus
        for i in movable:
            extra = min(most - counts[i], max(1, remaining * portions[i] // whole), surplus)
            counts[i] = counts[i] + extra
            surplus = surplus - extra
    return np.array([most] + counts)


def ragged_sizes(stream_key, number_of, total, bound, slope):
    if number_of == 2:
        one = jax.random.randint(stream_key, (), max(1, total - bound), min(bound, total - 1) + 1)
        return jnp.stack([one, total - one])
    sizes = jnp.asarray(length_profile(number_of, total, bound, slope), jnp.int32)
    pairs = (number_of - 1) // 2
    donor, taker = sizes[1:1 + 2 * pairs:2], sizes[2:2 + 2 * pairs:2]
    margin = jnp.minimum(donor - 1, bound - taker)
    moved = jax.random.randint(jax.random.fold_in(stream_key, 1), (pairs,), 0, 1 << 20) % (margin + 1)
    sizes = sizes.at[1:1 + 2 * pairs:2].set(donor - moved).at[2:2 + 2 * pairs:2].set(taker + moved)
    return sizes[jax.random.permutation(jax.random.fold_in(stream_key, 2), number_of)]


def noise(own_key, shape, width, most, split=(), kind=jnp.bfloat16):
    factor_of = block_scale(own_key, shape, split, -0.22, 0.18) if split else 1.0
    array = jax.random.normal(own_key, shape, jnp.float32) * width * factor_of
    return jnp.minimum(jnp.maximum(array, -most), most).astype(kind)


def setup_inputs(seed: int = 0) -> dict:
    key_list = jax.random.split(jax.random.key(seed), 23)
    tokens = noise(key_list[0], (SEQS, LENGTH, D), 1.0, 6.0, ((0, 8), (1, 4)))
    cotangent = noise(key_list[1], (SEQS, LENGTH, D), 1.0, 6.0, ((0, 8), (1, 4)))
    doc_lengths = jax.vmap(lambda own: ragged_sizes(own, DOCS, LENGTH, LENGTH - TOK_DEV + 1, 0))(jax.random.split(key_list[2], SEQS)).reshape((SEQS, DOCS)).astype(jnp.int32)
    meta_tokens = noise(key_list[3], (META, D), 1.0, 6.0, ((0, 8),))
    norm_gain = jnp.clip(1.0 + 0.1 * jax.random.normal(key_list[4], (D,), jnp.float32), 0.5, 1.5).astype(jnp.bfloat16)
    w_query = noise(key_list[5], (D, HEADS * HEAD), D ** -0.5, 0.15625, ((0, 8),))
    w_keyval = noise(key_list[6], (D, 2 * KV_HEADS * HEAD), D ** -0.5, 0.15625, ((0, 8),))
    w_attn_out = noise(key_list[7], (HEADS * HEAD, D), (HEADS * HEAD) ** -0.5, 0.15625, ((0, 8),))
    w_mixer_in = noise(key_list[8], (D, 2 * INNER), D ** -0.5, 0.15625, ((0, 8),))
    conv_taps = noise(key_list[9], (CONV, INNER), CONV ** -0.5, 3.0, ((1, 8),))
    conv_bias = noise(key_list[10], (INNER,), 0.5, 3.0, ((0, 8),))
    w_select = noise(key_list[11], (INNER, DT_RANK + 2 * STATE), INNER ** -0.5, 0.109375, ((0, 8),))
    w_step = noise(key_list[12], (DT_RANK, INNER), DT_RANK ** -0.5, 0.625, ((1, 8),))
    step_bias = jnp.clip(-1.5 + 2.0 * jax.random.uniform(key_list[13], (INNER,), jnp.float32) ** block_scale(key_list[13], (INNER,), ((0, 8),), -0.2, 0.2), -1.5, 0.5).astype(jnp.bfloat16)
    log_rates = jnp.clip(-6.0 + 3.5 * jax.random.uniform(key_list[14], (STATE, INNER), jnp.float32) ** block_scale(key_list[14], (STATE, INNER), ((1, 8),), -0.2, 0.2), -6.0, -2.5).astype(jnp.bfloat16)
    skip_gain = jnp.clip(0.5 + 1.0 * jax.random.uniform(key_list[15], (INNER,), jnp.float32) ** block_scale(key_list[15], (INNER,), ((0, 8),), -0.2, 0.2), 0.5, 1.5).astype(jnp.bfloat16)
    w_mixer_out = noise(key_list[16], (INNER, D), INNER ** -0.5, 0.109375, ((0, 8),))
    attn_gain = jnp.clip(1.0 + 0.1 * jax.random.normal(key_list[17], (D,), jnp.float32), 0.5, 1.5).astype(jnp.bfloat16)
    ssm_gain = jnp.clip(1.0 + 0.1 * jax.random.normal(key_list[18], (D,), jnp.float32), 0.5, 1.5).astype(jnp.bfloat16)
    ffn_norm_gain = jnp.clip(1.0 + 0.1 * jax.random.normal(key_list[19], (D,), jnp.float32), 0.5, 1.5).astype(jnp.bfloat16)
    w_gate_up = noise(key_list[20], (D, 2 * FF), D ** -0.5, 0.15625, ((0, 8),))
    w_down = noise(key_list[21], (FF, D), FF ** -0.5, 0.078125, ((0, 8),))
    return dict(tokens=tokens, cotangent=cotangent, doc_lengths=doc_lengths, meta_tokens=meta_tokens, norm_gain=norm_gain, w_query=w_query, w_keyval=w_keyval, w_attn_out=w_attn_out, w_mixer_in=w_mixer_in, conv_taps=conv_taps, conv_bias=conv_bias, w_select=w_select, w_step=w_step, step_bias=step_bias, log_rates=log_rates, skip_gain=skip_gain, w_mixer_out=w_mixer_out, attn_gain=attn_gain, ssm_gain=ssm_gain, ffn_norm_gain=ffn_norm_gain, w_gate_up=w_gate_up, w_down=w_down)


EPS = 1e-05
HIGH = lax.Precision.HIGHEST
NEG = -1e+30

@jax.custom_vjp
def low(v):
    return lax.optimization_barrier(v.astype(jnp.bfloat16)).astype(jnp.float32)

@jax.custom_vjp
def low_back(v):
    return v

def low_keep(v):
    return (low(v), None)

def low_pass(kept, grad):
    return (grad,)

def back_keep(v):
    return (v, None)

def back_low(kept, grad):
    return (low(grad),)
low.defvjp(low_keep, low_pass)
low_back.defvjp(back_keep, back_low)

def rounded_both(value):
    return low_back(low(value))

def product(left, right):
    return jnp.dot(left, right, precision=HIGH, preferred_element_type=jnp.float32)

def norm_rows(value, gain):
    return value * lax.rsqrt(lax.optimization_barrier(jnp.mean(value * value, axis=-1, keepdims=True)) + EPS) * gain

def doc_number(positions, bounds):
    return lax.optimization_barrier(jnp.sum((positions[:, None] >= bounds[None, :]).astype(jnp.int32), axis=1))

def attention(queries, keyvals, meta_kv, positions, docs):
    kv_width = KV_HEADS * HEAD
    groups = HEADS // KV_HEADS
    joined = jnp.concatenate([meta_kv, keyvals], 0)
    keys = joined[:, :kv_width].reshape(-1, KV_HEADS, HEAD)
    values = joined[:, kv_width:].reshape(-1, KV_HEADS, HEAD)
    key_pos = jnp.concatenate([jnp.full((META,), -1, jnp.int32), positions])
    key_doc = jnp.concatenate([jnp.full((META,), -1, jnp.int32), docs])
    block_rows = min(512, LENGTH)
    blocks = LENGTH // block_rows
    query_heads = queries.reshape(blocks, block_rows, KV_HEADS, groups, HEAD)

    def one_block(item):
        query_block, query_pos, query_doc = item
        scores = jnp.einsum('qgha,kga->qghk', query_block, keys, precision=HIGH) * 0.125
        scores = low_back(scores)
        visible = (key_pos[None, :] <= query_pos[:, None]) & ((key_doc[None, :] == query_doc[:, None]) | (key_doc[None, :] < 0))
        scores = jnp.where(visible[:, None, None, :], scores, NEG)
        weights = jax.nn.softmax(scores, axis=-1)
        return jnp.einsum('qghk,kga->qgha', weights, values, precision=HIGH)
    result = lax.map(jax.checkpoint(one_block), (query_heads, positions.reshape(blocks, block_rows), docs.reshape(blocks, block_rows)))
    return result.reshape(LENGTH, HEADS * HEAD)

def selective(steps, conv_out, entry, exit_w, rates, keep):
    span_rows = min(64, LENGTH)
    pieces = LENGTH // span_rows
    items = (steps.reshape(pieces, span_rows, INNER), conv_out.reshape(pieces, span_rows, INNER), entry.reshape(pieces, span_rows, STATE), exit_w.reshape(pieces, span_rows, STATE), keep.reshape(pieces, span_rows))

    def advance(state, item):

        def single(state, element):
            step_row, conv_row, entry_row, exit_row, keep_row = element
            state = jnp.exp(step_row[None, :] * rates) * keep_row * state + entry_row[:, None] * (step_row * conv_row)[None, :]
            return (state, lax.optimization_barrier(jnp.sum(exit_row[:, None] * state, axis=0)))
        return lax.scan(single, state, item)
    _, outputs = lax.scan(jax.checkpoint(advance), jnp.zeros((STATE, INNER), jnp.float32), items)
    return outputs.reshape(LENGTH, INNER)

def sequence(params, hidden_in, lengths):
    meta, gain_one, query_w, keyval_w, attn_out_w, mixer_in_w, taps_w, taps_bias, select_w, step_w, step_shift, rates_log, skip_w, mixer_out_w, attn_norm, ssm_norm, ffn_gain, gate_up_w, down_w = params
    positions = jnp.arange(LENGTH, dtype=jnp.int32)
    bounds = jnp.cumsum(lengths)[:-1].astype(jnp.int32)
    docs = doc_number(positions, bounds)
    starts = (positions == 0) | (docs != doc_number(positions - 1, bounds))
    normed = low(norm_rows(hidden_in, gain_one))
    queries = rounded_both(product(normed, query_w))
    keyvals = rounded_both(product(normed, keyval_w))
    meta_kv = rounded_both(product(low(norm_rows(meta, gain_one)), keyval_w))
    attended = rounded_both(attention(queries, keyvals, meta_kv, positions, docs))
    attn_branch = norm_rows(low_back(product(attended, attn_out_w)), attn_norm)
    mixed_in = rounded_both(product(normed, mixer_in_w))
    conv_in = mixed_in[:, :INNER]
    gate_in = mixed_in[:, INNER:]
    pre_conv = taps_bias[None, :] + jnp.zeros((LENGTH, INNER), jnp.float32)
    for tap in range(CONV):
        behind = CONV - 1 - tap
        earlier = positions - behind
        valid = ((earlier >= 0) & (doc_number(earlier, bounds) == docs)).astype(jnp.float32)
        shifted = jnp.pad(conv_in, ((behind, 0), (0, 0)))[:LENGTH]
        pre_conv = pre_conv + taps_w[tap][None, :] * shifted * valid[:, None]
    conv_out = low(jax.nn.silu(pre_conv))
    selected = low_back(product(conv_out, select_w))
    step_low = low(selected[:, :DT_RANK])
    entry = selected[:, DT_RANK:DT_RANK + STATE]
    exit_w = selected[:, DT_RANK + STATE:]
    steps = jax.nn.softplus(low_back(product(step_low, step_w)) + step_shift)
    rates = -jnp.exp(rates_log)
    keep = 1.0 - starts.astype(jnp.float32)
    ssm_out = selective(steps, conv_out, entry, exit_w, rates, keep) + skip_w * conv_out
    mixer_mid = rounded_both(ssm_out * jax.nn.silu(gate_in))
    ssm_branch = norm_rows(low_back(product(mixer_mid, mixer_out_w)), ssm_norm)
    middle = hidden_in + 0.5 * (attn_branch + ssm_branch)
    normed_two = low(norm_rows(middle, ffn_gain))
    gate_up = rounded_both(product(normed_two, gate_up_w))
    hidden_ff = rounded_both(jax.nn.silu(gate_up[:, :FF]) * gate_up[:, FF:])
    return middle + product(hidden_ff, down_w)

def reference(tokens, cotangent, doc_lengths, meta_tokens, norm_gain, w_query, w_keyval, w_attn_out, w_mixer_in, conv_taps, conv_bias, w_select, w_step, step_bias, log_rates, skip_gain, w_mixer_out, attn_gain, ssm_gain, ffn_norm_gain, w_gate_up, w_down):
    params = tuple((weight.astype(jnp.float32) for weight in (meta_tokens, norm_gain, w_query, w_keyval, w_attn_out, w_mixer_in, conv_taps, conv_bias, w_select, w_step, step_bias, log_rates, skip_gain, w_mixer_out, attn_gain, ssm_gain, ffn_norm_gain, w_gate_up, w_down)))
    inputs = tokens.astype(jnp.float32)

    def whole(weights, hidden):
        return lax.map(lambda item: jax.checkpoint(sequence)(weights, item[0], item[1]), (hidden, doc_lengths))
    outputs, pullback = jax.vjp(whole, params, inputs)
    param_back, input_back = pullback(cotangent.astype(jnp.float32))
    return (outputs.astype(jnp.bfloat16), input_back, param_back[0], param_back[1], param_back[2], param_back[3], param_back[4], param_back[5], param_back[6], param_back[7], param_back[8], param_back[9], param_back[10], param_back[11], param_back[12], param_back[13], param_back[14], param_back[15], param_back[16], param_back[17], param_back[18])
```

```python
import jax
import jax.numpy as jnp
from jax import lax
from jax.experimental import pallas as pl
from jax.experimental.pallas import tpu as pltpu
from jax.sharding import PartitionSpec as P

HEADS = 25
KV_HEADS = 5
HEAD = 64
META = 128
STATE = 16
CONV = 4
DT_RANK = 100

EPS = 1e-05
NEG = -1e30
CUT = 1e30
LANES = 128
ROWS = 8
f32 = jnp.float32
bf16 = jnp.bfloat16


def matmul(left, right):
    return jnp.dot(left, right, preferred_element_type=f32)


def tmatmul(left, right):
    return lax.dot_general(left, right, (((0,), (0,)), ((), ())), preferred_element_type=f32)


def matmul_t(left, right):
    return lax.dot_general(left, right, (((1,), (1,)), ((), ())), preferred_element_type=f32)


def norm_rows(value, gain):
    scale = lax.rsqrt(jnp.mean(value * value, axis=-1, keepdims=True) + EPS)
    return (value * scale * gain, scale)


def norm_back(value, scale, gain, upstream):
    tilted = upstream * gain
    mixing = jnp.mean(tilted * value, axis=-1, keepdims=True)
    return (
        scale * tilted - value * scale * scale * scale * mixing,
        jnp.sum(upstream * value * scale, axis=0),
    )


def doc_number(positions, bounds):
    return jnp.sum((positions[:, None] >= bounds[None, :]).astype(jnp.int32), axis=1)


def padded(array, axis, size):
    widths = [(0, 0)] * array.ndim
    widths[axis] = (0, size - array.shape[axis])
    return jnp.pad(array, widths)


def shifted(block, axis, distance):
    devices = range(lax.axis_size(axis))
    route = [(i - distance, i) for i in devices if i - distance in devices]
    return lax.ppermute(block, axis, route)


def gathered(array, axis):
    return lax.all_gather(array, axis, axis=0)


def exchanged(array):
    return lax.all_to_all(array, "fsdp", 0, 0)


def scattered(array):
    return lax.psum_scatter(array.astype(bf16), "fsdp", scatter_dimension=0, tiled=False).astype(
        f32
    )


def columns(weight, count):
    return weight.reshape(weight.shape[0], count, -1).swapaxes(0, 1)


def swapped(array):
    return array.swapaxes(0, 1)


def rates_of(rate_ref):
    return [jnp.broadcast_to(rate_ref[n : n + 1, :], (ROWS, LANES)) for n in range(STATE)]


def carry_body(step_ref, conv_ref, sel_ref, rate_ref, out_ref):
    rates = rates_of(rate_ref)

    def turn(t, state):
        step, sel = step_ref[t], sel_ref[t]
        push = step * conv_ref[t]
        fade = step + sel[:, 2 * STATE : 2 * STATE + 1]
        new = [
            jnp.exp(fade * rates[n]) * state[n] + sel[:, n : n + 1] * push for n in range(STATE)
        ]
        return (*new, state[STATE] + fade)

    zero = jnp.zeros((ROWS, LANES), f32)
    state = lax.fori_loop(0, step_ref.shape[0], turn, (zero,) * (STATE + 1))
    for n in range(STATE + 1):
        out_ref[n] = state[n]


def scan_body(mine_ref, step_ref, conv_ref, sel_ref, rate_ref, carry_ref, out_ref, states_ref):
    rates = rates_of(rate_ref)

    def join(j, state):
        return tuple(
            jnp.exp(rates[n] * carry_ref[j, STATE]) * state[n] + carry_ref[j, n]
            for n in range(STATE)
        )

    zero = jnp.zeros((ROWS, LANES), f32)
    state = lax.fori_loop(0, mine_ref[0], join, (zero,) * STATE)
    for n in range(STATE):
        states_ref[0, n] = state[n]

    def turn(t, state):
        step, sel = step_ref[t], sel_ref[t]
        push = step * conv_ref[t]
        fade = step + sel[:, 2 * STATE : 2 * STATE + 1]
        new, total = [], zero
        for n in range(STATE):
            now = jnp.exp(fade * rates[n]) * state[n] + sel[:, n : n + 1] * push
            states_ref[t + 1, n] = now
            total = total + sel[:, STATE + n : STATE + n + 1] * now
            new.append(now)
        out_ref[t] = total
        return tuple(new)

    lax.fori_loop(0, step_ref.shape[0], turn, state)


def carry_back_body(step_ref, sel_ref, rate_ref, up_ref, out_ref):
    rates = rates_of(rate_ref)
    count = step_ref.shape[0]

    def turn(i, state):
        t = count - 1 - i
        sel, up = sel_ref[t], up_ref[t]
        fade = step_ref[t] + sel[:, 2 * STATE : 2 * STATE + 1]
        return tuple(
            jnp.exp(fade * rates[n]) * (sel[:, STATE + n : STATE + n + 1] * up + state[n])
            for n in range(STATE)
        )

    zero = jnp.zeros((ROWS, LANES), f32)
    state = lax.fori_loop(0, count, turn, (zero,) * STATE)
    for n in range(STATE):
        out_ref[n] = state[n]


def scan_back_body(
    mine_ref,
    step_ref,
    conv_ref,
    sel_ref,
    rate_ref,
    up_ref,
    states_ref,
    span_ref,
    leave_ref,
    step_out,
    conv_out,
    sel_out,
    rate_out,
    enter_terms,
    exit_terms,
):
    rates = rates_of(rate_ref)
    count = step_ref.shape[0]
    devices = span_ref.shape[0]
    zero = jnp.zeros((ROWS, LANES), f32)

    def join(i, state):
        j = devices - 1 - i
        return tuple(
            jnp.exp(rates[n] * span_ref[j]) * state[n] + leave_ref[j, n] for n in range(STATE)
        )

    state = lax.fori_loop(0, devices - 1 - mine_ref[0], join, (zero,) * STATE)

    def turn(i, carried):
        t = count - 1 - i
        step, conv, sel, up = step_ref[t], conv_ref[t], sel_ref[t], up_ref[t]
        push = step * conv
        fade = step + sel[:, 2 * STATE : 2 * STATE + 1]
        rows = pl.ds(pl.multiple_of(t * ROWS, ROWS), ROWS)
        push_back, fade_back, new, rate_back = zero, zero, [], []
        for n in range(STATE):
            lanes = slice(n * LANES, (n + 1) * LANES)
            total = sel[:, STATE + n : STATE + n + 1] * up + carried[n]
            exit_terms[rows, lanes] = up * states_ref[t + 1, n]
            enter_terms[rows, lanes] = total * push
            push_back = push_back + total * sel[:, n : n + 1]
            earlier = jnp.exp(fade * rates[n]) * total
            slope = earlier * states_ref[t, n]
            fade_back = fade_back + slope * rates[n]
            new.append(earlier)
            rate_back.append(carried[STATE + n] + slope * step)
        step_out[t] = push_back * conv + fade_back
        conv_out[t] = push_back * step
        return (*new, *rate_back)

    state = lax.fori_loop(0, count, turn, state + (zero,) * STATE)
    for n in range(STATE):
        rate_out[0, n : n + 1] = jnp.sum(state[STATE + n], axis=0, keepdims=True)

    @pl.when(pl.program_id(1) == 0)
    def _():
        sel_out[...] = jnp.zeros_like(sel_out)

    place = lax.broadcasted_iota(jnp.int32, (2 * LANES, LANES), 1)
    half = lax.broadcasted_iota(jnp.int32, (2 * LANES, LANES), 0) // LANES
    total = jnp.zeros((count * ROWS, LANES), f32)
    for n in range(0, STATE, 2):
        lanes = slice(n * LANES, (n + 2) * LANES)
        pick = (place == n + half).astype(bf16)
        total = total + matmul(enter_terms[:, lanes].astype(bf16), pick)
        pick = (place == STATE + n + half).astype(bf16)
        total = total + matmul(exit_terms[:, lanes].astype(bf16), pick)
    sel_out[...] += total.reshape(count, ROWS, LANES)


def scan_specs(count, seqs, wide, devices):
    specs = dict(
        mine=pl.BlockSpec(memory_space=pltpu.SMEM),
        row=pl.BlockSpec((count, ROWS, LANES), lambda s, c: (0, s, c)),
        sel=pl.BlockSpec((count, ROWS, LANES), lambda s, c: (0, s, 0)),
        rate=pl.BlockSpec((STATE, LANES), lambda s, c: (0, c)),
        carry=pl.BlockSpec((STATE + 1, ROWS, LANES), lambda s, c: (0, s, c)),
        carries=pl.BlockSpec((devices, STATE + 1, ROWS, LANES), lambda s, c: (0, 0, s, c)),
        leave=pl.BlockSpec((STATE, ROWS, LANES), lambda s, c: (0, s, c)),
        leaves=pl.BlockSpec((devices, STATE, ROWS, LANES), lambda s, c: (0, 0, s, c)),
        span=pl.BlockSpec((devices, ROWS, LANES), lambda s, c: (0, s, c)),
        states=pl.BlockSpec((count + 1, STATE, ROWS, LANES), lambda s, c: (0, 0, s, c)),
        rates=pl.BlockSpec((1, STATE, LANES), lambda s, c: (s, 0, c)),
    )
    return specs, (seqs // ROWS, wide // LANES)


def scan_call(body, name, grid, ins, outs, shapes, scratch, work, args):
    cells = work * STATE * args[1].size
    return pl.pallas_call(
        body,
        name=name,
        grid=grid,
        in_specs=ins,
        out_specs=outs,
        out_shape=[jax.ShapeDtypeStruct(shape, f32) for shape in shapes],
        scratch_shapes=scratch,
        compiler_params=pltpu.CompilerParams(
            dimension_semantics=("arbitrary", "arbitrary"), vmem_limit_bytes=56 * 2**20
        ),
        cost_estimate=pl.CostEstimate(
            flops=cells, bytes_accessed=64 * 2**20, transcendentals=cells // 8
        ),
    )(*args)


def shards(
    tokens,
    cotangent,
    doc_lengths,
    meta_tokens,
    norm_gain,
    w_query,
    w_keyval,
    w_attn_out,
    w_mixer_in,
    conv_taps,
    conv_bias,
    w_select,
    w_step,
    step_bias,
    log_rates,
    skip_gain,
    w_mixer_out,
    attn_gain,
    ssm_gain,
    ffn_norm_gain,
    w_gate_up,
    w_down,
):
    count = tokens.shape[1]
    width = tokens.shape[2]
    seqs = lax.axis_size("fsdp")
    ctx_index = lax.axis_index("ctx")
    ctx_count = lax.axis_size("ctx")
    inner = conv_bias.shape[0]
    wide = -(-inner // LANES) * LANES
    ff_all = w_gate_up.shape[1] // 2
    q_cols = w_query.shape[1] // seqs
    kv_width = KV_HEADS * HEAD
    groups = HEADS // KV_HEADS
    mine = jnp.reshape(ctx_index, (1,)).astype(jnp.int32)

    positions = ctx_index * count + jnp.arange(count, dtype=jnp.int32)
    last_pos = ctx_index * count + count - 1
    bounds = jnp.cumsum(doc_lengths[0])[:-1]
    docs = doc_number(positions, bounds)

    hidden_in = tokens[0].astype(f32)
    small = lax.all_gather(
        jnp.stack([norm_gain, attn_gain, ssm_gain, ffn_norm_gain]), "fsdp", axis=1, tiled=True
    ).astype(f32)
    gain_f, attn_norm_f, ssm_norm_f, ffn_gain_f = small[0], small[1], small[2], small[3]
    lengths = lax.all_gather(doc_lengths, "fsdp", axis=0, tiled=True)

    normed_f, scale_one = norm_rows(hidden_in, gain_f)
    meta_f = meta_tokens.astype(f32)
    meta_normed_f, meta_scale = norm_rows(meta_f, gain_f)
    normed = gathered(normed_f.astype(bf16), "fsdp").reshape(seqs * count, width)
    meta_normed = gathered(meta_normed_f.astype(bf16), "fsdp").reshape(META, width)

    inner_all = w_mixer_in.shape[1] // 2
    conv_w = exchanged(padded(columns(w_mixer_in[:, :inner_all], seqs), 2, wide))
    conv_w = conv_w.reshape(width, wide)
    gate_w = exchanged(padded(columns(w_mixer_in[:, inner_all:], seqs), 2, wide))
    gate_w = gate_w.reshape(width, wide)
    qkv_w = exchanged(
        jnp.concatenate([columns(w_query, seqs), columns(w_keyval, seqs)], 2)
    ).reshape(width, -1)
    ff_gate_w = exchanged(columns(w_gate_up[:, :ff_all], seqs)).reshape(width, -1)
    ff_up_w = exchanged(columns(w_gate_up[:, ff_all:], seqs)).reshape(width, -1)
    out_back_all = gathered(cotangent[0], "fsdp").reshape(seqs * count, width)

    conv_in = swapped(matmul(normed, conv_w).astype(bf16).reshape(seqs, count, wide))
    gate_in = swapped(matmul(normed, gate_w).astype(bf16).reshape(seqs, count, wide))
    qkv = matmul(normed, qkv_w).astype(bf16).reshape(seqs, count, -1)
    meta_kv = matmul(meta_normed, qkv_w[:, q_cols:]).astype(bf16)

    qkv = exchanged(qkv)
    queries = swapped(qkv[:, :, :q_cols]).reshape(count, HEADS * HEAD)
    keyvals = swapped(qkv[:, :, q_cols:]).reshape(count, 2 * kv_width)
    meta_kv = swapped(gathered(meta_kv, "fsdp")).reshape(META, 2 * kv_width)
    query_heads = queries.reshape(count, KV_HEADS, groups, HEAD)
    piece = lax.all_gather(keyvals, "ctx", axis=0, tiled=True)
    joined = jnp.concatenate([meta_kv, piece], 0)
    keys = joined[:, :kv_width].reshape(-1, KV_HEADS, HEAD)
    values = joined[:, kv_width:].reshape(-1, KV_HEADS, HEAD)
    key_pos = jnp.arange(piece.shape[0], dtype=jnp.int32)
    key_doc = doc_number(key_pos, bounds)
    shown = (key_pos[None, :] <= positions[:, None]) & (key_doc[None, :] == docs[:, None])
    shown = jnp.concatenate([jnp.full((count, META), True), shown], 1)
    scores = (
        jnp.einsum("qgha,kga->ghqk", query_heads, keys, preferred_element_type=f32) * 0.125
    )
    scores = jnp.where(shown[None, None], scores, NEG)
    top = jnp.max(scores, axis=-1, keepdims=True)
    weights = jnp.exp(scores - top)
    weights = weights / jnp.sum(weights, axis=-1, keepdims=True)
    attn_heads_f = jnp.einsum(
        "ghqk,kga->qgha", weights.astype(bf16), values, preferred_element_type=f32
    )
    attn_b = attn_heads_f.reshape(count, HEADS * HEAD).astype(bf16)
    attn_cols = exchanged(columns(attn_b, seqs)).reshape(seqs * count, -1)
    attn_proj = scattered(matmul(attn_cols, w_attn_out).reshape(seqs, count, width))
    attn_branch, attn_scale = norm_rows(attn_proj, attn_norm_f)

    seq_bounds = jnp.cumsum(lengths, axis=1)[:, :-1]

    def numbers(places):
        return jnp.sum((places[:, None, None] >= seq_bounds[None]).astype(jnp.int32), axis=-1)

    seq_docs = numbers(positions)
    starts = (positions[:, None] == 0) | (seq_docs != numbers(positions - 1))
    taps_f = padded(conv_taps.astype(f32), 1, wide)
    rim = shifted(conv_in[count - (CONV - 1) :], "ctx", 1)
    extended = jnp.concatenate([rim, conv_in], 0).astype(f32)
    valid_rows = []
    for tap in range(CONV):
        earlier = positions - (CONV - 1 - tap)
        valid = (earlier[:, None] >= 0) & (numbers(earlier) == seq_docs)
        valid_rows.append(valid.astype(f32)[:, :, None])
    pre_conv = padded(conv_bias.astype(f32), 0, wide)[None, None, :]
    for tap in range(CONV):
        pre_conv = pre_conv + taps_f[tap] * extended[tap : tap + count] * valid_rows[tap]
    conv_sig = jax.nn.sigmoid(pre_conv)
    conv_out = (pre_conv * conv_sig).astype(bf16)
    conv_f = conv_out.astype(f32)
    conv_rows = conv_out.reshape(count * seqs, wide)
    select_w = padded(w_select, 0, wide)
    step_w = padded(w_step, 1, wide)
    selected = lax.psum(matmul(conv_rows, select_w), "fsdp")
    step_low = selected[:, :DT_RANK].astype(bf16)
    step_pre = matmul(step_low, step_w) + padded(step_bias.astype(f32), 0, wide)[None, :]
    step_pre = step_pre.reshape(count, seqs, wide)
    steps = jax.nn.softplus(step_pre)
    rates = -jnp.exp(padded(log_rates.astype(f32), 1, wide))
    sel = jnp.concatenate(
        [
            selected[:, DT_RANK:].reshape(count, seqs, 2 * STATE),
            jnp.where(starts, CUT, 0.0).astype(f32)[:, :, None],
        ],
        2,
    )
    sel = padded(sel, 2, LANES)
    spec, grid = scan_specs(count, seqs, wide, ctx_count)
    row_shape = (count, seqs, wide)
    (carry,) = scan_call(
        carry_body,
        "mamba_carry",
        grid,
        [spec["row"], spec["row"], spec["sel"], spec["rate"]],
        [spec["carry"]],
        [(STATE + 1, seqs, wide)],
        [],
        8,
        (steps, conv_f, sel, rates),
    )
    carries = gathered(carry, "ctx")
    scanned, states = scan_call(
        scan_body,
        "mamba_scan",
        grid,
        [spec["mine"], spec["row"], spec["row"], spec["sel"], spec["rate"], spec["carries"]],
        [spec["row"], spec["states"]],
        [row_shape, (count + 1, STATE, seqs, wide)],
        [],
        10,
        (mine, steps, conv_f, sel, rates, carries),
    )
    skip_f = padded(skip_gain.astype(f32), 0, wide)
    ssm_out = scanned + skip_f * conv_f
    gate_f = gate_in.astype(f32)
    gate_sig = jax.nn.sigmoid(gate_f)
    gate_act = gate_f * gate_sig
    mixer_mid = swapped((ssm_out * gate_act).astype(bf16)).reshape(seqs * count, wide)
    mixer_out_w = padded(w_mixer_out, 0, wide)
    mixer_proj = scattered(matmul(mixer_mid, mixer_out_w).reshape(seqs, count, width))
    ssm_branch, ssm_scale = norm_rows(mixer_proj, ssm_norm_f)
    middle = hidden_in + 0.5 * (attn_branch + ssm_branch)

    normed_two_f, scale_two = norm_rows(middle, ffn_gain_f)
    normed_two = gathered(normed_two_f.astype(bf16), "fsdp").reshape(seqs * count, width)
    gate_v = matmul(normed_two, ff_gate_w).astype(bf16).astype(f32)
    up_v = matmul(normed_two, ff_up_w).astype(bf16).astype(f32)
    ffn_sig = jax.nn.sigmoid(gate_v)
    hidden_ff = (gate_v * ffn_sig * up_v).astype(bf16)
    output = middle + scattered(matmul(hidden_ff, w_down).reshape(seqs, count, width))
    block_out = output.astype(bf16)[None]

    down_back = tmatmul(hidden_ff, out_back_all)
    hidden_back = matmul_t(out_back_all, w_down).astype(bf16).astype(f32)
    up_back = (hidden_back * gate_v * ffn_sig).astype(bf16)
    gate_back = (hidden_back * up_v * ffn_sig * (1.0 + gate_v * (1.0 - ffn_sig))).astype(bf16)
    ff_gate_back = tmatmul(normed_two, gate_back)
    ff_up_back = tmatmul(normed_two, up_back)
    normed_two_back = scattered(
        (matmul_t(gate_back, ff_gate_w) + matmul_t(up_back, ff_up_w)).reshape(seqs, count, width)
    )
    ffn_sums = lax.psum(
        (down_back.astype(bf16), ff_gate_back.astype(bf16), ff_up_back.astype(bf16)), "ctx"
    )
    middle_norm_back, ffn_gain_back = norm_back(middle, scale_two, ffn_gain_f, normed_two_back)
    middle_back = cotangent[0].astype(f32) + middle_norm_back
    branch_back = 0.5 * middle_back
    ssm_proj_back, ssm_gain_back = norm_back(mixer_proj, ssm_scale, ssm_norm_f, branch_back)
    attn_proj_back, attn_gain_back = norm_back(attn_proj, attn_scale, attn_norm_f, branch_back)
    ssm_proj_back = gathered(ssm_proj_back.astype(bf16), "fsdp").reshape(seqs * count, width)
    attn_proj_back = gathered(attn_proj_back.astype(bf16), "fsdp").reshape(seqs * count, width)

    mixer_out_back = tmatmul(mixer_mid, ssm_proj_back)[:inner]
    mid_back = matmul_t(ssm_proj_back, mixer_out_w).astype(bf16).reshape(seqs, count, wide)
    mid_back = swapped(mid_back).astype(f32)
    ssm_back = mid_back * gate_act
    gate_in_back = mid_back * ssm_out * gate_sig * (1.0 + gate_f * (1.0 - gate_sig))
    skip_back = jnp.sum(ssm_back * conv_f, axis=(0, 1))
    (leave,) = scan_call(
        carry_back_body,
        "mamba_carry_back",
        grid,
        [spec["row"], spec["sel"], spec["rate"], spec["row"]],
        [spec["leave"]],
        [(STATE, seqs, wide)],
        [],
        8,
        (steps, sel, rates, ssm_back),
    )
    leaves = gathered(leave, "ctx")
    steps_back, conv_back, sel_back, rates_back = scan_call(
        scan_back_body,
        "mamba_scan_back",
        grid,
        [
            spec["mine"],
            spec["row"],
            spec["row"],
            spec["sel"],
            spec["rate"],
            spec["row"],
            spec["states"],
            spec["span"],
            spec["leaves"],
        ],
        [spec["row"], spec["row"], spec["sel"], spec["rates"]],
        [row_shape, row_shape, (count, seqs, LANES), (seqs // ROWS, STATE, wide)],
        [pltpu.VMEM((count * ROWS, STATE * LANES), f32)] * 2,
        20,
        (mine, steps, conv_f, sel, rates, ssm_back, states, carries[:, STATE], leaves),
    )
    rates_log_back = jnp.sum(rates_back, axis=0) * rates
    step_pre_back = steps_back * jax.nn.sigmoid(step_pre)
    step_shift_back = jnp.sum(step_pre_back, axis=(0, 1))
    step_pre_back = step_pre_back.astype(bf16).reshape(count * seqs, wide)
    step_w_back = tmatmul(step_low, step_pre_back)[:, :inner]
    selected_back = lax.psum(
        jnp.concatenate(
            [
                matmul_t(step_pre_back, step_w),
                sel_back[:, :, : 2 * STATE].reshape(count * seqs, 2 * STATE),
            ],
            1,
        ),
        "fsdp",
    ).astype(bf16)
    select_w_back = tmatmul(conv_rows, selected_back)[:inner]
    conv_back = (
        conv_back
        + skip_f * ssm_back
        + matmul_t(selected_back, select_w).reshape(count, seqs, wide)
    )
    pre_back = conv_back * conv_sig * (1.0 + pre_conv * (1.0 - conv_sig))
    taps_bias_back = jnp.sum(pre_back, axis=(0, 1))
    tap_rows = []
    extended_back = jnp.zeros((count + CONV - 1, seqs, wide), f32)
    for tap in range(CONV):
        masked_back = pre_back * valid_rows[tap]
        tap_rows.append(jnp.sum(masked_back * extended[tap : tap + count], axis=(0, 1)))
        extended_back = extended_back + jnp.pad(
            taps_f[tap] * masked_back, ((tap, CONV - 1 - tap), (0, 0), (0, 0))
        )
    rim_back = shifted(extended_back[: CONV - 1].astype(bf16), "ctx", -1).astype(f32)
    conv_in_back = extended_back[CONV - 1 :] + jnp.pad(
        rim_back, ((count - (CONV - 1), 0), (0, 0), (0, 0))
    )
    conv_in_back = swapped(conv_in_back.astype(bf16)).reshape(seqs * count, wide)
    gate_in_back = swapped(gate_in_back.astype(bf16)).reshape(seqs * count, wide)
    conv_w_back = tmatmul(normed, conv_in_back)[:, :inner]
    gate_w_back = tmatmul(normed, gate_in_back)[:, :inner]

    attn_out_back = tmatmul(attn_cols, attn_proj_back)
    heads_back = matmul_t(attn_proj_back, w_attn_out).astype(bf16).reshape(seqs, count, -1)
    heads_back = swapped(exchanged(heads_back)).reshape(count, KV_HEADS, groups, HEAD)
    delta = jnp.sum(heads_back.astype(f32) * attn_heads_f, axis=-1)
    delta = delta.transpose(1, 2, 0)[..., None]
    weights_back = jnp.einsum("qgha,kga->ghqk", heads_back, values, preferred_element_type=f32)
    scores_back = (weights * (weights_back - delta)).astype(bf16)
    query_back = (
        jnp.einsum("ghqk,kga->qgha", scores_back, keys, preferred_element_type=f32) * 0.125
    )
    keys_back = (
        jnp.einsum("ghqk,qgha->kga", scores_back, query_heads, preferred_element_type=f32) * 0.125
    )
    values_back = jnp.einsum(
        "ghqk,qgha->kga", weights.astype(bf16), heads_back, preferred_element_type=f32
    )
    kv_back = jnp.concatenate(
        [keys_back.reshape(-1, kv_width), values_back.reshape(-1, kv_width)], 1
    )
    buffer = jnp.zeros((ctx_count, count + META, 2 * kv_width), f32)
    buffer = buffer.at[0, count:].set(kv_back[:META])
    buffer = buffer.at[:, :count].set(kv_back[META:].reshape(ctx_count, count, 2 * kv_width))
    owned = lax.psum_scatter(buffer.astype(bf16), "ctx", scatter_dimension=0, tiled=True)[0]
    query_back = query_back.reshape(count, HEADS * HEAD).astype(bf16)
    qkv_back = exchanged(
        jnp.concatenate([columns(query_back, seqs), columns(owned[:count], seqs)], 2)
    ).reshape(seqs * count, -1)
    meta_kv_back = exchanged(columns(owned[count:], seqs))
    meta_kv_back = jnp.sum(meta_kv_back.astype(f32), axis=0).astype(bf16)
    qkv_w_back = tmatmul(normed, qkv_back)
    keyval_w_back = qkv_w_back[:, q_cols:] + tmatmul(meta_normed, meta_kv_back)
    meta_back = lax.psum_scatter(
        matmul_t(meta_kv_back, qkv_w[:, q_cols:]).astype(bf16),
        "fsdp",
        scatter_dimension=0,
        tiled=True,
    ).astype(f32)
    normed_back = scattered(
        (
            matmul_t(conv_in_back, conv_w)
            + matmul_t(gate_in_back, gate_w)
            + matmul_t(qkv_back, qkv_w)
        ).reshape(seqs, count, width)
    )
    input_norm_back, gain_back_a = norm_back(hidden_in, scale_one, gain_f, normed_back)
    meta_back, gain_back_b = norm_back(meta_f, meta_scale, gain_f, meta_back)
    grad_tokens = (middle_back + input_norm_back)[None]

    sums = lax.psum(
        tuple(
            part.astype(bf16)
            for part in (
                meta_back,
                qkv_w_back[:, :q_cols],
                keyval_w_back,
                attn_out_back,
                conv_w_back,
                gate_w_back,
                select_w_back,
                step_w_back,
                mixer_out_back,
            )
        ),
        "ctx",
    )
    thin = lax.psum(
        jnp.concatenate(
            [
                tap_rows[0][None],
                tap_rows[1][None],
                tap_rows[2][None],
                tap_rows[3][None],
                taps_bias_back[None],
                step_shift_back[None],
                skip_back[None],
                rates_log_back,
            ],
            0,
        ),
        "ctx",
    )[:, :inner]
    gains = lax.psum(
        jnp.stack([gain_back_a + gain_back_b, attn_gain_back, ssm_gain_back, ffn_gain_back]),
        ("fsdp", "ctx"),
    )
    share = norm_gain.shape[0]
    gains = lax.dynamic_slice_in_dim(gains, lax.axis_index("fsdp") * share, share, 1)

    def owner(part):
        rows = part.shape[0] // seqs
        return swapped(exchanged(part.reshape(seqs, rows, -1))).reshape(rows, -1).astype(f32)

    grad_gate_up = jnp.concatenate([owner(ffn_sums[1]), owner(ffn_sums[2])], 1)
    grad_mixer_in = jnp.concatenate([owner(sums[4]), owner(sums[5])], 1)
    return (
        block_out,
        grad_tokens,
        sums[0].astype(f32),
        gains[0],
        owner(sums[1]),
        owner(sums[2]),
        sums[3].astype(f32),
        grad_mixer_in,
        thin[:CONV],
        thin[CONV],
        sums[6].astype(f32),
        sums[7].astype(f32),
        thin[CONV + 1],
        thin[CONV + 3 :],
        thin[CONV + 2],
        sums[8].astype(f32),
        gains[1],
        gains[2],
        gains[3],
        grad_gate_up,
        ffn_sums[0].astype(f32),
    )


def solution(mesh):
    rows, cols, one = P("fsdp", None), P(None, "fsdp"), P("fsdp")
    split = P("fsdp", "ctx", None)
    in_specs = (
        split,
        split,
        rows,
        rows,
        one,
        rows,
        rows,
        rows,
        rows,
        cols,
        one,
        rows,
        cols,
        one,
        cols,
        one,
        rows,
        one,
        one,
        one,
        rows,
        rows,
    )
    out_specs = (
        split,
        split,
        rows,
        one,
        rows,
        rows,
        rows,
        rows,
        cols,
        one,
        rows,
        cols,
        one,
        cols,
        one,
        rows,
        one,
        one,
        one,
        rows,
        rows,
    )
    return jax.shard_map(shards, mesh=mesh, in_specs=in_specs, out_specs=out_specs, check_vma=False)
```

```python
import jax
import jax.numpy as jnp
from jax import lax
from jax.experimental import pallas as pl
from jax.experimental.pallas import tpu as pltpu
from jax.sharding import PartitionSpec as P

HEADS = 25
KV_HEADS = 5
HEAD = 64
META = 128
STATE = 16
CONV = 4
DT_RANK = 100

EPS = 1e-05
NEG = -1e30
CUT = 1e30
LANES = 128
ROWS = 8
f32 = jnp.float32
bf16 = jnp.bfloat16


def matmul(left, right):
    return jnp.dot(left, right, preferred_element_type=f32)


def tmatmul(left, right):
    return lax.dot_general(left, right, (((0,), (0,)), ((), ())), preferred_element_type=f32)


def matmul_t(left, right):
    return lax.dot_general(left, right, (((1,), (1,)), ((), ())), preferred_element_type=f32)


def norm_rows(value, gain):
    scale = lax.rsqrt(jnp.mean(value * value, axis=-1, keepdims=True) + EPS)
    return (value * scale * gain, scale)


def norm_back(value, scale, gain, upstream):
    tilted = upstream * gain
    mixing = jnp.mean(tilted * value, axis=-1, keepdims=True)
    return (
        scale * tilted - value * scale * scale * scale * mixing,
        jnp.sum(upstream * value * scale, axis=0),
    )


def doc_number(positions, bounds):
    return jnp.sum((positions[:, None] >= bounds[None, :]).astype(jnp.int32), axis=1)


def padded(array, axis, size):
    widths = [(0, 0)] * array.ndim
    widths[axis] = (0, size - array.shape[axis])
    return jnp.pad(array, widths)


def shifted(block, axis, distance):
    devices = range(lax.axis_size(axis))
    route = [(i - distance, i) for i in devices if i - distance in devices]
    return lax.ppermute(block, axis, route)


def gathered(array, axis):
    return lax.all_gather(array, axis, axis=0)


def exchanged(array):
    return lax.all_to_all(array, "fsdp", 0, 0)


def scattered(array):
    return lax.psum_scatter(array.astype(bf16), "fsdp", scatter_dimension=0, tiled=False).astype(
        f32
    )


AT = pl.DeviceIdType.MESH
ANY = pl.BlockSpec(memory_space=pl.ANY)
INSIDE = pl.BlockSpec(memory_space=pltpu.VMEM)

def greet(axis, peers):
    barrier = pltpu.get_barrier_semaphore()
    for peer in peers:
        pl.semaphore_signal(barrier, inc=1, device_id={axis: peer}, device_id_type=AT)
    pl.semaphore_wait(barrier, len(peers))

def sender(axis, src, dst, send, recv, peer):
    return pltpu.make_async_remote_copy(src_ref=src, dst_ref=dst, send_sem=send, recv_sem=recv, device_id={axis: peer}, device_id_type=AT)

def comm_call(body, name, number, ins, shape, out_spec, scratch):
    return pl.pallas_call(body, name=name, out_shape=shape, in_specs=[spec for spec, _ in ins], out_specs=out_spec, scratch_shapes=scratch,
        compiler_params=pltpu.CompilerParams(collective_id=number, has_side_effects=True, vmem_limit_bytes=40*2**20))(*[array for _, array in ins])

def pair_gather(array, number):
    devices = lax.axis_size("fsdp"); pairs = devices // 2
    def body(mine, out, own, sent, got, passed, taken):
        me = lax.axis_index("fsdp"); pair = me // 2; core = lax.rem(me, 2); mate = me + 1 - 2 * core
        peers = [2 * lax.rem(pair + k, pairs) + core for k in range(1, pairs)]
        greet("fsdp", [mate, *peers])
        local = pltpu.make_async_copy(mine, out.at[me], own)
        local.start()
        first = [sender("fsdp", mine, out.at[me], sent.at[k], got.at[k], peer) for k, peer in enumerate([mate, *peers])]
        for copy in first[1:]: copy.start()
        first[0].start()
        second = []
        for k in range(1, pairs):
            slot = 2 * lax.rem(pair + pairs - k, pairs) + core
            first[k].wait_recv()
            copy = sender("fsdp", out.at[slot], out.at[slot], passed.at[k-1], taken.at[k-1], mate)
            copy.start(); second.append(copy)
        first[0].wait_recv()
        for copy in first: copy.wait_send()
        for copy in second: copy.wait()
        local.wait()
    return comm_call(body, "pair_gather", number, [(ANY, array)], jax.ShapeDtypeStruct((devices,) + array.shape, array.dtype), ANY,
        [pltpu.SemaphoreType.DMA, pltpu.SemaphoreType.DMA((pairs,)), pltpu.SemaphoreType.DMA((pairs,)), pltpu.SemaphoreType.DMA((pairs-1,)), pltpu.SemaphoreType.DMA((pairs-1,))])

def pair_scatter(array, number):
    devices = array.shape[0]; pairs = devices // 2; shape = array.shape[1:]
    def body(mine, out, near, summed, far, sent, got, passed, taken):
        me = lax.axis_index("fsdp"); pair = me // 2; core = lax.rem(me, 2); mate = me + 1 - 2 * core
        places = [lax.rem(pair + k, pairs) for k in range(1, pairs + 1)]
        greet("fsdp", [mate, *[2 * q + core for q in places[:-1]]])
        first = [sender("fsdp", mine.at[2 * q + 1 - core], near.at[k], sent.at[k], got.at[k], mate) for k, q in enumerate(places)]
        for copy in first: copy.start()
        second = []
        for k, q in enumerate(places):
            first[k].wait_recv()
            total = mine[2 * q + core].astype(f32) + near[k].astype(f32)
            if k < pairs - 1:
                summed[k] = total.astype(bf16)
                copy = sender("fsdp", summed.at[k], far.at[k], passed.at[k], taken.at[k], 2 * q + core)
                copy.start(); second.append(copy)
            else:
                out[...] = total
        for copy in second:
            copy.wait_recv()
        total = out[...]
        for k in range(pairs - 1): total = total + far[k].astype(f32)
        out[...] = total
        for copy in first: copy.wait_send()
        for copy in second: copy.wait_send()
    return comm_call(body, "pair_scatter", number, [(INSIDE, array)], jax.ShapeDtypeStruct(shape, f32), INSIDE,
        [pltpu.VMEM((pairs,) + shape, bf16), pltpu.VMEM((pairs-1,) + shape, bf16), pltpu.VMEM((pairs-1,) + shape, bf16),
         pltpu.SemaphoreType.DMA((pairs,)), pltpu.SemaphoreType.DMA((pairs,)), pltpu.SemaphoreType.DMA((pairs-1,)), pltpu.SemaphoreType.DMA((pairs-1,))])

def direct_sum(array, number):
    devices = array.shape[0]; shape = array.shape[1:]
    def body(mine, out, near, sent, got, passed, taken):
        me = lax.axis_index("fsdp")
        peers = [lax.rem(me + k, devices) for k in range(1, devices)]
        greet("fsdp", peers)
        first = [sender("fsdp", mine.at[peer], near.at[k], sent.at[k], got.at[k], peer) for k, peer in enumerate(peers)]
        for copy in first: copy.start()
        total = mine[me].astype(f32)
        for k in range(devices - 1):
            first[k].wait_recv()
            total = total + near[k].astype(f32)
        out[me] = total.astype(bf16)
        second = [sender("fsdp", out.at[me], out.at[me], passed.at[k], taken.at[k], peer) for k, peer in enumerate(peers)]
        for copy in second: copy.start()
        for copy in second: copy.wait()
        for copy in first: copy.wait_send()
    return comm_call(body, "direct_sum", number, [(INSIDE, array)], jax.ShapeDtypeStruct(array.shape, bf16), INSIDE,
        [pltpu.VMEM((devices-1,) + shape, bf16)] + [pltpu.SemaphoreType.DMA((devices-1,))] * 4)

def direct_gather(array, axis, number):
    devices = lax.axis_size(axis)
    def body(mine, out, own, sent, got):
        me = lax.axis_index(axis)
        peers = [lax.rem(me + k, devices) for k in range(1, devices)]
        greet(axis, peers)
        copies = [sender(axis, mine, out.at[me], sent.at[k], got.at[k], peer) for k, peer in enumerate(peers)]
        for copy in copies: copy.start()
        local = pltpu.make_async_copy(mine, out.at[me], own)
        local.start(); local.wait()
        for copy in copies: copy.wait()
    return comm_call(body, "direct_gather", number, [(ANY, array)], jax.ShapeDtypeStruct((devices,) + array.shape, array.dtype), ANY,
        [pltpu.SemaphoreType.DMA, pltpu.SemaphoreType.DMA((devices-1,)), pltpu.SemaphoreType.DMA((devices-1,))])


def columns(weight, count):
    return weight.reshape(weight.shape[0], count, -1).swapaxes(0, 1)


def swapped(array):
    return array.swapaxes(0, 1)


def rates_of(rate_ref):
    return [jnp.broadcast_to(rate_ref[n : n + 1, :], (ROWS, LANES)) for n in range(STATE)]


def spread(sel_ref, picks, cuts):
    @pl.when(pl.program_id(1) == 0)
    def _():
        def turn(t, _):
            sel = sel_ref[t]
            for first, into in picks:
                for n in range(STATE):
                    lane = sel[:, first + n : first + n + 1]
                    into[t, n] = jnp.broadcast_to(lane, (ROWS, LANES))
            cuts[t] = jnp.broadcast_to(sel[:, 2 * STATE : 2 * STATE + 1], (ROWS, LANES))
            return 0

        lax.fori_loop(0, sel_ref.shape[0], turn, 0, unroll=4)


def carry_body(step_ref, conv_ref, sel_ref, rate_ref, out_ref, enters, cuts):
    rates = rates_of(rate_ref)
    spread(sel_ref, [(0, enters)], cuts)

    def turn(t, state):
        step = step_ref[t]
        push = step * conv_ref[t]
        fade = step + cuts[t]
        new = [
            jnp.exp(fade * rates[n]) * state[n] + enters[t, n] * push for n in range(STATE)
        ]
        return (*new, state[STATE] + fade)

    zero = jnp.zeros((ROWS, LANES), f32)
    state = lax.fori_loop(0, step_ref.shape[0], turn, (zero,) * (STATE + 1), unroll=8)
    for n in range(STATE + 1):
        out_ref[n] = state[n]


def scan_body(
    mine_ref,
    step_ref,
    conv_ref,
    sel_ref,
    rate_ref,
    carry_ref,
    out_ref,
    states_ref,
    enters,
    exits,
    cuts,
):
    rates = rates_of(rate_ref)
    spread(sel_ref, [(0, enters), (STATE, exits)], cuts)

    def join(j, state):
        return tuple(
            jnp.exp(rates[n] * carry_ref[j, STATE]) * state[n] + carry_ref[j, n]
            for n in range(STATE)
        )

    zero = jnp.zeros((ROWS, LANES), f32)
    state = lax.fori_loop(0, mine_ref[0], join, (zero,) * STATE)
    for n in range(STATE):
        states_ref[0, n] = state[n]

    def turn(t, state):
        step = step_ref[t]
        push = step * conv_ref[t]
        fade = step + cuts[t]
        new, total = [], zero
        for n in range(STATE):
            now = jnp.exp(fade * rates[n]) * state[n] + enters[t, n] * push
            states_ref[t + 1, n] = now
            total = total + exits[t, n] * now
            new.append(now)
        out_ref[t] = total
        return tuple(new)

    lax.fori_loop(0, step_ref.shape[0], turn, state, unroll=8)


def carry_back_body(step_ref, sel_ref, rate_ref, up_ref, out_ref, exits, cuts):
    rates = rates_of(rate_ref)
    spread(sel_ref, [(STATE, exits)], cuts)
    count = step_ref.shape[0]

    def turn(i, state):
        t = count - 1 - i
        up = up_ref[t]
        fade = step_ref[t] + cuts[t]
        return tuple(
            jnp.exp(fade * rates[n]) * (exits[t, n] * up + state[n]) for n in range(STATE)
        )

    zero = jnp.zeros((ROWS, LANES), f32)
    state = lax.fori_loop(0, count, turn, (zero,) * STATE, unroll=8)
    for n in range(STATE):
        out_ref[n] = state[n]


def scan_back_body(
    mine_ref,
    step_ref,
    conv_ref,
    sel_ref,
    rate_ref,
    up_ref,
    states_ref,
    span_ref,
    leave_ref,
    step_out,
    conv_out,
    sel_out,
    rate_out,
    enter_terms,
    exit_terms,
    enters,
    exits,
    cuts,
):
    rates = rates_of(rate_ref)
    spread(sel_ref, [(0, enters), (STATE, exits)], cuts)
    count = step_ref.shape[0]
    devices = span_ref.shape[0]
    zero = jnp.zeros((ROWS, LANES), f32)

    def join(i, state):
        j = devices - 1 - i
        return tuple(
            jnp.exp(rates[n] * span_ref[j]) * state[n] + leave_ref[j, n] for n in range(STATE)
        )

    state = lax.fori_loop(0, devices - 1 - mine_ref[0], join, (zero,) * STATE)
    state = state + (zero,) * STATE
    place = lax.broadcasted_iota(jnp.int32, (2 * LANES, LANES), 1)
    half = lax.broadcasted_iota(jnp.int32, (2 * LANES, LANES), 0) // LANES
    span = count // 2

    @pl.when(pl.program_id(1) == 0)
    def _():
        sel_out[...] = jnp.zeros_like(sel_out)

    for start in (span, 0):

        def turn(i, carried):
            t = start + span - 1 - i
            step, conv, up = step_ref[t], conv_ref[t], up_ref[t]
            push = step * conv
            fade = step + cuts[t]
            rows = pl.ds(pl.multiple_of((t - start) * ROWS, ROWS), ROWS)
            push_back, fade_back, new, rate_back = zero, zero, [], []
            for n in range(STATE):
                lanes = slice(n * LANES, (n + 1) * LANES)
                total = exits[t, n] * up + carried[n]
                exit_terms[rows, lanes] = up * states_ref[t + 1, n]
                enter_terms[rows, lanes] = total * push
                push_back = push_back + total * enters[t, n]
                earlier = jnp.exp(fade * rates[n]) * total
                slope = earlier * states_ref[t, n]
                fade_back = fade_back + slope * rates[n]
                new.append(earlier)
                rate_back.append(carried[STATE + n] + slope * step)
            step_out[t] = push_back * conv + fade_back
            conv_out[t] = push_back * step
            return (*new, *rate_back)

        state = lax.fori_loop(0, span, turn, state, unroll=4)
        total = jnp.zeros((span * ROWS, LANES), f32)
        for n in range(0, STATE, 2):
            lanes = slice(n * LANES, (n + 2) * LANES)
            pick = (place == n + half).astype(bf16)
            total = total + matmul(enter_terms[:, lanes].astype(bf16), pick)
            pick = (place == STATE + n + half).astype(bf16)
            total = total + matmul(exit_terms[:, lanes].astype(bf16), pick)
        sel_out[start : start + span] += total.reshape(span, ROWS, LANES)
    for n in range(STATE):
        rate_out[0, n : n + 1] = jnp.sum(state[STATE + n], axis=0, keepdims=True)


def scan_specs(count, seqs, wide, devices):
    specs = dict(
        mine=pl.BlockSpec(memory_space=pltpu.SMEM),
        row=pl.BlockSpec((count, ROWS, LANES), lambda s, c: (0, s, c)),
        sel=pl.BlockSpec((count, ROWS, LANES), lambda s, c: (0, s, 0)),
        rate=pl.BlockSpec((STATE, LANES), lambda s, c: (0, c)),
        carry=pl.BlockSpec((STATE + 1, ROWS, LANES), lambda s, c: (0, s, c)),
        carries=pl.BlockSpec((devices, STATE + 1, ROWS, LANES), lambda s, c: (0, 0, s, c)),
        leave=pl.BlockSpec((STATE, ROWS, LANES), lambda s, c: (0, s, c)),
        leaves=pl.BlockSpec((devices, STATE, ROWS, LANES), lambda s, c: (0, 0, s, c)),
        span=pl.BlockSpec((devices, ROWS, LANES), lambda s, c: (0, s, c)),
        states=pl.BlockSpec((count + 1, STATE, ROWS, LANES), lambda s, c: (0, 0, s, c)),
        rates=pl.BlockSpec((1, STATE, LANES), lambda s, c: (s, 0, c)),
    )
    spreads = pltpu.VMEM((count, STATE, ROWS, LANES), f32)
    cuts = pltpu.VMEM((count, ROWS, LANES), f32)
    terms = pltpu.VMEM((count // 2 * ROWS, STATE * LANES), f32)
    specs["one"], specs["two"] = [spreads, cuts], [spreads, spreads, cuts]
    specs["four"] = [terms, terms, spreads, spreads, cuts]
    return specs, (seqs // ROWS, wide // LANES)


def scan_call(body, name, grid, ins, outs, shapes, scratch, work, args):
    cells = work * STATE * args[1].size
    return pl.pallas_call(
        body,
        name=name,
        grid=grid,
        in_specs=ins,
        out_specs=outs,
        out_shape=[jax.ShapeDtypeStruct(shape, f32) for shape in shapes],
        scratch_shapes=scratch,
        compiler_params=pltpu.CompilerParams(
            dimension_semantics=("arbitrary", "arbitrary"), vmem_limit_bytes=60 * 2**20
        ),
        cost_estimate=pl.CostEstimate(
            flops=cells, bytes_accessed=64 * 2**20, transcendentals=cells // 8
        ),
    )(*args)


def shards(
    tokens,
    cotangent,
    doc_lengths,
    meta_tokens,
    norm_gain,
    w_query,
    w_keyval,
    w_attn_out,
    w_mixer_in,
    conv_taps,
    conv_bias,
    w_select,
    w_step,
    step_bias,
    log_rates,
    skip_gain,
    w_mixer_out,
    attn_gain,
    ssm_gain,
    ffn_norm_gain,
    w_gate_up,
    w_down,
):
    count = tokens.shape[1]
    width = tokens.shape[2]
    seqs = lax.axis_size("fsdp")
    ctx_index = lax.axis_index("ctx")
    ctx_count = lax.axis_size("ctx")
    inner = conv_bias.shape[0]
    wide = -(-inner // LANES) * LANES
    ff_all = w_gate_up.shape[1] // 2
    kv_width = KV_HEADS * HEAD
    groups = HEADS // KV_HEADS
    mine = jnp.reshape(ctx_index, (1,)).astype(jnp.int32)

    positions = ctx_index * count + jnp.arange(count, dtype=jnp.int32)
    last_pos = ctx_index * count + count - 1
    bounds = jnp.cumsum(doc_lengths[0])[:-1]
    docs = doc_number(positions, bounds)

    hidden_in = tokens[0].astype(f32)
    meta_rows = meta_tokens.shape[0]
    share = norm_gain.shape[0]
    extra_rows = -(-(meta_rows + 1) // 16) * 16
    few = doc_lengths[0]
    thin = jnp.concatenate(
        [
            norm_gain,
            attn_gain,
            ssm_gain,
            ffn_norm_gain,
            (few // 32).astype(bf16),
            (few % 32).astype(bf16),
        ]
    )
    extra = padded(
        jnp.concatenate([meta_tokens, padded(thin, 0, width)[None]], 0), 0, extra_rows
    )
    everyone = pair_gather(jnp.concatenate([tokens[0], extra], 0), 1)
    tokens_all = everyone[:, :count].astype(f32).reshape(seqs * count, width)
    meta_f = meta_tokens.astype(f32)
    meta_all = everyone[:, count : count + meta_rows].astype(f32).reshape(META, width)
    thin = everyone[:, count + meta_rows]
    gains = thin[:, : 4 * share].reshape(seqs, 4, share).swapaxes(0, 1).astype(f32)
    gains = gains.reshape(4, width)
    gain_f, attn_norm_f, ssm_norm_f, ffn_gain_f = gains[0], gains[1], gains[2], gains[3]
    lengths = thin[:, 4 * share :].astype(jnp.int32)
    doc_count = doc_lengths.shape[1]
    lengths = 32 * lengths[:, :doc_count] + lengths[:, doc_count : 2 * doc_count]

    normed_all_f, _ = norm_rows(tokens_all, gain_f)
    normed = normed_all_f.astype(bf16)
    normed_own_f, scale_one = norm_rows(hidden_in, gain_f)
    normed_own = normed_own_f.astype(bf16)
    _, meta_scale = norm_rows(meta_f, gain_f)
    meta_normed = norm_rows(meta_all, gain_f)[0].astype(bf16)

    inner_all = w_mixer_in.shape[1] // 2
    conv_w = exchanged(padded(columns(w_mixer_in[:, :inner_all], seqs), 2, wide))
    conv_w = conv_w.reshape(width, wide)
    gate_w = exchanged(padded(columns(w_mixer_in[:, inner_all:], seqs), 2, wide))
    gate_w = gate_w.reshape(width, wide)
    query_w = lax.all_gather(w_query, "fsdp", axis=0, tiled=True)
    keyval_w = lax.all_gather(w_keyval, "fsdp", axis=0, tiled=True)
    attn_out_w = lax.all_gather(w_attn_out, "fsdp", axis=0, tiled=True)
    ff_gate_w = exchanged(columns(w_gate_up[:, :ff_all], seqs)).reshape(width, -1)
    ff_up_w = exchanged(columns(w_gate_up[:, ff_all:], seqs)).reshape(width, -1)
    out_back_all = gathered(cotangent[0], "fsdp").reshape(seqs * count, width)

    conv_in = swapped(matmul(normed, conv_w).astype(bf16).reshape(seqs, count, wide))
    gate_in = swapped(matmul(normed, gate_w).astype(bf16).reshape(seqs, count, wide))
    queries = matmul(normed_own, query_w).astype(bf16)
    keyvals = matmul(normed_own, keyval_w).astype(bf16)
    meta_kv = matmul(meta_normed, keyval_w).astype(bf16)
    query_heads = queries.reshape(count, KV_HEADS, groups, HEAD)
    piece = direct_gather(keyvals, "ctx", 2).reshape(ctx_count * count, 2 * kv_width)
    joined = jnp.concatenate([meta_kv, piece], 0)
    keys = joined[:, :kv_width].reshape(-1, KV_HEADS, HEAD)
    values = joined[:, kv_width:].reshape(-1, KV_HEADS, HEAD)
    key_pos = jnp.arange(piece.shape[0], dtype=jnp.int32)
    key_doc = doc_number(key_pos, bounds)
    shown = (key_pos[None, :] <= positions[:, None]) & (key_doc[None, :] == docs[:, None])
    shown = jnp.concatenate([jnp.full((count, META), True), shown], 1)
    scores = (
        jnp.einsum("qgha,kga->ghqk", query_heads, keys, preferred_element_type=f32) * 0.125
    )
    scores = jnp.where(shown[None, None], scores, NEG)
    top = jnp.max(scores, axis=-1, keepdims=True)
    weights = jnp.exp(scores - top)
    weights = weights / jnp.sum(weights, axis=-1, keepdims=True)
    attn_heads_f = jnp.einsum(
        "ghqk,kga->qgha", weights.astype(bf16), values, preferred_element_type=f32
    )
    attn_b = attn_heads_f.reshape(count, HEADS * HEAD).astype(bf16)
    attn_cols = exchanged(columns(attn_b, seqs)).reshape(seqs * count, -1)
    attn_proj = matmul(attn_b, attn_out_w)
    attn_branch, attn_scale = norm_rows(attn_proj, attn_norm_f)

    seq_bounds = jnp.cumsum(lengths, axis=1)[:, :-1]

    def numbers(places):
        return jnp.sum((places[:, None, None] >= seq_bounds[None]).astype(jnp.int32), axis=-1)

    seq_docs = numbers(positions)
    starts = (positions[:, None] == 0) | (seq_docs != numbers(positions - 1))
    taps_f = padded(conv_taps.astype(f32), 1, wide)
    rim = shifted(conv_in[count - (CONV - 1) :], "ctx", 1)
    extended = jnp.concatenate([rim, conv_in], 0).astype(f32)
    valid_rows = []
    for tap in range(CONV):
        earlier = positions - (CONV - 1 - tap)
        valid = (earlier[:, None] >= 0) & (numbers(earlier) == seq_docs)
        valid_rows.append(valid.astype(f32)[:, :, None])
    pre_conv = padded(conv_bias.astype(f32), 0, wide)[None, None, :]
    for tap in range(CONV):
        pre_conv = pre_conv + taps_f[tap] * extended[tap : tap + count] * valid_rows[tap]
    conv_sig = jax.nn.sigmoid(pre_conv)
    conv_out = (pre_conv * conv_sig).astype(bf16)
    conv_f = conv_out.astype(f32)
    conv_rows = conv_out.reshape(count * seqs, wide)
    select_w = padded(w_select, 0, wide)
    step_w = padded(w_step, 1, wide)
    selected = direct_sum(
        matmul(conv_rows, select_w).astype(bf16).reshape(seqs, count, -1), 3
    ).reshape(count * seqs, -1)
    step_low = selected[:, :DT_RANK]
    step_pre = matmul(step_low, step_w) + padded(step_bias.astype(f32), 0, wide)[None, :]
    step_pre = step_pre.reshape(count, seqs, wide)
    steps = jax.nn.softplus(step_pre)
    rates = -jnp.exp(padded(log_rates.astype(f32), 1, wide))
    sel = jnp.concatenate(
        [
            selected[:, DT_RANK:].astype(f32).reshape(count, seqs, 2 * STATE),
            jnp.where(starts, CUT, 0.0).astype(f32)[:, :, None],
        ],
        2,
    )
    sel = padded(sel, 2, LANES)
    spec, grid = scan_specs(count, seqs, wide, ctx_count)
    row_shape = (count, seqs, wide)
    (carry,) = scan_call(
        carry_body,
        "mamba_carry",
        grid,
        [spec["row"], spec["row"], spec["sel"], spec["rate"]],
        [spec["carry"]],
        [(STATE + 1, seqs, wide)],
        spec["one"],
        8,
        (steps, conv_f, sel, rates),
    )
    carries = direct_gather(carry.astype(bf16), "ctx", 4).astype(f32)
    scanned, states = scan_call(
        scan_body,
        "mamba_scan",
        grid,
        [spec["mine"], spec["row"], spec["row"], spec["sel"], spec["rate"], spec["carries"]],
        [spec["row"], spec["states"]],
        [row_shape, (count + 1, STATE, seqs, wide)],
        spec["two"],
        10,
        (mine, steps, conv_f, sel, rates, carries),
    )
    skip_f = padded(skip_gain.astype(f32), 0, wide)
    ssm_out = scanned + skip_f * conv_f
    gate_f = gate_in.astype(f32)
    gate_sig = jax.nn.sigmoid(gate_f)
    gate_act = gate_f * gate_sig
    mixer_mid = swapped((ssm_out * gate_act).astype(bf16)).reshape(seqs * count, wide)
    mixer_out_w = padded(w_mixer_out, 0, wide)
    mixer_proj = pair_scatter(
        matmul(mixer_mid, mixer_out_w).astype(bf16).reshape(seqs, count, width), 6
    )
    ssm_branch, ssm_scale = norm_rows(mixer_proj, ssm_norm_f)
    middle = hidden_in + 0.5 * (attn_branch + ssm_branch)

    normed_two_f, scale_two = norm_rows(middle, ffn_gain_f)
    normed_two = pair_gather(normed_two_f.astype(bf16), 7).reshape(seqs * count, width)
    gate_v = matmul(normed_two, ff_gate_w).astype(bf16).astype(f32)
    up_v = matmul(normed_two, ff_up_w).astype(bf16).astype(f32)
    ffn_sig = jax.nn.sigmoid(gate_v)
    hidden_ff = (gate_v * ffn_sig * up_v).astype(bf16)
    output = middle + scattered(matmul(hidden_ff, w_down).reshape(seqs, count, width))
    block_out = output.astype(bf16)[None]

    down_back = tmatmul(hidden_ff, out_back_all)
    hidden_back = matmul_t(out_back_all, w_down).astype(bf16).astype(f32)
    up_back = (hidden_back * gate_v * ffn_sig).astype(bf16)
    gate_back = (hidden_back * up_v * ffn_sig * (1.0 + gate_v * (1.0 - ffn_sig))).astype(bf16)
    ff_gate_back = tmatmul(normed_two, gate_back)
    ff_up_back = tmatmul(normed_two, up_back)
    normed_two_back = matmul_t(gate_back, ff_gate_w) + matmul_t(up_back, ff_up_w)
    normed_two_back = pair_scatter(normed_two_back.astype(bf16).reshape(seqs, count, width), 8)
    ffn_sums = lax.psum(
        (down_back.astype(bf16), ff_gate_back.astype(bf16), ff_up_back.astype(bf16)), "ctx"
    )
    middle_norm_back, ffn_gain_back = norm_back(middle, scale_two, ffn_gain_f, normed_two_back)
    middle_back = cotangent[0].astype(f32) + middle_norm_back
    branch_back = 0.5 * middle_back
    ssm_proj_back, ssm_gain_back = norm_back(mixer_proj, ssm_scale, ssm_norm_f, branch_back)
    attn_proj_back, attn_gain_back = norm_back(attn_proj, attn_scale, attn_norm_f, branch_back)
    ssm_proj_back = pair_gather(ssm_proj_back.astype(bf16), 9).reshape(seqs * count, width)
    attn_own_back = attn_proj_back.astype(bf16)
    attn_proj_back = gathered(attn_own_back, "fsdp").reshape(seqs * count, width)

    mixer_out_back = tmatmul(mixer_mid, ssm_proj_back)[:inner]
    mid_back = matmul_t(ssm_proj_back, mixer_out_w).astype(bf16).reshape(seqs, count, wide)
    mid_back = swapped(mid_back).astype(f32)
    ssm_back = mid_back * gate_act
    gate_in_back = mid_back * ssm_out * gate_sig * (1.0 + gate_f * (1.0 - gate_sig))
    skip_back = jnp.sum(ssm_back * conv_f, axis=(0, 1))
    (leave,) = scan_call(
        carry_back_body,
        "mamba_carry_back",
        grid,
        [spec["row"], spec["sel"], spec["rate"], spec["row"]],
        [spec["leave"]],
        [(STATE, seqs, wide)],
        spec["one"],
        8,
        (steps, sel, rates, ssm_back),
    )
    leaves = direct_gather(leave.astype(bf16), "ctx", 5).astype(f32)
    steps_back, conv_back, sel_back, rates_back = scan_call(
        scan_back_body,
        "mamba_scan_back",
        grid,
        [
            spec["mine"],
            spec["row"],
            spec["row"],
            spec["sel"],
            spec["rate"],
            spec["row"],
            spec["states"],
            spec["span"],
            spec["leaves"],
        ],
        [spec["row"], spec["row"], spec["sel"], spec["rates"]],
        [row_shape, row_shape, (count, seqs, LANES), (seqs // ROWS, STATE, wide)],
        spec["four"],
        20,
        (mine, steps, conv_f, sel, rates, ssm_back, states, carries[:, STATE], leaves),
    )
    rates_log_back = jnp.sum(rates_back, axis=0) * rates
    step_pre_back = steps_back * jax.nn.sigmoid(step_pre)
    step_shift_back = jnp.sum(step_pre_back, axis=(0, 1))
    step_pre_back = step_pre_back.astype(bf16).reshape(count * seqs, wide)
    step_w_back = tmatmul(step_low, step_pre_back)[:, :inner]
    selected_back = jnp.concatenate(
        [
            matmul_t(step_pre_back, step_w),
            sel_back[:, :, : 2 * STATE].reshape(count * seqs, 2 * STATE),
        ],
        1,
    ).astype(bf16)
    selected_back = direct_sum(selected_back.reshape(seqs, count, -1), 10)
    selected_back = selected_back.reshape(count * seqs, -1)
    select_w_back = tmatmul(conv_rows, selected_back)[:inner]
    conv_back = (
        conv_back
        + skip_f * ssm_back
        + matmul_t(selected_back, select_w).reshape(count, seqs, wide)
    )
    pre_back = conv_back * conv_sig * (1.0 + pre_conv * (1.0 - conv_sig))
    taps_bias_back = jnp.sum(pre_back, axis=(0, 1))
    tap_rows = []
    extended_back = jnp.zeros((count + CONV - 1, seqs, wide), f32)
    for tap in range(CONV):
        masked_back = pre_back * valid_rows[tap]
        tap_rows.append(jnp.sum(masked_back * extended[tap : tap + count], axis=(0, 1)))
        extended_back = extended_back + jnp.pad(
            taps_f[tap] * masked_back, ((tap, CONV - 1 - tap), (0, 0), (0, 0))
        )
    rim_back = shifted(extended_back[: CONV - 1].astype(bf16), "ctx", -1).astype(f32)
    conv_in_back = extended_back[CONV - 1 :] + jnp.pad(
        rim_back, ((count - (CONV - 1), 0), (0, 0), (0, 0))
    )
    conv_in_back = swapped(conv_in_back.astype(bf16)).reshape(seqs * count, wide)
    gate_in_back = swapped(gate_in_back.astype(bf16)).reshape(seqs * count, wide)
    conv_w_back = tmatmul(normed, conv_in_back)[:, :inner]
    gate_w_back = tmatmul(normed, gate_in_back)[:, :inner]

    attn_out_back = tmatmul(attn_cols, attn_proj_back)
    heads_back = matmul_t(attn_own_back, attn_out_w).astype(bf16)
    heads_back = heads_back.reshape(count, KV_HEADS, groups, HEAD)
    delta = jnp.sum(heads_back.astype(f32) * attn_heads_f, axis=-1)
    delta = delta.transpose(1, 2, 0)[..., None]
    weights_back = jnp.einsum("qgha,kga->ghqk", heads_back, values, preferred_element_type=f32)
    scores_back = (weights * (weights_back - delta)).astype(bf16)
    query_back = (
        jnp.einsum("ghqk,kga->qgha", scores_back, keys, preferred_element_type=f32) * 0.125
    )
    keys_back = (
        jnp.einsum("ghqk,qgha->kga", scores_back, query_heads, preferred_element_type=f32) * 0.125
    )
    values_back = jnp.einsum(
        "ghqk,qgha->kga", weights.astype(bf16), heads_back, preferred_element_type=f32
    )
    kv_back = jnp.concatenate(
        [keys_back.reshape(-1, kv_width), values_back.reshape(-1, kv_width)], 1
    )
    buffer = jnp.zeros((ctx_count, count + META, 2 * kv_width), f32)
    buffer = buffer.at[0, count:].set(kv_back[:META])
    buffer = buffer.at[:, :count].set(kv_back[META:].reshape(ctx_count, count, 2 * kv_width))
    owned = lax.psum_scatter(buffer.astype(bf16), "ctx", scatter_dimension=0, tiled=True)[0]
    query_back = query_back.reshape(count, HEADS * HEAD).astype(bf16)
    kv_own = owned[:count]
    attn_normed_back = matmul_t(query_back, query_w) + matmul_t(kv_own, keyval_w)
    meta_normed_back = matmul_t(owned[count:], keyval_w)
    qkv_back = exchanged(
        jnp.concatenate([columns(query_back, seqs), columns(kv_own, seqs)], 2)
    ).reshape(seqs * count, -1)
    meta_kv_back = exchanged(columns(owned[count:], seqs))
    meta_kv_back = jnp.sum(meta_kv_back.astype(f32), axis=0).astype(bf16)
    q_cols = w_query.shape[1] // seqs
    query_w_back = tmatmul(normed, qkv_back[:, :q_cols])
    keyval_w_back = tmatmul(normed, qkv_back[:, q_cols:]) + tmatmul(meta_normed, meta_kv_back)
    part = matmul_t(conv_in_back, conv_w) + matmul_t(gate_in_back, gate_w)
    tokens_scale = lax.rsqrt(jnp.mean(tokens_all * tokens_all, axis=-1, keepdims=True) + EPS)
    meta_all_scale = lax.rsqrt(jnp.mean(meta_all * meta_all, axis=-1, keepdims=True) + EPS)
    gain_back = (
        jnp.sum(part * tokens_all * tokens_scale, axis=0)
        + jnp.sum(attn_normed_back * hidden_in * scale_one, axis=0)
        + jnp.sum(meta_normed_back * meta_all * meta_all_scale, axis=0)
    )
    gains_back = jnp.stack([gain_back, attn_gain_back, ssm_gain_back, ffn_gain_back])
    gains_back = gains_back.astype(bf16).reshape(4, seqs, share).swapaxes(0, 1)
    tail = jnp.concatenate(
        [
            meta_normed_back.astype(bf16).reshape(seqs, meta_rows, width),
            padded(gains_back.reshape(seqs, 1, 4 * share), 2, width),
        ],
        1,
    )
    totals = pair_scatter(
        jnp.concatenate(
            [
                part.astype(bf16).reshape(seqs, count, width),
                padded(tail, 1, extra_rows),
            ],
            1,
        ),
        11,
    )
    input_norm_back, _ = norm_back(
        hidden_in, scale_one, gain_f, totals[:count] + attn_normed_back
    )
    meta_back, _ = norm_back(meta_f, meta_scale, gain_f, totals[count : count + meta_rows])
    gains_back = totals[count + meta_rows, : 4 * share]
    grad_tokens = (middle_back + input_norm_back)[None]

    early, ffn_sums = lax.optimization_barrier(
        (
            (
                attn_out_back.astype(bf16),
                gate_w_back.astype(bf16),
                mixer_out_back.astype(bf16),
            ),
            ffn_sums,
        )
    )
    early = lax.psum(early, "ctx")
    late, early = lax.optimization_barrier(
        (
            tuple(
                part.astype(bf16)
                for part in (
                    meta_back,
                    query_w_back,
                    keyval_w_back,
                    conv_w_back,
                    select_w_back,
                    step_w_back,
                )
            ),
            early,
        )
    )
    late = lax.psum(late, "ctx")
    sums = (*late[:3], early[0], late[3], early[1], late[4], late[5], early[2])
    thin = jnp.concatenate(
        [
            tap_rows[0][None],
            tap_rows[1][None],
            tap_rows[2][None],
            tap_rows[3][None],
            taps_bias_back[None],
            step_shift_back[None],
            skip_back[None],
            rates_log_back,
        ],
        0,
    )
    thin, gains = lax.psum((thin, gains_back), "ctx")
    thin = thin[:, :inner]
    gains = gains.reshape(4, share)

    def owner(part):
        rows = part.shape[0] // seqs
        return swapped(exchanged(part.reshape(seqs, rows, -1))).reshape(rows, -1).astype(f32)

    grad_gate_up = jnp.concatenate([owner(ffn_sums[1]), owner(ffn_sums[2])], 1)
    grad_mixer_in = jnp.concatenate([owner(sums[4]), owner(sums[5])], 1)
    return (
        block_out,
        grad_tokens,
        sums[0].astype(f32),
        gains[0],
        owner(sums[1]),
        owner(sums[2]),
        sums[3].astype(f32),
        grad_mixer_in,
        thin[:CONV],
        thin[CONV],
        sums[6].astype(f32),
        sums[7].astype(f32),
        thin[CONV + 1],
        thin[CONV + 3 :],
        thin[CONV + 2],
        sums[8].astype(f32),
        gains[1],
        gains[2],
        gains[3],
        grad_gate_up,
        ffn_sums[0].astype(f32),
    )


def solution(mesh):
    rows, cols, one = P("fsdp", None), P(None, "fsdp"), P("fsdp")
    split = P("fsdp", "ctx", None)
    in_specs = (
        split,
        split,
        rows,
        rows,
        one,
        rows,
        rows,
        rows,
        rows,
        cols,
        one,
        rows,
        cols,
        one,
        cols,
        one,
        rows,
        one,
        one,
        one,
        rows,
        rows,
    )
    out_specs = (
        split,
        split,
        rows,
        one,
        rows,
        rows,
        rows,
        rows,
        cols,
        one,
        rows,
        cols,
        one,
        cols,
        one,
        rows,
        one,
        one,
        one,
        rows,
        rows,
    )
    return jax.shard_map(shards, mesh=mesh, in_specs=in_specs, out_specs=out_specs, check_vma=False)
```

```python
import jax
import jax.numpy as jnp
from jax import lax
from jax.experimental import pallas as pl
from jax.experimental.pallas import tpu as pltpu
from jax.sharding import PartitionSpec as P

HEADS = 25
KV_HEADS = 5
HEAD = 64
META = 128
STATE = 16
CONV = 4
DT_RANK = 100

EPS = 1e-05
NEG = -1e30
CUT = 1e30
LANES = 128
ROWS = 8
f32 = jnp.float32
bf16 = jnp.bfloat16


def matmul(left, right):
    return jnp.dot(left, right, preferred_element_type=f32)


def tmatmul(left, right):
    return lax.dot_general(left, right, (((0,), (0,)), ((), ())), preferred_element_type=f32)


def matmul_t(left, right):
    return lax.dot_general(left, right, (((1,), (1,)), ((), ())), preferred_element_type=f32)


def norm_rows(value, gain):
    scale = lax.rsqrt(jnp.mean(value * value, axis=-1, keepdims=True) + EPS)
    return (value * scale * gain, scale)


def norm_back(value, scale, gain, upstream):
    tilted = upstream * gain
    mixing = jnp.mean(tilted * value, axis=-1, keepdims=True)
    return (
        scale * tilted - value * scale * scale * scale * mixing,
        jnp.sum(upstream * value * scale, axis=0),
    )


def doc_number(positions, bounds):
    return jnp.sum((positions[:, None] >= bounds[None, :]).astype(jnp.int32), axis=1)


def padded(array, axis, size):
    widths = [(0, 0)] * array.ndim
    widths[axis] = (0, size - array.shape[axis])
    return jnp.pad(array, widths)


def shifted(block, axis, distance):
    devices = range(lax.axis_size(axis))
    route = [(i - distance, i) for i in devices if i - distance in devices]
    return lax.ppermute(block, axis, route)


def gathered(array, axis):
    return lax.all_gather(array, axis, axis=0)


def exchanged(array):
    return lax.all_to_all(array, "fsdp", 0, 0)


def scattered(array):
    return lax.psum_scatter(array.astype(bf16), "fsdp", scatter_dimension=0, tiled=False).astype(
        f32
    )


AT = pl.DeviceIdType.MESH
ANY = pl.BlockSpec(memory_space=pl.ANY)
INSIDE = pl.BlockSpec(memory_space=pltpu.VMEM)

def greet(axis, peers):
    barrier = pltpu.get_barrier_semaphore()
    for peer in peers:
        pl.semaphore_signal(barrier, inc=1, device_id={axis: peer}, device_id_type=AT)
    pl.semaphore_wait(barrier, len(peers))

def sender(axis, src, dst, send, recv, peer):
    return pltpu.make_async_remote_copy(src_ref=src, dst_ref=dst, send_sem=send, recv_sem=recv, device_id={axis: peer}, device_id_type=AT)

def comm_call(body, name, number, ins, shape, out_spec, scratch, time=25):
    return pl.pallas_call(body, name=name, out_shape=shape, in_specs=[spec for spec, _ in ins], out_specs=out_spec, scratch_shapes=scratch,
        cost_estimate=lasting(time), compiler_params=pltpu.CompilerParams(collective_id=number, has_side_effects=True, vmem_limit_bytes=40*2**20))(*[array for _, array in ins])

def pair_gather(array, number, swaps=()):
    devices = lax.axis_size("fsdp")
    pairs = devices // 2
    many = len(swaps)

    def body(*refs):
        mine, moved = refs[0], refs[1 : many + 1]
        out, landed = refs[many + 1], refs[many + 2 : 2 * many + 2]
        own, sent, got, passed, taken, moved_sent, moved_got = refs[2 * many + 2 :]
        me = lax.axis_index("fsdp")
        pair, core = me // 2, lax.rem(me, 2)
        mate = me + 1 - 2 * core
        peers = [2 * lax.rem(pair + k, pairs) + core for k in range(1, pairs)]
        others = [lax.rem(me + k, devices) for k in range(1, devices)]
        greet("fsdp", others if many else [mate, *peers])
        first = [
            sender("fsdp", mine, out.at[me], sent.at[k], got.at[k], peer)
            for k, peer in enumerate([mate, *peers])
        ]
        for copy in first[1:]:
            copy.start()
        first[0].start()
        extra = [
            sender(
                "fsdp",
                src.at[peer],
                dst.at[me],
                moved_sent.at[m, k],
                moved_got.at[m, k],
                peer,
            )
            for m, (src, dst) in enumerate(zip(moved, landed))
            for k, peer in enumerate(others)
        ]
        for copy in extra:
            copy.start()
        local = [pltpu.make_async_copy(mine, out.at[me], own.at[0])]
        for m, (src, dst) in enumerate(zip(moved, landed)):
            local.append(pltpu.make_async_copy(src.at[me], dst.at[me], own.at[m + 1]))
        for copy in local:
            copy.start()
        second = []
        for k in range(1, pairs):
            slot = 2 * lax.rem(pair + pairs - k, pairs) + core
            first[k].wait_recv()
            copy = sender(
                "fsdp", out.at[slot], out.at[slot], passed.at[k - 1], taken.at[k - 1], mate
            )
            copy.start()
            second.append(copy)
        first[0].wait_recv()
        for copy in first:
            copy.wait_send()
        for copy in second + extra + local:
            copy.wait()

    dma = pltpu.SemaphoreType.DMA
    shapes = [jax.ShapeDtypeStruct((devices,) + array.shape, array.dtype)]
    shapes += [jax.ShapeDtypeStruct(swap.shape, swap.dtype) for swap in swaps]
    result = comm_call(
        body,
        "pair_gather",
        number,
        [(ANY, array)] + [(ANY, swap) for swap in swaps],
        shapes,
        [ANY] * (many + 1),
        [dma((many + 1,)), dma((pairs,)), dma((pairs,)), dma((pairs - 1,)), dma((pairs - 1,))]
        + [dma((max(many, 1), devices - 1))] * 2,
    )
    return result if many else result[0]


def direct_many(arrays, modes, axis, number):
    devices = lax.axis_size(axis)
    many = len(arrays)

    def body(*refs):
        mine, out, (own, sent, got) = refs[:many], refs[many : 2 * many], refs[2 * many :]
        me = lax.axis_index(axis)
        peers = [lax.rem(me + k, devices) for k in range(1, devices)]
        greet(axis, peers)
        copies = []
        for m, (src, dst, mode) in enumerate(zip(mine, out, modes)):
            for k, peer in enumerate(peers):
                part = src if mode == "gather" else src.at[peer]
                copies.append(sender(axis, part, dst.at[me], sent.at[m, k], got.at[m, k], peer))
        for copy in copies:
            copy.start()
        for m, (src, dst, mode) in enumerate(zip(mine, out, modes)):
            part = src if mode == "gather" else src.at[me]
            copies.append(pltpu.make_async_copy(part, dst.at[me], own.at[m]))
            copies[-1].start()
        for copy in copies:
            copy.wait()

    dma = pltpu.SemaphoreType.DMA
    shapes = [
        jax.ShapeDtypeStruct(
            (devices,) + array.shape if mode == "gather" else array.shape, array.dtype
        )
        for array, mode in zip(arrays, modes)
    ]
    return comm_call(
        body,
        "direct_many",
        number,
        [(ANY, array) for array in arrays],
        shapes,
        [ANY] * many,
        [dma((many,)), dma((many, devices - 1)), dma((many, devices - 1))],
    )


def split_columns(weight, cols, wide, seqs):
    rows = weight.shape[0]
    kinds = weight.shape[1] // (cols * seqs)

    def body(mine, *outs):
        for m, out in enumerate(outs):
            for f in range(seqs):
                first = (m * seqs + f) * cols
                out[f, :, :cols] = mine[:, first : first + cols]
                if wide > cols:
                    out[f, :, cols:] = jnp.zeros((rows, wide - cols), bf16)

    return pl.pallas_call(
        body,
        name="split_columns",
        out_shape=[jax.ShapeDtypeStruct((seqs, rows, wide), bf16)] * kinds,
        in_specs=[INSIDE],
        out_specs=[INSIDE] * kinds,
        compiler_params=pltpu.CompilerParams(vmem_limit_bytes=40 * 2**20),
    )(weight)


def pair_scatter(array, number):
    devices = array.shape[0]; pairs = devices // 2; shape = array.shape[1:]
    def body(mine, out, near, summed, far, sent, got, passed, taken):
        me = lax.axis_index("fsdp"); pair = me // 2; core = lax.rem(me, 2); mate = me + 1 - 2 * core
        places = [lax.rem(pair + k, pairs) for k in range(1, pairs + 1)]
        greet("fsdp", [mate, *[2 * q + core for q in places[:-1]]])
        first = [sender("fsdp", mine.at[2 * q + 1 - core], near.at[k], sent.at[k], got.at[k], mate) for k, q in enumerate(places)]
        for copy in first: copy.start()
        second = []
        for k, q in enumerate(places):
            first[k].wait_recv()
            total = mine[2 * q + core].astype(f32) + near[k].astype(f32)
            if k < pairs - 1:
                summed[k] = total.astype(bf16)
                copy = sender("fsdp", summed.at[k], far.at[k], passed.at[k], taken.at[k], 2 * q + core)
                copy.start(); second.append(copy)
            else:
                out[...] = total
        for copy in second:
            copy.wait_recv()
        total = out[...]
        for k in range(pairs - 1): total = total + far[k].astype(f32)
        out[...] = total
        for copy in first: copy.wait_send()
        for copy in second: copy.wait_send()
    return comm_call(body, "pair_scatter", number, [(INSIDE, array)], jax.ShapeDtypeStruct(shape, f32), INSIDE,
        [pltpu.VMEM((pairs,) + shape, bf16), pltpu.VMEM((pairs-1,) + shape, bf16), pltpu.VMEM((pairs-1,) + shape, bf16),
         pltpu.SemaphoreType.DMA((pairs,)), pltpu.SemaphoreType.DMA((pairs,)), pltpu.SemaphoreType.DMA((pairs-1,)), pltpu.SemaphoreType.DMA((pairs-1,))])

def direct_sum(array, number):
    devices = array.shape[0]; shape = array.shape[1:]
    def body(mine, out, near, sent, got, passed, taken):
        me = lax.axis_index("fsdp")
        peers = [lax.rem(me + k, devices) for k in range(1, devices)]
        greet("fsdp", peers)
        first = [sender("fsdp", mine.at[peer], near.at[k], sent.at[k], got.at[k], peer) for k, peer in enumerate(peers)]
        for copy in first: copy.start()
        total = mine[me].astype(f32)
        for k in range(devices - 1):
            first[k].wait_recv()
            total = total + near[k].astype(f32)
        out[me] = total.astype(bf16)
        second = [sender("fsdp", out.at[me], out.at[me], passed.at[k], taken.at[k], peer) for k, peer in enumerate(peers)]
        for copy in second: copy.start()
        for copy in second: copy.wait()
        for copy in first: copy.wait_send()
    return comm_call(body, "direct_sum", number, [(INSIDE, array)], jax.ShapeDtypeStruct(array.shape, bf16), INSIDE,
        [pltpu.VMEM((devices-1,) + shape, bf16)] + [pltpu.SemaphoreType.DMA((devices-1,))] * 4)

def finish(part, number):
    devices = lax.axis_size("fsdp")
    line = lax.axis_size("ctx")
    total = part.shape[0]
    half, sub = total // 2, total // devices

    def body(part, part_out, near, mid, done, own, sent, got, back_sent, back_got, out_sent, out_got):
        me, place = lax.axis_index("fsdp"), lax.axis_index("ctx")
        barrier = pltpu.get_barrier_semaphore()
        peers = [lax.rem(me + k, devices) for k in range(1, devices)]
        for peer in peers:
            pl.semaphore_signal(barrier, inc=1, device_id={"fsdp": peer}, device_id_type=AT)
        for step in (1, line - 1):
            pl.semaphore_signal(barrier, inc=1, device_id={"ctx": lax.rem(place + step, line)}, device_id_type=AT)
        pl.semaphore_wait(barrier, devices + 1)

        def moves(way, i):
            slot = i + way * half
            onward = place + 1 - 2 * way
            back = place - 1 + 2 * way
            begin = sender("ctx", part.at[slot], near.at[slot], sent.at[slot], got.at[slot], onward)
            relay = sender("ctx", mid.at[slot], near.at[slot], sent.at[slot], got.at[slot], onward)
            spread = sender("ctx", done.at[slot], done.at[slot], back_sent.at[slot], back_got.at[slot], back)
            return slot, begin, relay, spread

        def ends(way):
            return (0, line - 1) if way == 0 else (line - 1, 0)

        def turn(s, _):
            for way in range(2):
                first, last = ends(way)
                hops = place if way == 0 else line - 1 - place

                def inward(i):
                    slot, begin, relay, spread = moves(way, i)

                    @pl.when(place == first)
                    def _():
                        begin.start()

                    @pl.when(place != first)
                    def _():
                        relay.wait_recv()

                        @pl.when(place != last)
                        def _():
                            mid[slot] = (part[slot].astype(f32) + near[slot].astype(f32)).astype(bf16)
                            relay.start()

                        @pl.when(place == last)
                        def _():
                            done[slot] = (part[slot].astype(f32) + near[slot].astype(f32)).astype(bf16)

                def outward(i):
                    slot, begin, relay, spread = moves(way, i)

                    @pl.when(place != last)
                    def _():
                        spread.wait_recv()

                    @pl.when(place != first)
                    def _():
                        spread.start()

                    owner, rank = slot // sub, lax.rem(slot, sub)
                    here = me * sub + rank

                    @pl.when(me != owner)
                    def _():
                        sender("fsdp", done.at[slot], part_out.at[here], out_sent.at[slot], out_got.at[here], owner).start()

                    @pl.when(me == owner)
                    def _():
                        pltpu.make_async_copy(done.at[slot], part_out.at[slot], own.at[rank]).start()

                i = s - hops
                pl.when((i >= 0) & (i < half))(lambda: inward(i))
                k = s - (2 * (line - 1) - hops)
                pl.when((k >= 0) & (k < half))(lambda: outward(k))
            return 0

        lax.fori_loop(0, half + 2 * (line - 1), turn, 0)

        def drain(i, _):
            for way in range(2):
                first, last = ends(way)
                slot, begin, relay, spread = moves(way, i)

                @pl.when(place == first)
                def _():
                    begin.wait_send()

                @pl.when((place != first) & (place != last))
                def _():
                    relay.wait_send()

                @pl.when(place != first)
                def _():
                    spread.wait_send()

                owner, rank = slot // sub, lax.rem(slot, sub)
                copy = sender("fsdp", done.at[slot], part_out.at[slot], out_sent.at[slot], out_got.at[slot], owner)

                @pl.when(me != owner)
                def _():
                    copy.wait_send()
                    copy.wait_recv()

                @pl.when(me == owner)
                def _():
                    pltpu.make_async_copy(done.at[slot], part_out.at[slot], own.at[rank]).wait()
            return 0

        lax.fori_loop(0, half, drain, 0)

    dma = pltpu.SemaphoreType.DMA
    return pl.pallas_call(
        body,
        name="finish",
        out_shape=jax.ShapeDtypeStruct(part.shape, part.dtype),
        in_specs=[INSIDE],
        out_specs=ANY,
        scratch_shapes=[pltpu.VMEM(part.shape, bf16)] * 3
        + [dma((sub,))]
        + [dma((total,))] * 6,
        compiler_params=pltpu.CompilerParams(
            collective_id=number, has_side_effects=True, vmem_limit_bytes=50 * 2**20
        ),
        cost_estimate=pl.CostEstimate(flops=0, bytes_accessed=400 * 2**20, transcendentals=0),
    )(part)


def columns(weight, count):
    return weight.reshape(weight.shape[0], count, -1).swapaxes(0, 1)


def after(value, *earlier):
    zero = 0.0
    for array in earlier:
        corner = lax.slice(array, (0,) * array.ndim, (1,) * array.ndim).reshape(())
        zero = zero + jnp.minimum(jnp.abs(corner.astype(f32)), 0.0)
    return jax.tree.map(lambda part: part + zero.astype(part.dtype), value)


def relayed(value, earlier, rounds):
    corner = lax.slice(earlier, (0,) * earlier.ndim, (1,) * earlier.ndim).reshape(1, 1)
    token = jnp.broadcast_to(corner.astype(f32), (ROWS, LANES))
    devices = lax.axis_size("fsdp")
    for _ in range(rounds):
        token = lax.ppermute(token, "fsdp", [(i, i ^ 1) for i in range(devices)])
    return after(value, token)


def swapped(array):
    return array.swapaxes(0, 1)


def rates_of(rate_ref):
    return [jnp.broadcast_to(rate_ref[n : n + 1, :], (ROWS, LANES)) for n in range(STATE)]


def spread(sel_ref, picks, cuts):
    @pl.when(pl.program_id(1) == 0)
    def _():
        def turn(t, _):
            sel = sel_ref[t]
            for first, into in picks:
                for n in range(STATE):
                    lane = sel[:, first + n : first + n + 1]
                    into[t, n] = jnp.broadcast_to(lane, (ROWS, LANES))
            cuts[t] = jnp.broadcast_to(sel[:, 2 * STATE : 2 * STATE + 1], (ROWS, LANES))
            return 0

        lax.fori_loop(0, sel_ref.shape[0], turn, 0, unroll=4)


def carry_body(step_ref, conv_ref, sel_ref, rate_ref, out_ref, enters, cuts):
    rates = rates_of(rate_ref)
    spread(sel_ref, [(0, enters)], cuts)

    def turn(t, state):
        step = step_ref[t]
        push = step * conv_ref[t]
        fade = step + cuts[t]
        new = [
            jnp.exp(fade * rates[n]) * state[n] + enters[t, n] * push for n in range(STATE)
        ]
        return (*new, state[STATE] + fade)

    zero = jnp.zeros((ROWS, LANES), f32)
    state = lax.fori_loop(0, step_ref.shape[0], turn, (zero,) * (STATE + 1), unroll=8)
    for n in range(STATE + 1):
        out_ref[n] = state[n]


def scan_body(
    mine_ref,
    step_ref,
    conv_ref,
    sel_ref,
    rate_ref,
    carry_ref,
    out_ref,
    states_ref,
    enters,
    exits,
    cuts,
):
    rates = rates_of(rate_ref)
    spread(sel_ref, [(0, enters), (STATE, exits)], cuts)

    def join(j, state):
        return tuple(
            jnp.exp(rates[n] * carry_ref[j, STATE]) * state[n] + carry_ref[j, n]
            for n in range(STATE)
        )

    zero = jnp.zeros((ROWS, LANES), f32)
    state = lax.fori_loop(0, mine_ref[0], join, (zero,) * STATE)
    for n in range(STATE):
        states_ref[0, n] = state[n]

    def turn(t, state):
        step = step_ref[t]
        push = step * conv_ref[t]
        fade = step + cuts[t]
        new, total = [], zero
        for n in range(STATE):
            now = jnp.exp(fade * rates[n]) * state[n] + enters[t, n] * push
            states_ref[t + 1, n] = now
            total = total + exits[t, n] * now
            new.append(now)
        out_ref[t] = total
        return tuple(new)

    lax.fori_loop(0, step_ref.shape[0], turn, state, unroll=8)


def carry_back_body(step_ref, sel_ref, rate_ref, up_ref, out_ref, exits, cuts):
    rates = rates_of(rate_ref)
    spread(sel_ref, [(STATE, exits)], cuts)
    count = step_ref.shape[0]

    def turn(i, state):
        t = count - 1 - i
        up = up_ref[t]
        fade = step_ref[t] + cuts[t]
        return tuple(
            jnp.exp(fade * rates[n]) * (exits[t, n] * up + state[n]) for n in range(STATE)
        )

    zero = jnp.zeros((ROWS, LANES), f32)
    state = lax.fori_loop(0, count, turn, (zero,) * STATE, unroll=8)
    for n in range(STATE):
        out_ref[n] = state[n]


def scan_back_body(
    mine_ref,
    step_ref,
    conv_ref,
    sel_ref,
    rate_ref,
    up_ref,
    states_ref,
    span_ref,
    leave_ref,
    step_out,
    conv_out,
    sel_out,
    rate_out,
    enter_terms,
    exit_terms,
    enters,
    exits,
    cuts,
):
    rates = rates_of(rate_ref)
    spread(sel_ref, [(0, enters), (STATE, exits)], cuts)
    count = step_ref.shape[0]
    devices = span_ref.shape[0]
    zero = jnp.zeros((ROWS, LANES), f32)

    def join(i, state):
        j = devices - 1 - i
        return tuple(
            jnp.exp(rates[n] * span_ref[j]) * state[n] + leave_ref[j, n] for n in range(STATE)
        )

    state = lax.fori_loop(0, devices - 1 - mine_ref[0], join, (zero,) * STATE)
    state = state + (zero,) * STATE
    place = lax.broadcasted_iota(jnp.int32, (2 * LANES, LANES), 1)
    half = lax.broadcasted_iota(jnp.int32, (2 * LANES, LANES), 0) // LANES
    span = count // 2

    @pl.when(pl.program_id(1) == 0)
    def _():
        sel_out[...] = jnp.zeros_like(sel_out)

    for start in (span, 0):

        def turn(i, carried):
            t = start + span - 1 - i
            step, conv, up = step_ref[t], conv_ref[t], up_ref[t]
            push = step * conv
            fade = step + cuts[t]
            rows = pl.ds(pl.multiple_of((t - start) * ROWS, ROWS), ROWS)
            push_back, fade_back, new, rate_back = zero, zero, [], []
            for n in range(STATE):
                lanes = slice(n * LANES, (n + 1) * LANES)
                total = exits[t, n] * up + carried[n]
                exit_terms[rows, lanes] = up * states_ref[t + 1, n]
                enter_terms[rows, lanes] = total * push
                push_back = push_back + total * enters[t, n]
                earlier = jnp.exp(fade * rates[n]) * total
                slope = earlier * states_ref[t, n]
                fade_back = fade_back + slope * rates[n]
                new.append(earlier)
                rate_back.append(carried[STATE + n] + slope * step)
            step_out[t] = push_back * conv + fade_back
            conv_out[t] = push_back * step
            return (*new, *rate_back)

        state = lax.fori_loop(0, span, turn, state, unroll=4)
        total = jnp.zeros((span * ROWS, LANES), f32)
        for n in range(0, STATE, 2):
            lanes = slice(n * LANES, (n + 2) * LANES)
            pick = (place == n + half).astype(bf16)
            total = total + matmul(enter_terms[:, lanes].astype(bf16), pick)
            pick = (place == STATE + n + half).astype(bf16)
            total = total + matmul(exit_terms[:, lanes].astype(bf16), pick)
        sel_out[start : start + span] += total.reshape(span, ROWS, LANES)
    for n in range(STATE):
        rate_out[0, n : n + 1] = jnp.sum(state[STATE + n], axis=0, keepdims=True)


def lasting(time):
    return pl.CostEstimate(flops=0, bytes_accessed=int(time * 3.6e6), transcendentals=0)


def scan_specs(count, seqs, wide, devices):
    specs = dict(
        mine=pl.BlockSpec(memory_space=pltpu.SMEM),
        row=pl.BlockSpec((count, ROWS, LANES), lambda s, c: (0, s, c)),
        sel=pl.BlockSpec((count, ROWS, LANES), lambda s, c: (0, s, 0)),
        rate=pl.BlockSpec((STATE, LANES), lambda s, c: (0, c)),
        carry=pl.BlockSpec((STATE + 1, ROWS, LANES), lambda s, c: (0, s, c)),
        carries=pl.BlockSpec((devices, STATE + 1, ROWS, LANES), lambda s, c: (0, 0, s, c)),
        leave=pl.BlockSpec((STATE, ROWS, LANES), lambda s, c: (0, s, c)),
        leaves=pl.BlockSpec((devices, STATE, ROWS, LANES), lambda s, c: (0, 0, s, c)),
        span=pl.BlockSpec((devices, ROWS, LANES), lambda s, c: (0, s, c)),
        states=pl.BlockSpec((count + 1, STATE, ROWS, LANES), lambda s, c: (0, 0, s, c)),
        rates=pl.BlockSpec((1, STATE, LANES), lambda s, c: (s, 0, c)),
    )
    spreads = pltpu.VMEM((count, STATE, ROWS, LANES), f32)
    cuts = pltpu.VMEM((count, ROWS, LANES), f32)
    terms = pltpu.VMEM((count // 2 * ROWS, STATE * LANES), f32)
    specs["one"], specs["two"] = [spreads, cuts], [spreads, spreads, cuts]
    specs["four"] = [terms, terms, spreads, spreads, cuts]
    return specs, (seqs // ROWS, wide // LANES)


def scan_call(body, name, grid, ins, outs, shapes, scratch, work, args):
    return pl.pallas_call(
        body,
        name=name,
        grid=grid,
        in_specs=ins,
        out_specs=outs,
        out_shape=[jax.ShapeDtypeStruct(shape, f32) for shape in shapes],
        scratch_shapes=scratch,
        compiler_params=pltpu.CompilerParams(
            dimension_semantics=("arbitrary", "arbitrary"), vmem_limit_bytes=60 * 2**20
        ),
        cost_estimate=lasting(work),
    )(*args)


def shards(
    tokens,
    cotangent,
    doc_lengths,
    meta_tokens,
    norm_gain,
    w_query,
    w_keyval,
    w_attn_out,
    w_mixer_in,
    conv_taps,
    conv_bias,
    w_select,
    w_step,
    step_bias,
    log_rates,
    skip_gain,
    w_mixer_out,
    attn_gain,
    ssm_gain,
    ffn_norm_gain,
    w_gate_up,
    w_down,
):
    count = tokens.shape[1]
    width = tokens.shape[2]
    seqs = lax.axis_size("fsdp")
    ctx_index = lax.axis_index("ctx")
    ctx_count = lax.axis_size("ctx")
    inner = conv_bias.shape[0]
    wide = -(-inner // LANES) * LANES
    kv_width = KV_HEADS * HEAD
    groups = HEADS // KV_HEADS
    mine = jnp.reshape(ctx_index, (1,)).astype(jnp.int32)

    positions = ctx_index * count + jnp.arange(count, dtype=jnp.int32)
    last_pos = ctx_index * count + count - 1
    bounds = jnp.cumsum(doc_lengths[0])[:-1]
    docs = doc_number(positions, bounds)

    hidden_in = tokens[0].astype(f32)
    meta_rows = meta_tokens.shape[0]
    share = norm_gain.shape[0]
    extra_rows = -(-(meta_rows + 1) // 16) * 16
    few = doc_lengths[0]
    thin = jnp.concatenate(
        [
            norm_gain,
            attn_gain,
            ssm_gain,
            ffn_norm_gain,
            (few // 32).astype(bf16),
            (few % 32).astype(bf16),
        ]
    )
    extra = padded(
        jnp.concatenate([meta_tokens, padded(thin, 0, width)[None]], 0), 0, extra_rows
    )
    ff_cols = w_gate_up.shape[1] // (2 * seqs)
    conv_w, gate_w = split_columns(w_mixer_in, inner, wide, seqs)
    everyone, conv_w = pair_gather(jnp.concatenate([tokens[0], extra], 0), 1, [conv_w])
    conv_w = conv_w.reshape(width, wide)
    tokens_all = everyone[:, :count].astype(f32).reshape(seqs * count, width)
    meta_f = meta_tokens.astype(f32)
    meta_all = everyone[:, count : count + meta_rows].astype(f32).reshape(META, width)
    thin = everyone[:, count + meta_rows]
    gains = thin[:, : 4 * share].reshape(seqs, 4, share).swapaxes(0, 1).astype(f32)
    gains = gains.reshape(4, width)
    gain_f, attn_norm_f, ssm_norm_f, ffn_gain_f = gains[0], gains[1], gains[2], gains[3]
    lengths = thin[:, 4 * share :].astype(jnp.int32)
    doc_count = doc_lengths.shape[1]
    lengths = 32 * lengths[:, :doc_count] + lengths[:, doc_count : 2 * doc_count]

    normed_all_f, _ = norm_rows(tokens_all, gain_f)
    normed = normed_all_f.astype(bf16)
    normed_own_f, scale_one = norm_rows(hidden_in, gain_f)
    normed_own = normed_own_f.astype(bf16)
    _, meta_scale = norm_rows(meta_f, gain_f)
    meta_normed = norm_rows(meta_all, gain_f)[0].astype(bf16)

    gate_w = exchanged(gate_w).reshape(width, wide)
    keyval_w = lax.all_gather(w_keyval, "fsdp", axis=0, tiled=True)
    query_w = lax.all_gather(w_query, "fsdp", axis=0, tiled=True)
    ff_wide = -(-ff_cols // LANES) * LANES
    ff_gate_w, ff_up_w = split_columns(w_gate_up, ff_cols, ff_wide, seqs)
    ff_gate_w = exchanged(ff_gate_w).reshape(width, ff_wide)
    ff_up_w = exchanged(ff_up_w).reshape(width, ff_wide)

    conv_in = swapped(matmul(normed, conv_w).astype(bf16).reshape(seqs, count, wide))
    gate_in = swapped(matmul(normed, gate_w).astype(bf16).reshape(seqs, count, wide))
    seq_bounds = jnp.cumsum(lengths, axis=1)[:, :-1]

    def numbers(places):
        return jnp.sum((places[:, None, None] >= seq_bounds[None]).astype(jnp.int32), axis=-1)

    seq_docs = numbers(positions)
    starts = (positions[:, None] == 0) | (seq_docs != numbers(positions - 1))
    taps_f = padded(conv_taps.astype(f32), 1, wide)
    rim = shifted(conv_in[count - (CONV - 1) :], "ctx", 1)
    extended = jnp.concatenate([rim, conv_in], 0).astype(f32)
    valid_rows = []
    for tap in range(CONV):
        earlier = positions - (CONV - 1 - tap)
        valid = (earlier[:, None] >= 0) & (numbers(earlier) == seq_docs)
        valid_rows.append(valid.astype(f32)[:, :, None])
    pre_conv = padded(conv_bias.astype(f32), 0, wide)[None, None, :]
    for tap in range(CONV):
        pre_conv = pre_conv + taps_f[tap] * extended[tap : tap + count] * valid_rows[tap]
    conv_sig = jax.nn.sigmoid(pre_conv)
    conv_out = (pre_conv * conv_sig).astype(bf16)
    conv_f = conv_out.astype(f32)
    conv_rows = conv_out.reshape(count * seqs, wide)
    select_w = padded(w_select, 0, wide)
    step_w = padded(w_step, 1, wide)
    selected = direct_sum(
        matmul(conv_rows, select_w).astype(bf16).reshape(seqs, count, -1), 3
    ).reshape(count * seqs, -1)
    step_low = selected[:, :DT_RANK]
    step_pre = matmul(step_low, step_w) + padded(step_bias.astype(f32), 0, wide)[None, :]
    step_pre = step_pre.reshape(count, seqs, wide)
    steps = jax.nn.softplus(step_pre)
    rates = -jnp.exp(padded(log_rates.astype(f32), 1, wide))
    sel = jnp.concatenate(
        [
            selected[:, DT_RANK:].astype(f32).reshape(count, seqs, 2 * STATE),
            jnp.where(starts, CUT, 0.0).astype(f32)[:, :, None],
        ],
        2,
    )
    sel = padded(sel, 2, LANES)
    spec, grid = scan_specs(count, seqs, wide, ctx_count)
    row_shape = (count, seqs, wide)
    (carry,) = scan_call(
        carry_body,
        "mamba_carry",
        grid,
        [spec["row"], spec["row"], spec["sel"], spec["rate"]],
        [spec["carry"]],
        [(STATE + 1, seqs, wide)],
        spec["one"],
        15,
        (steps, conv_f, sel, rates),
    )
    keyvals = matmul(normed_own, keyval_w).astype(bf16)
    carries, keyvals_all = direct_many(
        [carry.astype(bf16), keyvals], ["gather", "gather"], "ctx", 4
    )
    carries = carries.astype(f32)
    attn_out_w = lax.all_gather(w_attn_out, "fsdp", axis=0, tiled=True)
    out_back_all = gathered(cotangent[0], "fsdp").reshape(seqs * count, width)
    scanned, states = scan_call(
        scan_body,
        "mamba_scan",
        grid,
        [spec["mine"], spec["row"], spec["row"], spec["sel"], spec["rate"], spec["carries"]],
        [spec["row"], spec["states"]],
        [row_shape, (count + 1, STATE, seqs, wide)],
        spec["two"],
        26,
        (mine, steps, conv_f, sel, rates, carries),
    )
    skip_f = padded(skip_gain.astype(f32), 0, wide)
    ssm_out = scanned + skip_f * conv_f
    gate_f = gate_in.astype(f32)
    gate_sig = jax.nn.sigmoid(gate_f)
    gate_act = gate_f * gate_sig
    mixer_mid = swapped((ssm_out * gate_act).astype(bf16)).reshape(seqs * count, wide)
    mixer_out_w = padded(w_mixer_out, 0, wide)
    mixer_proj = pair_scatter(
        matmul(mixer_mid, mixer_out_w).astype(bf16).reshape(seqs, count, width), 6
    )
    queries = matmul(normed_own, query_w).astype(bf16)
    meta_kv = matmul(meta_normed, keyval_w).astype(bf16)
    query_heads = queries.reshape(count, KV_HEADS, groups, HEAD)
    piece = keyvals_all.reshape(ctx_count * count, 2 * kv_width)
    joined = jnp.concatenate([meta_kv, piece], 0)
    keys = joined[:, :kv_width].reshape(-1, KV_HEADS, HEAD)
    values = joined[:, kv_width:].reshape(-1, KV_HEADS, HEAD)
    key_pos = jnp.arange(piece.shape[0], dtype=jnp.int32)
    key_doc = doc_number(key_pos, bounds)
    shown = (key_pos[None, :] <= positions[:, None]) & (key_doc[None, :] == docs[:, None])
    shown = jnp.concatenate([jnp.full((count, META), True), shown], 1)
    scores = (
        jnp.einsum("qgha,kga->ghqk", query_heads, keys, preferred_element_type=f32) * 0.125
    )
    scores = jnp.where(shown[None, None], scores, NEG)
    top = jnp.max(scores, axis=-1, keepdims=True)
    weights = jnp.exp(scores - top)
    weights = weights / jnp.sum(weights, axis=-1, keepdims=True)
    attn_heads_f = jnp.einsum(
        "ghqk,kga->qgha", weights.astype(bf16), values, preferred_element_type=f32
    )
    attn_b = attn_heads_f.reshape(count, HEADS * HEAD).astype(bf16)
    attn_proj = matmul(attn_b, attn_out_w)
    attn_branch, attn_scale = norm_rows(attn_proj, attn_norm_f)

    ssm_branch, ssm_scale = norm_rows(mixer_proj, ssm_norm_f)
    middle = hidden_in + 0.5 * (attn_branch + ssm_branch)

    normed_two_f, scale_two = norm_rows(middle, ffn_gain_f)
    normed_two = pair_gather(normed_two_f.astype(bf16), 7).reshape(seqs * count, width)
    gate_v = matmul(normed_two, ff_gate_w).astype(bf16).astype(f32)
    up_v = matmul(normed_two, ff_up_w).astype(bf16).astype(f32)
    ffn_sig = jax.nn.sigmoid(gate_v)
    hidden_ff = (gate_v * ffn_sig * up_v).astype(bf16)
    down_w = padded(w_down, 0, ff_wide)
    output = matmul(hidden_ff, down_w).astype(bf16)

    down_back = tmatmul(hidden_ff, out_back_all)[:ff_cols]
    hidden_back = matmul_t(out_back_all, down_w).astype(bf16).astype(f32)
    up_back = (hidden_back * gate_v * ffn_sig).astype(bf16)
    gate_back = (hidden_back * up_v * ffn_sig * (1.0 + gate_v * (1.0 - ffn_sig))).astype(bf16)
    ff_gate_back = tmatmul(normed_two, gate_back)
    ff_up_back = tmatmul(normed_two, up_back)
    normed_two_back = matmul_t(gate_back, ff_gate_w) + matmul_t(up_back, ff_up_w)
    ffn_grads = (down_back.astype(bf16), ff_gate_back.astype(bf16), ff_up_back.astype(bf16))
    ffn_sums = lax.psum(ffn_grads, "ctx")
    normed_two_back = after(normed_two_back.astype(bf16), *ffn_grads)
    normed_two_back = pair_scatter(normed_two_back.reshape(seqs, count, width), 8)
    ffn_gain_f = relayed(ffn_gain_f, normed_two_back, 2)
    middle_norm_back, ffn_gain_back = norm_back(middle, scale_two, ffn_gain_f, normed_two_back)
    middle_back = cotangent[0].astype(f32) + middle_norm_back
    branch_back = 0.5 * middle_back
    ssm_proj_back, ssm_gain_back = norm_back(mixer_proj, ssm_scale, ssm_norm_f, branch_back)
    attn_proj_back, attn_gain_back = norm_back(attn_proj, attn_scale, attn_norm_f, branch_back)
    attn_own_back = attn_proj_back.astype(bf16)
    proj_back = pair_gather(
        jnp.concatenate([ssm_proj_back.astype(bf16), attn_own_back], 0), 9
    )
    ssm_proj_back = proj_back[:, :count].reshape(seqs * count, width)
    attn_proj_back = proj_back[:, count:].reshape(seqs * count, width)

    mixer_out_back = tmatmul(mixer_mid, ssm_proj_back)[:inner].astype(bf16)
    mid_back = matmul_t(ssm_proj_back, mixer_out_w).astype(bf16).reshape(seqs, count, wide)
    mid_back = swapped(mid_back).astype(f32)
    ssm_back = mid_back * gate_act
    gate_in_back = mid_back * ssm_out * gate_sig * (1.0 + gate_f * (1.0 - gate_sig))
    skip_back = jnp.sum(ssm_back * conv_f, axis=(0, 1))
    (leave,) = scan_call(
        carry_back_body,
        "mamba_carry_back",
        grid,
        [spec["row"], spec["sel"], spec["rate"], spec["row"]],
        [spec["leave"]],
        [(STATE, seqs, wide)],
        spec["one"],
        15,
        (steps, sel, rates, ssm_back),
    )
    heads_back = matmul_t(attn_own_back, attn_out_w).astype(bf16)
    heads_back = heads_back.reshape(count, KV_HEADS, groups, HEAD)
    delta = jnp.sum(heads_back.astype(f32) * attn_heads_f, axis=-1)
    delta = delta.transpose(1, 2, 0)[..., None]
    weights_back = jnp.einsum("qgha,kga->ghqk", heads_back, values, preferred_element_type=f32)
    scores_back = (weights * (weights_back - delta)).astype(bf16)
    query_back = (
        jnp.einsum("ghqk,kga->qgha", scores_back, keys, preferred_element_type=f32) * 0.125
    )
    keys_back = (
        jnp.einsum("ghqk,qgha->kga", scores_back, query_heads, preferred_element_type=f32) * 0.125
    )
    values_back = jnp.einsum(
        "ghqk,qgha->kga", weights.astype(bf16), heads_back, preferred_element_type=f32
    )
    kv_back = jnp.concatenate(
        [keys_back.reshape(-1, kv_width), values_back.reshape(-1, kv_width)], 1
    )
    meta_own = META // ctx_count
    buffer = jnp.concatenate(
        [
            kv_back[META:].reshape(ctx_count, count, 2 * kv_width),
            kv_back[:META].reshape(ctx_count, meta_own, 2 * kv_width),
        ],
        1,
    ).astype(bf16)
    query_back = query_back.reshape(count, HEADS * HEAD).astype(bf16)
    leaves, owned = direct_many([leave.astype(bf16), buffer], ["gather", "swap"], "ctx", 5)
    leaves = leaves.astype(f32)
    owned = jnp.sum(owned.astype(f32), axis=0).astype(bf16)
    kv_own, meta_kv_own = owned[:count], owned[count:]
    steps_back, conv_back, sel_back, rates_back = scan_call(
        scan_back_body,
        "mamba_scan_back",
        grid,
        [
            spec["mine"],
            spec["row"],
            spec["row"],
            spec["sel"],
            spec["rate"],
            spec["row"],
            spec["states"],
            spec["span"],
            spec["leaves"],
        ],
        [spec["row"], spec["row"], spec["sel"], spec["rates"]],
        [row_shape, row_shape, (count, seqs, LANES), (seqs // ROWS, STATE, wide)],
        spec["four"],
        47,
        (mine, steps, conv_f, sel, rates, ssm_back, states, carries[:, STATE], leaves),
    )
    rates_log_back = jnp.sum(rates_back, axis=0) * rates
    step_pre_back = steps_back * jax.nn.sigmoid(step_pre)
    step_shift_back = jnp.sum(step_pre_back, axis=(0, 1))
    step_pre_back = step_pre_back.astype(bf16).reshape(count * seqs, wide)
    step_w_back = tmatmul(step_low, step_pre_back)
    selected_back = jnp.concatenate(
        [
            matmul_t(step_pre_back, step_w),
            sel_back[:, :, : 2 * STATE].reshape(count * seqs, 2 * STATE),
        ],
        1,
    ).astype(bf16)
    selected_back = direct_sum(selected_back.reshape(seqs, count, -1), 10)
    selected_back = selected_back.reshape(count * seqs, -1)
    select_w_back = tmatmul(conv_rows, selected_back)[:inner]
    conv_back = (
        conv_back
        + skip_f * ssm_back
        + matmul_t(selected_back, select_w).reshape(count, seqs, wide)
    )
    pre_back = conv_back * conv_sig * (1.0 + pre_conv * (1.0 - conv_sig))
    taps_bias_back = jnp.sum(pre_back, axis=(0, 1))
    tap_rows = []
    extended_back = jnp.zeros((count + CONV - 1, seqs, wide), f32)
    for tap in range(CONV):
        masked_back = pre_back * valid_rows[tap]
        tap_rows.append(jnp.sum(masked_back * extended[tap : tap + count], axis=(0, 1)))
        extended_back = extended_back + jnp.pad(
            taps_f[tap] * masked_back, ((tap, CONV - 1 - tap), (0, 0), (0, 0))
        )
    rim_back = shifted(extended_back[: CONV - 1].astype(bf16), "ctx", -1).astype(f32)
    conv_in_back = extended_back[CONV - 1 :] + jnp.pad(
        rim_back, ((count - (CONV - 1), 0), (0, 0), (0, 0))
    )
    conv_in_back = swapped(conv_in_back.astype(bf16)).reshape(seqs * count, wide)
    gate_in_back = swapped(gate_in_back.astype(bf16)).reshape(seqs * count, wide)

    attn_normed_back = matmul_t(query_back, query_w) + matmul_t(kv_own, keyval_w)
    meta_first = ctx_index * meta_own
    meta_normed_back = lax.dynamic_update_slice_in_dim(
        jnp.zeros((META, width), f32), matmul_t(meta_kv_own, keyval_w), meta_first, 0
    )
    qkv_back, meta_kv_back, attn_cols = direct_many(
        [
            jnp.concatenate([columns(query_back, seqs), columns(kv_own, seqs)], 2),
            columns(meta_kv_own, seqs),
            columns(attn_b, seqs),
        ],
        ["swap"] * 3,
        "fsdp",
        12,
    )
    qkv_back = qkv_back.reshape(seqs * count, -1)
    meta_kv_back = jnp.sum(meta_kv_back.astype(f32), axis=0).astype(bf16)
    attn_cols = attn_cols.reshape(seqs * count, -1)
    attn_out_back = tmatmul(attn_cols, attn_proj_back)
    meta_mine = lax.dynamic_slice_in_dim(meta_normed, meta_first, meta_own, 0)
    q_cols = w_query.shape[1] // seqs
    in_cols = 2 * inner + qkv_back.shape[1]
    in_wide = -(-in_cols // LANES) * LANES
    in_back = padded(
        jnp.concatenate([conv_in_back[:, :inner], gate_in_back[:, :inner], qkv_back], 1),
        1,
        in_wide,
    )
    in_w_back = tmatmul(normed, in_back) + jnp.pad(
        tmatmul(meta_mine, meta_kv_back), ((0, 0), (2 * inner + q_cols, in_wide - in_cols))
    )
    in_w_back = in_w_back.astype(bf16)
    part = matmul_t(conv_in_back, conv_w) + matmul_t(gate_in_back, gate_w)
    tokens_scale = lax.rsqrt(jnp.mean(tokens_all * tokens_all, axis=-1, keepdims=True) + EPS)
    meta_all_scale = lax.rsqrt(jnp.mean(meta_all * meta_all, axis=-1, keepdims=True) + EPS)
    gain_back = (
        jnp.sum(part * tokens_all * tokens_scale, axis=0)
        + jnp.sum(attn_normed_back * hidden_in * scale_one, axis=0)
        + jnp.sum(meta_normed_back * meta_all * meta_all_scale, axis=0)
    )
    gains_back = jnp.stack([gain_back, attn_gain_back, ssm_gain_back, ffn_gain_back])
    gains_back = gains_back.astype(bf16).reshape(4, seqs, share).swapaxes(0, 1)
    tail = jnp.concatenate(
        [
            meta_normed_back.astype(bf16).reshape(seqs, meta_rows, width),
            padded(gains_back.reshape(seqs, 1, 4 * share), 2, width),
        ],
        1,
    )
    thin = jnp.concatenate(
        [
            tap_rows[0][None],
            tap_rows[1][None],
            tap_rows[2][None],
            tap_rows[3][None],
            taps_bias_back[None],
            step_shift_back[None],
            skip_back[None],
            rates_log_back,
            step_w_back,
        ],
        0,
    )[:, :inner]
    late = tuple(
        part.astype(bf16) for part in (attn_out_back, select_w_back, mixer_out_back, thin)
    )
    late = after(late, *ffn_sums)
    tail = relayed(after(tail, *late), conv_in_back, 3)
    late = lax.psum(late, "ctx")
    attn_out_back, select_w_back, mixer_out_back, thin = [part.astype(f32) for part in late]
    totals = pair_scatter(
        jnp.concatenate(
            [
                part.astype(bf16).reshape(seqs, count, width),
                output.reshape(seqs, count, width),
                padded(tail, 1, extra_rows),
            ],
            1,
        ),
        11,
    )
    input_norm_back, _ = norm_back(
        hidden_in, scale_one, gain_f, totals[:count] + attn_normed_back
    )
    in_w_back = finish(after(in_w_back, totals).reshape(seqs, share, in_wide), 13)
    block_out = (middle + totals[count : 2 * count]).astype(bf16)[None]
    first = 2 * count
    meta_back, _ = norm_back(meta_f, meta_scale, gain_f, totals[first : first + meta_rows])
    gains_back = totals[first + meta_rows, : 4 * share]
    grad_tokens = (middle_back + input_norm_back)[None]

    small = jnp.concatenate([meta_back, padded(gains_back, 0, width)[None]], 0)
    small = padded(small.astype(bf16), 0, extra_rows)
    (small,) = direct_many([small], ["gather"], "ctx", 14)
    small = jnp.sum(small.astype(f32), axis=0)
    meta_back = small[:meta_rows]
    gains = small[meta_rows, : 4 * share].reshape(4, share)

    def joined_columns(pieces):
        return swapped(pieces).reshape(share, -1).astype(f32)

    def owner(part):
        return joined_columns(exchanged(part.reshape(seqs, share, -1))[:, :, :ff_cols])

    grad_gate_up = jnp.concatenate([owner(ffn_sums[1]), owner(ffn_sums[2])], 1)
    grad_mixer_in = jnp.concatenate(
        [
            joined_columns(in_w_back[:, :, :inner]),
            joined_columns(in_w_back[:, :, inner : 2 * inner]),
        ],
        1,
    )
    first = 2 * inner
    grad_query = joined_columns(in_w_back[:, :, first : first + q_cols])
    grad_keyval = joined_columns(in_w_back[:, :, first + q_cols : in_cols])
    return (
        block_out,
        grad_tokens,
        meta_back,
        gains[0],
        grad_query,
        grad_keyval,
        attn_out_back,
        grad_mixer_in,
        thin[:CONV],
        thin[CONV],
        select_w_back,
        thin[CONV + 3 + STATE :],
        thin[CONV + 1],
        thin[CONV + 3 : CONV + 3 + STATE],
        thin[CONV + 2],
        mixer_out_back,
        gains[1],
        gains[2],
        gains[3],
        grad_gate_up,
        ffn_sums[0].astype(f32),
    )


def solution(mesh):
    rows, cols, one = P("fsdp", None), P(None, "fsdp"), P("fsdp")
    split = P("fsdp", "ctx", None)
    in_specs = (
        split,
        split,
        rows,
        rows,
        one,
        rows,
        rows,
        rows,
        rows,
        cols,
        one,
        rows,
        cols,
        one,
        cols,
        one,
        rows,
        one,
        one,
        one,
        rows,
        rows,
    )
    out_specs = (
        split,
        split,
        rows,
        one,
        rows,
        rows,
        rows,
        rows,
        cols,
        one,
        rows,
        cols,
        one,
        cols,
        one,
        rows,
        one,
        one,
        one,
        rows,
        rows,
    )
    return jax.shard_map(shards, mesh=mesh, in_specs=in_specs, out_specs=out_specs, check_vma=False)
```

```python
import jax
import jax.numpy as jnp
from jax import lax
from jax.experimental import pallas as pl
from jax.experimental.layout import Layout, with_layout_constraint
from jax.experimental.pallas import tpu as pltpu
from jax.sharding import PartitionSpec as P

HEADS = 25
KV_HEADS = 5
HEAD = 64
META = 128
STATE = 16
CONV = 4
DT_RANK = 100

EPS = 1e-05
NEG = -1e30
CUT = 1e30
LANES = 128
ROWS = 8
f32 = jnp.float32
bf16 = jnp.bfloat16


def matmul(left, right):
    return jnp.dot(left, right, preferred_element_type=f32)


def tmatmul(left, right):
    return lax.dot_general(left, right, (((0,), (0,)), ((), ())), preferred_element_type=f32)


def matmul_t(left, right):
    return lax.dot_general(left, right, (((1,), (1,)), ((), ())), preferred_element_type=f32)


def norm_rows(value, gain):
    scale = lax.rsqrt(jnp.mean(value * value, axis=-1, keepdims=True) + EPS)
    return (value * scale * gain, scale)


def norm_back(value, scale, gain, upstream):
    tilted = upstream * gain
    mixing = jnp.mean(tilted * value, axis=-1, keepdims=True)
    return (
        scale * tilted - value * scale * scale * scale * mixing,
        jnp.sum(upstream * value * scale, axis=0),
    )


def doc_number(positions, bounds):
    return jnp.sum((positions[:, None] >= bounds[None, :]).astype(jnp.int32), axis=1)


def padded(array, axis, size):
    widths = [(0, 0)] * array.ndim
    widths[axis] = (0, size - array.shape[axis])
    return jnp.pad(array, widths)


def shifted(block, axis, distance):
    devices = range(lax.axis_size(axis))
    route = [(i - distance, i) for i in devices if i - distance in devices]
    return lax.ppermute(block, axis, route)


def gathered(array, axis):
    return lax.all_gather(array, axis, axis=0)


def exchanged(array):
    return lax.all_to_all(array, "fsdp", 0, 0)


def scattered(array):
    return lax.psum_scatter(array.astype(bf16), "fsdp", scatter_dimension=0, tiled=False).astype(
        f32
    )


AT = pl.DeviceIdType.MESH
ANY = pl.BlockSpec(memory_space=pl.ANY)
INSIDE = pl.BlockSpec(memory_space=pltpu.VMEM)

def greet(axis, peers):
    barrier = pltpu.get_barrier_semaphore()
    for peer in peers:
        pl.semaphore_signal(barrier, inc=1, device_id={axis: peer}, device_id_type=AT)
    pl.semaphore_wait(barrier, len(peers))

def sender(axis, src, dst, send, recv, peer):
    return pltpu.make_async_remote_copy(src_ref=src, dst_ref=dst, send_sem=send, recv_sem=recv, device_id={axis: peer}, device_id_type=AT)

def comm_call(body, name, number, ins, shape, out_spec, scratch, time=25):
    return pl.pallas_call(body, name=name, out_shape=shape, in_specs=[spec for spec, _ in ins], out_specs=out_spec, scratch_shapes=scratch,
        cost_estimate=lasting(time), compiler_params=pltpu.CompilerParams(collective_id=number, has_side_effects=True, vmem_limit_bytes=40*2**20))(*[array for _, array in ins])

def pair_gather(array, number, swaps=()):
    devices = lax.axis_size("fsdp")
    pairs = devices // 2
    many = len(swaps)

    def body(*refs):
        mine, moved = refs[0], refs[1 : many + 1]
        out, landed = refs[many + 1], refs[many + 2 : 2 * many + 2]
        own, sent, got, passed, taken, moved_sent, moved_got = refs[2 * many + 2 :]
        me = lax.axis_index("fsdp")
        pair, core = me // 2, lax.rem(me, 2)
        mate = me + 1 - 2 * core
        peers = [2 * lax.rem(pair + k, pairs) + core for k in range(1, pairs)]
        others = [lax.rem(me + k, devices) for k in range(1, devices)]
        greet("fsdp", others if many else [mate, *peers])
        first = [
            sender("fsdp", mine, out.at[me], sent.at[k], got.at[k], peer)
            for k, peer in enumerate([mate, *peers])
        ]
        for copy in first[1:]:
            copy.start()
        first[0].start()
        extra = [
            sender(
                "fsdp",
                src.at[peer],
                dst.at[me],
                moved_sent.at[m, k],
                moved_got.at[m, k],
                peer,
            )
            for m, (src, dst) in enumerate(zip(moved, landed))
            for k, peer in enumerate(others)
        ]
        for copy in extra:
            copy.start()
        local = [pltpu.make_async_copy(mine, out.at[me], own.at[0])]
        for m, (src, dst) in enumerate(zip(moved, landed)):
            local.append(pltpu.make_async_copy(src.at[me], dst.at[me], own.at[m + 1]))
        for copy in local:
            copy.start()
        second = []
        for k in range(1, pairs):
            slot = 2 * lax.rem(pair + pairs - k, pairs) + core
            first[k].wait_recv()
            copy = sender(
                "fsdp", out.at[slot], out.at[slot], passed.at[k - 1], taken.at[k - 1], mate
            )
            copy.start()
            second.append(copy)
        first[0].wait_recv()
        for copy in first:
            copy.wait_send()
        for copy in second + extra + local:
            copy.wait()

    dma = pltpu.SemaphoreType.DMA
    shapes = [jax.ShapeDtypeStruct((devices,) + array.shape, array.dtype)]
    shapes += [jax.ShapeDtypeStruct(swap.shape, swap.dtype) for swap in swaps]
    result = comm_call(
        body,
        "pair_gather",
        number,
        [(ANY, array)] + [(ANY, swap) for swap in swaps],
        shapes,
        [ANY] * (many + 1),
        [dma((many + 1,)), dma((pairs,)), dma((pairs,)), dma((pairs - 1,)), dma((pairs - 1,))]
        + [dma((max(many, 1), devices - 1))] * 2,
    )
    return result if many else result[0]


def direct_many(arrays, modes, axis, number):
    devices = lax.axis_size(axis)
    many = len(arrays)

    def body(*refs):
        mine, out, (own, sent, got) = refs[:many], refs[many : 2 * many], refs[2 * many :]
        me = lax.axis_index(axis)
        peers = [lax.rem(me + k, devices) for k in range(1, devices)]
        greet(axis, peers)
        copies = []
        for m, (src, dst, mode) in enumerate(zip(mine, out, modes)):
            for k, peer in enumerate(peers):
                part = src if mode == "gather" else src.at[peer]
                copies.append(sender(axis, part, dst.at[me], sent.at[m, k], got.at[m, k], peer))
        for copy in copies:
            copy.start()
        for m, (src, dst, mode) in enumerate(zip(mine, out, modes)):
            part = src if mode == "gather" else src.at[me]
            copies.append(pltpu.make_async_copy(part, dst.at[me], own.at[m]))
            copies[-1].start()
        for copy in copies:
            copy.wait()

    dma = pltpu.SemaphoreType.DMA
    shapes = [
        jax.ShapeDtypeStruct(
            (devices,) + array.shape if mode == "gather" else array.shape, array.dtype
        )
        for array, mode in zip(arrays, modes)
    ]
    return comm_call(
        body,
        "direct_many",
        number,
        [(ANY, array) for array in arrays],
        shapes,
        [ANY] * many,
        [dma((many,)), dma((many, devices - 1)), dma((many, devices - 1))],
    )


def split_columns(weight, cols, wide, seqs):
    rows = weight.shape[0]
    kinds = weight.shape[1] // (cols * seqs)

    def body(mine, out):
        for m in range(kinds):
            for f in range(seqs):
                first = (m * seqs + f) * cols
                out[f, :, m * wide : m * wide + cols] = mine[:, first : first + cols]
                if wide > cols:
                    blank = jnp.zeros((rows, wide - cols), bf16)
                    out[f, :, m * wide + cols : (m + 1) * wide] = blank

    return pl.pallas_call(
        body,
        name="split_columns",
        out_shape=jax.ShapeDtypeStruct((seqs, rows, kinds * wide), bf16),
        in_specs=[INSIDE],
        out_specs=INSIDE,
        compiler_params=pltpu.CompilerParams(vmem_limit_bytes=40 * 2**20),
    )(weight)


def join_columns(array, kinds):
    seqs, rows, _ = array.shape

    def body(mine, *outs):
        for out, parts in zip(outs, kinds):
            for m, (first, cols) in enumerate(parts):
                for f in range(seqs):
                    place = (m * seqs + f) * cols
                    out[:, place : place + cols] = mine[f, :, first : first + cols].astype(f32)

    return pl.pallas_call(
        body,
        name="join_columns",
        out_shape=[
            jax.ShapeDtypeStruct((rows, seqs * sum(cols for _, cols in parts)), f32)
            for parts in kinds
        ],
        in_specs=[INSIDE],
        out_specs=[INSIDE] * len(kinds),
        compiler_params=pltpu.CompilerParams(vmem_limit_bytes=48 * 2**20),
    )(array)


def pair_scatter(array, number):
    devices = array.shape[0]; pairs = devices // 2; shape = array.shape[1:]
    def body(mine, out, near, summed, far, sent, got, passed, taken):
        me = lax.axis_index("fsdp"); pair = me // 2; core = lax.rem(me, 2); mate = me + 1 - 2 * core
        places = [lax.rem(pair + k, pairs) for k in range(1, pairs + 1)]
        greet("fsdp", [mate, *[2 * q + core for q in places[:-1]]])
        first = [sender("fsdp", mine.at[2 * q + 1 - core], near.at[k], sent.at[k], got.at[k], mate) for k, q in enumerate(places)]
        for copy in first: copy.start()
        second = []
        for k, q in enumerate(places):
            first[k].wait_recv()
            total = mine[2 * q + core].astype(f32) + near[k].astype(f32)
            if k < pairs - 1:
                summed[k] = total.astype(bf16)
                copy = sender("fsdp", summed.at[k], far.at[k], passed.at[k], taken.at[k], 2 * q + core)
                copy.start(); second.append(copy)
            else:
                out[...] = total
        for copy in second:
            copy.wait_recv()
        total = out[...]
        for k in range(pairs - 1): total = total + far[k].astype(f32)
        out[...] = total
        for copy in first: copy.wait_send()
        for copy in second: copy.wait_send()
    return comm_call(body, "pair_scatter", number, [(INSIDE, array)], jax.ShapeDtypeStruct(shape, f32), INSIDE,
        [pltpu.VMEM((pairs,) + shape, bf16), pltpu.VMEM((pairs-1,) + shape, bf16), pltpu.VMEM((pairs-1,) + shape, bf16),
         pltpu.SemaphoreType.DMA((pairs,)), pltpu.SemaphoreType.DMA((pairs,)), pltpu.SemaphoreType.DMA((pairs-1,)), pltpu.SemaphoreType.DMA((pairs-1,))])

def direct_sum(array, number):
    devices = array.shape[0]; shape = array.shape[1:]
    def body(mine, out, near, sent, got, passed, taken):
        me = lax.axis_index("fsdp")
        peers = [lax.rem(me + k, devices) for k in range(1, devices)]
        greet("fsdp", peers)
        first = [sender("fsdp", mine.at[peer], near.at[k], sent.at[k], got.at[k], peer) for k, peer in enumerate(peers)]
        for copy in first: copy.start()
        total = mine[me].astype(f32)
        for k in range(devices - 1):
            first[k].wait_recv()
            total = total + near[k].astype(f32)
        out[me] = total.astype(bf16)
        second = [sender("fsdp", out.at[me], out.at[me], passed.at[k], taken.at[k], peer) for k, peer in enumerate(peers)]
        for copy in second: copy.start()
        for copy in second: copy.wait()
        for copy in first: copy.wait_send()
    return comm_call(body, "direct_sum", number, [(INSIDE, array)], jax.ShapeDtypeStruct(array.shape, bf16), INSIDE,
        [pltpu.VMEM((devices-1,) + shape, bf16)] + [pltpu.SemaphoreType.DMA((devices-1,))] * 4)

def finish(part, smalls, number):
    devices = lax.axis_size("fsdp")
    line = lax.axis_size("ctx")
    total = part.shape[0]
    half, sub = total // 2, total // devices

    few = len(smalls)

    def body(part, *refs):
        small, (part_out, *small_out) = refs[:few], refs[few : 2 * few + 1]
        near, mid, done, own, sent, got, back_sent, back_got, out_sent, out_got, *rest = refs[2 * few + 1 :]
        small_sent, small_got = rest
        me, place = lax.axis_index("fsdp"), lax.axis_index("ctx")
        barrier = pltpu.get_barrier_semaphore()
        peers = [lax.rem(me + k, devices) for k in range(1, devices)]
        for peer in peers:
            pl.semaphore_signal(barrier, inc=1, device_id={"fsdp": peer}, device_id_type=AT)
        mates = [lax.rem(place + k, line) for k in range(1, line)]
        for mate in mates:
            pl.semaphore_signal(barrier, inc=1, device_id={"ctx": mate}, device_id_type=AT)
        pl.semaphore_wait(barrier, devices + line - 2)
        extra = []
        for m, (src, dst) in enumerate(zip(small, small_out)):
            for k, mate in enumerate(mates):
                sems = small_sent.at[m, k], small_got.at[m, k]
                extra.append(sender("ctx", src, dst.at[place], *sems, mate))
            extra.append(pltpu.make_async_copy(src, dst.at[place], own.at[sub + m]))
        for copy in extra:
            copy.start()

        def moves(way, i):
            slot = i + way * half
            onward = place + 1 - 2 * way
            back = place - 1 + 2 * way
            begin = sender("ctx", part.at[slot], near.at[slot], sent.at[slot], got.at[slot], onward)
            relay = sender("ctx", mid.at[slot], near.at[slot], sent.at[slot], got.at[slot], onward)
            spread = sender("ctx", done.at[slot], done.at[slot], back_sent.at[slot], back_got.at[slot], back)
            return slot, begin, relay, spread

        def ends(way):
            return (0, line - 1) if way == 0 else (line - 1, 0)

        def turn(s, _):
            for way in range(2):
                first, last = ends(way)
                hops = place if way == 0 else line - 1 - place

                def inward(i):
                    slot, begin, relay, spread = moves(way, i)

                    @pl.when(place == first)
                    def _():
                        begin.start()

                    @pl.when(place != first)
                    def _():
                        relay.wait_recv()

                        @pl.when(place != last)
                        def _():
                            mid[slot] = (part[slot].astype(f32) + near[slot].astype(f32)).astype(bf16)
                            relay.start()

                        @pl.when(place == last)
                        def _():
                            done[slot] = (part[slot].astype(f32) + near[slot].astype(f32)).astype(bf16)

                def outward(i):
                    slot, begin, relay, spread = moves(way, i)

                    @pl.when(place != last)
                    def _():
                        spread.wait_recv()

                    @pl.when(place != first)
                    def _():
                        spread.start()

                    owner, rank = slot // sub, lax.rem(slot, sub)
                    here = me * sub + rank

                    @pl.when(me != owner)
                    def _():
                        sender("fsdp", done.at[slot], part_out.at[here], out_sent.at[slot], out_got.at[here], owner).start()

                    @pl.when(me == owner)
                    def _():
                        pltpu.make_async_copy(done.at[slot], part_out.at[slot], own.at[rank]).start()

                i = s - hops
                pl.when((i >= 0) & (i < half))(lambda: inward(i))
                k = s - (2 * (line - 1) - hops)
                pl.when((k >= 0) & (k < half))(lambda: outward(k))
            return 0

        lax.fori_loop(0, half + 2 * (line - 1), turn, 0)

        def drain(i, _):
            for way in range(2):
                first, last = ends(way)
                slot, begin, relay, spread = moves(way, i)

                @pl.when(place == first)
                def _():
                    begin.wait_send()

                @pl.when((place != first) & (place != last))
                def _():
                    relay.wait_send()

                @pl.when(place != first)
                def _():
                    spread.wait_send()

                owner, rank = slot // sub, lax.rem(slot, sub)
                copy = sender("fsdp", done.at[slot], part_out.at[slot], out_sent.at[slot], out_got.at[slot], owner)

                @pl.when(me != owner)
                def _():
                    copy.wait_send()
                    copy.wait_recv()

                @pl.when(me == owner)
                def _():
                    pltpu.make_async_copy(done.at[slot], part_out.at[slot], own.at[rank]).wait()
            return 0

        lax.fori_loop(0, half, drain, 0)
        for copy in extra:
            copy.wait()

    dma = pltpu.SemaphoreType.DMA
    return pl.pallas_call(
        body,
        name="finish",
        out_shape=[
            jax.ShapeDtypeStruct(part.shape, bf16),
            *[jax.ShapeDtypeStruct((line,) + small.shape, bf16) for small in smalls],
        ],
        in_specs=[INSIDE] + [ANY] * few,
        out_specs=[ANY] * (few + 1),
        scratch_shapes=[pltpu.VMEM(part.shape, bf16)] * 3
        + [dma((sub + few,))]
        + [dma((total,))] * 6
        + [dma((few, line - 1))] * 2,
        compiler_params=pltpu.CompilerParams(
            collective_id=number, has_side_effects=True, vmem_limit_bytes=50 * 2**20
        ),
        cost_estimate=pl.CostEstimate(flops=0, bytes_accessed=400 * 2**20, transcendentals=0),
    )(part, *smalls)


def columns(weight, count):
    return weight.reshape(weight.shape[0], count, -1).swapaxes(0, 1)


def by_rows(array):
    return with_layout_constraint(array, Layout((0, 1)))


def after(value, *earlier):
    zero = 0.0
    for array in earlier:
        corner = lax.slice(array, (0,) * array.ndim, (1,) * array.ndim).reshape(())
        zero = zero + jnp.minimum(jnp.abs(corner.astype(f32)), 0.0)
    return jax.tree.map(lambda part: part + zero.astype(part.dtype), value)


def relayed(value, earlier, rounds):
    corner = lax.slice(earlier, (0,) * earlier.ndim, (1,) * earlier.ndim).reshape(1, 1)
    token = jnp.broadcast_to(corner.astype(f32), (ROWS, LANES))
    devices = lax.axis_size("fsdp")
    for _ in range(rounds):
        token = lax.ppermute(token, "fsdp", [(i, i ^ 1) for i in range(devices)])
    return after(value, token)


def swapped(array):
    return array.swapaxes(0, 1)


def rates_of(rate_ref):
    return [jnp.broadcast_to(rate_ref[n : n + 1, :], (ROWS, LANES)) for n in range(STATE)]


def spread(sel_ref, picks, cuts):
    @pl.when(pl.program_id(1) == 0)
    def _():
        def turn(t, _):
            sel = sel_ref[t]
            for first, into in picks:
                for n in range(STATE):
                    lane = sel[:, first + n : first + n + 1]
                    into[t, n] = jnp.broadcast_to(lane, (ROWS, LANES))
            cuts[t] = jnp.broadcast_to(sel[:, 2 * STATE : 2 * STATE + 1], (ROWS, LANES))
            return 0

        lax.fori_loop(0, sel_ref.shape[0], turn, 0, unroll=4)


def carry_body(step_ref, conv_ref, sel_ref, rate_ref, out_ref, enters, cuts):
    rates = rates_of(rate_ref)
    spread(sel_ref, [(0, enters)], cuts)

    def turn(t, state):
        step = step_ref[t]
        push = step * conv_ref[t]
        fade = step + cuts[t]
        new = [
            jnp.exp(fade * rates[n]) * state[n] + enters[t, n] * push for n in range(STATE)
        ]
        return (*new, state[STATE] + fade)

    zero = jnp.zeros((ROWS, LANES), f32)
    state = lax.fori_loop(0, step_ref.shape[0], turn, (zero,) * (STATE + 1), unroll=8)
    for n in range(STATE + 1):
        out_ref[n] = state[n]


def scan_body(
    mine_ref,
    step_ref,
    conv_ref,
    sel_ref,
    rate_ref,
    carry_ref,
    out_ref,
    states_ref,
    enters,
    exits,
    cuts,
):
    rates = rates_of(rate_ref)
    spread(sel_ref, [(0, enters), (STATE, exits)], cuts)

    def join(j, state):
        return tuple(
            jnp.exp(rates[n] * carry_ref[j, STATE]) * state[n] + carry_ref[j, n]
            for n in range(STATE)
        )

    zero = jnp.zeros((ROWS, LANES), f32)
    state = lax.fori_loop(0, mine_ref[0], join, (zero,) * STATE)
    for n in range(STATE):
        states_ref[0, n] = state[n]

    def turn(t, state):
        step = step_ref[t]
        push = step * conv_ref[t]
        fade = step + cuts[t]
        new, total = [], zero
        for n in range(STATE):
            now = jnp.exp(fade * rates[n]) * state[n] + enters[t, n] * push
            states_ref[t + 1, n] = now
            total = total + exits[t, n] * now
            new.append(now)
        out_ref[t] = total
        return tuple(new)

    lax.fori_loop(0, step_ref.shape[0], turn, state, unroll=8)


def carry_back_body(step_ref, sel_ref, rate_ref, up_ref, out_ref, exits, cuts):
    rates = rates_of(rate_ref)
    spread(sel_ref, [(STATE, exits)], cuts)
    count = step_ref.shape[0]

    def turn(i, state):
        t = count - 1 - i
        up = up_ref[t]
        fade = step_ref[t] + cuts[t]
        return tuple(
            jnp.exp(fade * rates[n]) * (exits[t, n] * up + state[n]) for n in range(STATE)
        )

    zero = jnp.zeros((ROWS, LANES), f32)
    state = lax.fori_loop(0, count, turn, (zero,) * STATE, unroll=8)
    for n in range(STATE):
        out_ref[n] = state[n]


def scan_back_body(
    mine_ref,
    step_ref,
    conv_ref,
    sel_ref,
    rate_ref,
    up_ref,
    states_ref,
    span_ref,
    leave_ref,
    step_out,
    conv_out,
    sel_out,
    rate_out,
    enter_terms,
    exit_terms,
    enters,
    exits,
    cuts,
):
    rates = rates_of(rate_ref)
    spread(sel_ref, [(0, enters), (STATE, exits)], cuts)
    count = step_ref.shape[0]
    devices = span_ref.shape[0]
    zero = jnp.zeros((ROWS, LANES), f32)

    def join(i, state):
        j = devices - 1 - i
        return tuple(
            jnp.exp(rates[n] * span_ref[j]) * state[n] + leave_ref[j, n] for n in range(STATE)
        )

    state = lax.fori_loop(0, devices - 1 - mine_ref[0], join, (zero,) * STATE)
    state = state + (zero,) * STATE
    place = lax.broadcasted_iota(jnp.int32, (2 * LANES, LANES), 1)
    half = lax.broadcasted_iota(jnp.int32, (2 * LANES, LANES), 0) // LANES
    span = count // 2

    @pl.when(pl.program_id(1) == 0)
    def _():
        sel_out[...] = jnp.zeros_like(sel_out)

    for start in (span, 0):

        def turn(i, carried):
            t = start + span - 1 - i
            step, conv, up = step_ref[t], conv_ref[t], up_ref[t]
            push = step * conv
            fade = step + cuts[t]
            rows = pl.ds(pl.multiple_of((t - start) * ROWS, ROWS), ROWS)
            push_back, fade_back, new, rate_back = zero, zero, [], []
            for n in range(STATE):
                lanes = slice(n * LANES, (n + 1) * LANES)
                total = exits[t, n] * up + carried[n]
                exit_terms[rows, lanes] = up * states_ref[t + 1, n]
                enter_terms[rows, lanes] = total * push
                push_back = push_back + total * enters[t, n]
                earlier = jnp.exp(fade * rates[n]) * total
                slope = earlier * states_ref[t, n]
                fade_back = fade_back + slope * rates[n]
                new.append(earlier)
                rate_back.append(carried[STATE + n] + slope * step)
            step_out[t] = push_back * conv + fade_back
            conv_out[t] = push_back * step
            return (*new, *rate_back)

        state = lax.fori_loop(0, span, turn, state, unroll=4)
        total = jnp.zeros((span * ROWS, LANES), f32)
        for n in range(0, STATE, 2):
            lanes = slice(n * LANES, (n + 2) * LANES)
            pick = (place == n + half).astype(bf16)
            total = total + matmul(enter_terms[:, lanes].astype(bf16), pick)
            pick = (place == STATE + n + half).astype(bf16)
            total = total + matmul(exit_terms[:, lanes].astype(bf16), pick)
        sel_out[start : start + span] += total.reshape(span, ROWS, LANES)
    for n in range(STATE):
        rate_out[0, n : n + 1] = jnp.sum(state[STATE + n], axis=0, keepdims=True)


def lasting(time):
    return pl.CostEstimate(flops=0, bytes_accessed=int(time * 3.6e6), transcendentals=0)


def scan_specs(count, seqs, wide, devices):
    specs = dict(
        mine=pl.BlockSpec(memory_space=pltpu.SMEM),
        row=pl.BlockSpec((count, ROWS, LANES), lambda s, c: (0, s, c)),
        sel=pl.BlockSpec((count, ROWS, LANES), lambda s, c: (0, s, 0)),
        rate=pl.BlockSpec((STATE, LANES), lambda s, c: (0, c)),
        carry=pl.BlockSpec((STATE + 1, ROWS, LANES), lambda s, c: (0, s, c)),
        carries=pl.BlockSpec((devices, STATE + 1, ROWS, LANES), lambda s, c: (0, 0, s, c)),
        leave=pl.BlockSpec((STATE, ROWS, LANES), lambda s, c: (0, s, c)),
        leaves=pl.BlockSpec((devices, STATE, ROWS, LANES), lambda s, c: (0, 0, s, c)),
        span=pl.BlockSpec((devices, ROWS, LANES), lambda s, c: (0, s, c)),
        states=pl.BlockSpec((count + 1, STATE, ROWS, LANES), lambda s, c: (0, 0, s, c)),
        rates=pl.BlockSpec((1, STATE, LANES), lambda s, c: (s, 0, c)),
    )
    spreads = pltpu.VMEM((count, STATE, ROWS, LANES), f32)
    cuts = pltpu.VMEM((count, ROWS, LANES), f32)
    terms = pltpu.VMEM((count // 2 * ROWS, STATE * LANES), f32)
    specs["one"], specs["two"] = [spreads, cuts], [spreads, spreads, cuts]
    specs["four"] = [terms, terms, spreads, spreads, cuts]
    return specs, (seqs // ROWS, wide // LANES)


def scan_call(body, name, grid, ins, outs, shapes, scratch, work, args):
    return pl.pallas_call(
        body,
        name=name,
        grid=grid,
        in_specs=ins,
        out_specs=outs,
        out_shape=[jax.ShapeDtypeStruct(shape, f32) for shape in shapes],
        scratch_shapes=scratch,
        compiler_params=pltpu.CompilerParams(
            dimension_semantics=("arbitrary", "arbitrary"), vmem_limit_bytes=60 * 2**20
        ),
        cost_estimate=lasting(work),
    )(*args)


def shards(
    tokens,
    cotangent,
    doc_lengths,
    meta_tokens,
    norm_gain,
    w_query,
    w_keyval,
    w_attn_out,
    w_mixer_in,
    conv_taps,
    conv_bias,
    w_select,
    w_step,
    step_bias,
    log_rates,
    skip_gain,
    w_mixer_out,
    attn_gain,
    ssm_gain,
    ffn_norm_gain,
    w_gate_up,
    w_down,
):
    count = tokens.shape[1]
    width = tokens.shape[2]
    seqs = lax.axis_size("fsdp")
    ctx_index = lax.axis_index("ctx")
    ctx_count = lax.axis_size("ctx")
    inner = conv_bias.shape[0]
    wide = -(-inner // LANES) * LANES
    kv_width = KV_HEADS * HEAD
    groups = HEADS // KV_HEADS
    mine = jnp.reshape(ctx_index, (1,)).astype(jnp.int32)

    positions = ctx_index * count + jnp.arange(count, dtype=jnp.int32)
    last_pos = ctx_index * count + count - 1
    bounds = jnp.cumsum(doc_lengths[0])[:-1]
    docs = doc_number(positions, bounds)

    hidden_in = tokens[0].astype(f32)
    meta_rows = meta_tokens.shape[0]
    share = norm_gain.shape[0]
    extra_rows = -(-(meta_rows + 1) // 16) * 16
    few = doc_lengths[0]
    thin = jnp.concatenate(
        [
            norm_gain,
            attn_gain,
            ssm_gain,
            ffn_norm_gain,
            (few // 32).astype(bf16),
            (few % 32).astype(bf16),
        ]
    )
    extra = padded(
        jnp.concatenate([meta_tokens, padded(thin, 0, width)[None]], 0), 0, extra_rows
    )
    ff_cols = w_gate_up.shape[1] // (2 * seqs)
    conv_w = split_columns(w_mixer_in[:, : inner * seqs], inner, wide, seqs)
    gate_w = split_columns(w_mixer_in[:, inner * seqs :], inner, wide, seqs)
    everyone, conv_w = pair_gather(jnp.concatenate([tokens[0], extra], 0), 1, [conv_w])
    conv_w = conv_w.reshape(width, wide)
    tokens_all = everyone[:, :count].astype(f32).reshape(seqs * count, width)
    meta_f = meta_tokens.astype(f32)
    meta_all = everyone[:, count : count + meta_rows].astype(f32).reshape(META, width)
    thin = everyone[:, count + meta_rows]
    gains = thin[:, : 4 * share].reshape(seqs, 4, share).swapaxes(0, 1).astype(f32)
    gains = gains.reshape(4, width)
    gain_f, attn_norm_f, ssm_norm_f, ffn_gain_f = gains[0], gains[1], gains[2], gains[3]
    lengths = thin[:, 4 * share :].astype(jnp.int32)
    doc_count = doc_lengths.shape[1]
    lengths = 32 * lengths[:, :doc_count] + lengths[:, doc_count : 2 * doc_count]

    normed_all_f, _ = norm_rows(tokens_all, gain_f)
    normed = normed_all_f.astype(bf16)
    normed_own_f, scale_one = norm_rows(hidden_in, gain_f)
    normed_own = normed_own_f.astype(bf16)
    _, meta_scale = norm_rows(meta_f, gain_f)
    meta_normed = norm_rows(meta_all, gain_f)[0].astype(bf16)

    w_keyval, w_query = after((w_keyval, w_query), everyone)
    gate_w = exchanged(after(gate_w, everyone)).reshape(width, wide)
    keyval_w = lax.all_gather(w_keyval, "fsdp", axis=0, tiled=True)
    query_w = lax.all_gather(w_query, "fsdp", axis=0, tiled=True)
    ff_wide = -(-ff_cols // LANES) * LANES
    ff_w = exchanged(split_columns(w_gate_up, ff_cols, ff_wide, seqs))
    ff_w = ff_w.reshape(width, 2 * ff_wide)

    conv_in = swapped(matmul(normed, conv_w).astype(bf16).reshape(seqs, count, wide))
    gate_in = swapped(matmul(normed, gate_w).astype(bf16).reshape(seqs, count, wide))
    seq_bounds = jnp.cumsum(lengths, axis=1)[:, :-1]

    def numbers(places):
        return jnp.sum((places[:, None, None] >= seq_bounds[None]).astype(jnp.int32), axis=-1)

    seq_docs = numbers(positions)
    starts = (positions[:, None] == 0) | (seq_docs != numbers(positions - 1))
    taps_f = padded(conv_taps.astype(f32), 1, wide)
    rim = shifted(conv_in[count - (CONV - 1) :], "ctx", 1)
    extended = jnp.concatenate([rim, conv_in], 0).astype(f32)
    valid_rows = []
    for tap in range(CONV):
        earlier = positions - (CONV - 1 - tap)
        valid = (earlier[:, None] >= 0) & (numbers(earlier) == seq_docs)
        valid_rows.append(valid.astype(f32)[:, :, None])
    pre_conv = padded(conv_bias.astype(f32), 0, wide)[None, None, :]
    for tap in range(CONV):
        pre_conv = pre_conv + taps_f[tap] * extended[tap : tap + count] * valid_rows[tap]
    conv_sig = jax.nn.sigmoid(pre_conv)
    conv_out = (pre_conv * conv_sig).astype(bf16)
    conv_f = conv_out.astype(f32)
    conv_rows = conv_out.reshape(count * seqs, wide)
    select_w = padded(w_select, 0, wide)
    step_w = padded(w_step, 1, wide)
    selected = direct_sum(
        matmul(conv_rows, select_w).astype(bf16).reshape(seqs, count, -1), 3
    ).reshape(count * seqs, -1)
    step_low = selected[:, :DT_RANK]
    step_pre = matmul(step_low, step_w) + padded(step_bias.astype(f32), 0, wide)[None, :]
    step_pre = step_pre.reshape(count, seqs, wide)
    steps = jax.nn.softplus(step_pre)
    rates = -jnp.exp(padded(log_rates.astype(f32), 1, wide))
    sel = jnp.concatenate(
        [
            selected[:, DT_RANK:].astype(f32).reshape(count, seqs, 2 * STATE),
            jnp.where(starts, CUT, 0.0).astype(f32)[:, :, None],
        ],
        2,
    )
    sel = padded(sel, 2, LANES)
    spec, grid = scan_specs(count, seqs, wide, ctx_count)
    row_shape = (count, seqs, wide)
    (carry,) = scan_call(
        carry_body,
        "mamba_carry",
        grid,
        [spec["row"], spec["row"], spec["sel"], spec["rate"]],
        [spec["carry"]],
        [(STATE + 1, seqs, wide)],
        spec["one"],
        15,
        (steps, conv_f, sel, rates),
    )
    keyvals = matmul(normed_own, keyval_w).astype(bf16)
    carries, keyvals_all = direct_many(
        [carry.astype(bf16), keyvals], ["gather", "gather"], "ctx", 4
    )
    carries = carries.astype(f32)
    attn_out_w = lax.all_gather(w_attn_out, "fsdp", axis=0, tiled=True)
    out_back_all = gathered(cotangent[0], "fsdp").reshape(seqs * count, width)
    scanned, states = scan_call(
        scan_body,
        "mamba_scan",
        grid,
        [spec["mine"], spec["row"], spec["row"], spec["sel"], spec["rate"], spec["carries"]],
        [spec["row"], spec["states"]],
        [row_shape, (count + 1, STATE, seqs, wide)],
        spec["two"],
        26,
        (mine, steps, conv_f, sel, rates, carries),
    )
    skip_f = padded(skip_gain.astype(f32), 0, wide)
    ssm_out = scanned + skip_f * conv_f
    gate_f = gate_in.astype(f32)
    gate_sig = jax.nn.sigmoid(gate_f)
    gate_act = gate_f * gate_sig
    mixer_mid = swapped((ssm_out * gate_act).astype(bf16)).reshape(seqs * count, wide)
    mixer_out_w = padded(w_mixer_out, 0, wide)
    mixer_proj = pair_scatter(
        by_rows(matmul(mixer_mid, mixer_out_w).astype(bf16)).reshape(seqs, count, width), 6
    )
    queries = matmul(normed_own, query_w).astype(bf16)
    meta_kv = matmul(meta_normed, keyval_w).astype(bf16)
    query_heads = queries.reshape(count, KV_HEADS, groups, HEAD)
    piece = keyvals_all.reshape(ctx_count * count, 2 * kv_width)
    joined = jnp.concatenate([meta_kv, piece], 0)
    keys = joined[:, :kv_width].reshape(-1, KV_HEADS, HEAD)
    values = joined[:, kv_width:].reshape(-1, KV_HEADS, HEAD)
    key_pos = jnp.arange(piece.shape[0], dtype=jnp.int32)
    key_doc = doc_number(key_pos, bounds)
    shown = (key_pos[None, :] <= positions[:, None]) & (key_doc[None, :] == docs[:, None])
    shown = jnp.concatenate([jnp.full((count, META), True), shown], 1)
    scores = (
        jnp.einsum("qgha,kga->ghqk", query_heads, keys, preferred_element_type=f32) * 0.125
    )
    scores = jnp.where(shown[None, None], scores, NEG)
    top = jnp.max(scores, axis=-1, keepdims=True)
    weights = jnp.exp(scores - top)
    weights = weights / jnp.sum(weights, axis=-1, keepdims=True)
    attn_heads_f = jnp.einsum(
        "ghqk,kga->qgha", weights.astype(bf16), values, preferred_element_type=f32
    )
    attn_b = attn_heads_f.reshape(count, HEADS * HEAD).astype(bf16)
    attn_proj = matmul(attn_b, attn_out_w)
    attn_branch, attn_scale = norm_rows(attn_proj, attn_norm_f)

    ssm_branch, ssm_scale = norm_rows(mixer_proj, ssm_norm_f)
    middle = hidden_in + 0.5 * (attn_branch + ssm_branch)

    normed_two_f, scale_two = norm_rows(middle, ffn_gain_f)
    normed_two = pair_gather(normed_two_f.astype(bf16), 7).reshape(seqs * count, width)
    gate_up = matmul(normed_two, ff_w).astype(bf16)
    gate_v, up_v = gate_up[:, :ff_wide].astype(f32), gate_up[:, ff_wide:].astype(f32)
    ffn_sig = jax.nn.sigmoid(gate_v)
    hidden_ff = (gate_v * ffn_sig * up_v).astype(bf16)
    down_w = padded(w_down, 0, ff_wide)
    output = by_rows(matmul(hidden_ff, down_w).astype(bf16))

    output = exchanged(output.reshape(seqs, count, width)).astype(f32)
    block_out = (middle + jnp.sum(output, axis=0)).astype(bf16)[None]
    down_back = tmatmul(hidden_ff, out_back_all)[:ff_cols]
    hidden_back = matmul_t(out_back_all, down_w).astype(bf16).astype(f32)
    up_back = hidden_back * gate_v * ffn_sig
    gate_back = hidden_back * up_v * ffn_sig * (1.0 + gate_v * (1.0 - ffn_sig))
    gate_up_back = jnp.concatenate([gate_back.astype(bf16), up_back.astype(bf16)], 1)
    ff_w_back = tmatmul(normed_two, gate_up_back)
    normed_two_back = matmul_t(gate_up_back, ff_w).astype(bf16)
    down_back = down_back.astype(bf16)
    ff_w_back = ff_w_back.astype(bf16)
    ff_w_sum = lax.psum(ff_w_back, "ctx")
    normed_two_back = by_rows(relayed(normed_two_back, ff_w_back, 2))
    normed_two_back = pair_scatter(normed_two_back.reshape(seqs, count, width), 8)
    middle_norm_back, ffn_gain_back = norm_back(middle, scale_two, ffn_gain_f, normed_two_back)
    middle_back = cotangent[0].astype(f32) + middle_norm_back
    branch_back = 0.5 * middle_back
    ssm_proj_back, ssm_gain_back = norm_back(mixer_proj, ssm_scale, ssm_norm_f, branch_back)
    attn_proj_back, attn_gain_back = norm_back(attn_proj, attn_scale, attn_norm_f, branch_back)
    attn_own_back = attn_proj_back.astype(bf16)
    proj_back, attn_cols = pair_gather(
        jnp.concatenate([ssm_proj_back.astype(bf16), attn_own_back], 0),
        9,
        [columns(attn_b, seqs)],
    )
    attn_cols = attn_cols.reshape(seqs * count, -1)
    ssm_proj_back = proj_back[:, :count].reshape(seqs * count, width)
    attn_proj_back = proj_back[:, count:].reshape(seqs * count, width)

    mixer_out_back = tmatmul(mixer_mid, ssm_proj_back)[:inner].astype(bf16)
    attn_out_back = tmatmul(attn_cols, attn_proj_back).astype(bf16)
    mid_back = matmul_t(ssm_proj_back, mixer_out_w).astype(bf16).reshape(seqs, count, wide)
    mid_back = swapped(mid_back).astype(f32)
    ssm_back = mid_back * gate_act
    gate_in_back = mid_back * ssm_out * gate_sig * (1.0 + gate_f * (1.0 - gate_sig))
    skip_back = jnp.sum(ssm_back * conv_f, axis=(0, 1))
    (leave,) = scan_call(
        carry_back_body,
        "mamba_carry_back",
        grid,
        [spec["row"], spec["sel"], spec["rate"], spec["row"]],
        [spec["leave"]],
        [(STATE, seqs, wide)],
        spec["one"],
        15,
        (steps, sel, rates, ssm_back),
    )
    heads_back = matmul_t(attn_own_back, attn_out_w).astype(bf16)
    heads_back = heads_back.reshape(count, KV_HEADS, groups, HEAD)
    delta = jnp.sum(heads_back.astype(f32) * attn_heads_f, axis=-1)
    delta = delta.transpose(1, 2, 0)[..., None]
    weights_back = jnp.einsum("qgha,kga->ghqk", heads_back, values, preferred_element_type=f32)
    scores_back = (weights * (weights_back - delta)).astype(bf16)
    query_back = (
        jnp.einsum("ghqk,kga->qgha", scores_back, keys, preferred_element_type=f32) * 0.125
    )
    keys_back = (
        jnp.einsum("ghqk,qgha->kga", scores_back, query_heads, preferred_element_type=f32) * 0.125
    )
    values_back = jnp.einsum(
        "ghqk,qgha->kga", weights.astype(bf16), heads_back, preferred_element_type=f32
    )
    kv_back = jnp.concatenate(
        [keys_back.reshape(-1, kv_width), values_back.reshape(-1, kv_width)], 1
    )
    buffer = kv_back[META:].astype(bf16).reshape(ctx_count, count, 2 * kv_width)
    meta_kv_own = kv_back[:META].astype(bf16)
    query_back = query_back.reshape(count, HEADS * HEAD).astype(bf16)
    (leaves,) = direct_many([leave.astype(bf16)], ["gather"], "ctx", 5)
    owned = lax.all_to_all(buffer, "ctx", 0, 0)
    second = after((down_back, mixer_out_back, attn_out_back), ff_w_sum, owned)
    token = relayed(jnp.zeros((ROWS, LANES), f32), after(second[0], *second[1:]), 2)
    second = lax.psum(second, "ctx")
    down_back, mixer_out_back, attn_out_back = [part.astype(f32) for part in second]
    leaves = after(leaves.astype(f32), token)
    owned = jnp.sum(owned.astype(f32), axis=0).astype(bf16)
    kv_own = owned
    steps_back, conv_back, sel_back, rates_back = scan_call(
        scan_back_body,
        "mamba_scan_back",
        grid,
        [
            spec["mine"],
            spec["row"],
            spec["row"],
            spec["sel"],
            spec["rate"],
            spec["row"],
            spec["states"],
            spec["span"],
            spec["leaves"],
        ],
        [spec["row"], spec["row"], spec["sel"], spec["rates"]],
        [row_shape, row_shape, (count, seqs, LANES), (seqs // ROWS, STATE, wide)],
        spec["four"],
        47,
        (mine, steps, conv_f, sel, rates, ssm_back, states, carries[:, STATE], leaves),
    )
    rates_log_back = jnp.sum(rates_back, axis=0) * rates
    step_pre_back = steps_back * jax.nn.sigmoid(step_pre)
    step_shift_back = jnp.sum(step_pre_back, axis=(0, 1))
    step_pre_back = step_pre_back.astype(bf16).reshape(count * seqs, wide)
    step_w_back = tmatmul(step_low, step_pre_back)
    selected_back = jnp.concatenate(
        [
            matmul_t(step_pre_back, step_w),
            sel_back[:, :, : 2 * STATE].reshape(count * seqs, 2 * STATE),
        ],
        1,
    ).astype(bf16)
    selected_back = direct_sum(selected_back.reshape(seqs, count, -1), 10)
    selected_back = selected_back.reshape(count * seqs, -1)
    select_w_back = tmatmul(selected_back, conv_rows)[:, :inner]
    conv_back = (
        conv_back
        + skip_f * ssm_back
        + matmul_t(selected_back, select_w).reshape(count, seqs, wide)
    )
    pre_back = conv_back * conv_sig * (1.0 + pre_conv * (1.0 - conv_sig))
    taps_bias_back = jnp.sum(pre_back, axis=(0, 1))
    tap_rows = []
    extended_back = jnp.zeros((count + CONV - 1, seqs, wide), f32)
    for tap in range(CONV):
        masked_back = pre_back * valid_rows[tap]
        tap_rows.append(jnp.sum(masked_back * extended[tap : tap + count], axis=(0, 1)))
        extended_back = extended_back + jnp.pad(
            taps_f[tap] * masked_back, ((tap, CONV - 1 - tap), (0, 0), (0, 0))
        )
    rim_back = shifted(extended_back[: CONV - 1].astype(bf16), "ctx", -1).astype(f32)
    conv_in_back = extended_back[CONV - 1 :] + jnp.pad(
        rim_back, ((count - (CONV - 1), 0), (0, 0), (0, 0))
    )
    conv_in_back = swapped(conv_in_back.astype(bf16)).reshape(seqs * count, wide)
    gate_in_back = swapped(gate_in_back.astype(bf16)).reshape(seqs * count, wide)

    attn_normed_back = matmul_t(query_back, query_w) + matmul_t(kv_own, keyval_w)
    meta_normed_back = matmul_t(meta_kv_own, keyval_w)
    qkv_back, meta_kv_back = direct_many(
        [
            jnp.concatenate([columns(query_back, seqs), columns(kv_own, seqs)], 2),
            columns(meta_kv_own, seqs),
        ],
        ["swap"] * 2,
        "fsdp",
        12,
    )
    qkv_back = qkv_back.reshape(seqs * count, -1)
    meta_kv_back = jnp.sum(meta_kv_back.astype(f32), axis=0).astype(bf16)
    thin = jnp.concatenate(
        [
            tap_rows[0][None],
            tap_rows[1][None],
            tap_rows[2][None],
            tap_rows[3][None],
            taps_bias_back[None],
            step_shift_back[None],
            skip_back[None],
            rates_log_back,
            step_w_back,
        ],
        0,
    )[:, :inner]
    q_cols = w_query.shape[1] // seqs
    in_cols = 2 * inner + qkv_back.shape[1]
    in_wide = -(-in_cols // LANES) * LANES
    in_back = padded(
        jnp.concatenate([conv_in_back[:, :inner], gate_in_back[:, :inner], qkv_back], 1),
        1,
        in_wide,
    )
    in_w_back = tmatmul(normed, in_back) + jnp.pad(
        tmatmul(meta_normed, meta_kv_back), ((0, 0), (2 * inner + q_cols, in_wide - in_cols))
    )
    in_w_back = in_w_back.astype(bf16)
    part = by_rows(matmul_t(conv_in_back, conv_w) + matmul_t(gate_in_back, gate_w))
    tokens_scale = lax.rsqrt(jnp.mean(tokens_all * tokens_all, axis=-1, keepdims=True) + EPS)
    meta_all_scale = lax.rsqrt(jnp.mean(meta_all * meta_all, axis=-1, keepdims=True) + EPS)
    gain_back = (
        jnp.sum(part * tokens_all * tokens_scale, axis=0)
        + jnp.sum(attn_normed_back * hidden_in * scale_one, axis=0)
        + jnp.sum(meta_normed_back * meta_all * meta_all_scale, axis=0)
    )
    gains_back = jnp.stack([gain_back, attn_gain_back, ssm_gain_back, ffn_gain_back])
    gains_back = gains_back.astype(bf16).reshape(4, seqs, share).swapaxes(0, 1)
    tail = jnp.concatenate(
        [
            meta_normed_back.astype(bf16).reshape(seqs, meta_rows, width),
            padded(gains_back.reshape(seqs, 1, 4 * share), 2, width),
        ],
        1,
    )
    totals = pair_scatter(
        jnp.concatenate(
            [
                part.astype(bf16).reshape(seqs, count, width),
                padded(tail, 1, extra_rows),
            ],
            1,
        ),
        11,
    )
    input_norm_back, _ = norm_back(
        hidden_in, scale_one, gain_f, totals[:count] + attn_normed_back
    )
    first = count
    meta_back, _ = norm_back(meta_f, meta_scale, gain_f, totals[first : first + meta_rows])
    gains_back = totals[first + meta_rows, : 4 * share]
    grad_tokens = (middle_back + input_norm_back)[None]

    small = jnp.concatenate([meta_back, padded(gains_back, 0, width)[None]], 0)
    small = padded(small.astype(bf16), 0, extra_rows)
    thin = jnp.concatenate([thin, select_w_back], 0).astype(bf16)
    thin_rows = thin.shape[0]
    thin = padded(thin, 0, -(-thin_rows // 16) * 16)
    in_w_back, small, thin = finish(in_w_back.reshape(seqs, share, in_wide), [small, thin], 13)
    thin = jnp.sum(thin.astype(f32), axis=0)
    select_first = thin_rows - select_w_back.shape[0]
    select_w_back = thin[select_first:thin_rows].T
    small = jnp.sum(small.astype(f32), axis=0)
    meta_back = small[:meta_rows]
    gains = small[meta_rows, : 4 * share].reshape(4, share)

    (grad_gate_up,) = join_columns(
        exchanged(ff_w_sum.reshape(seqs, share, 2 * ff_wide)),
        [[(0, ff_cols), (ff_wide, ff_cols)]],
    )
    first = 2 * inner
    grad_mixer_in, grad_query, grad_keyval = join_columns(
        in_w_back,
        [
            [(0, inner), (inner, inner)],
            [(first, q_cols)],
            [(first + q_cols, in_cols - first - q_cols)],
        ],
    )
    return (
        block_out,
        grad_tokens,
        meta_back,
        gains[0],
        grad_query,
        grad_keyval,
        attn_out_back,
        grad_mixer_in,
        thin[:CONV],
        thin[CONV],
        select_w_back,
        thin[CONV + 3 + STATE : CONV + 3 + STATE + DT_RANK],
        thin[CONV + 1],
        thin[CONV + 3 : CONV + 3 + STATE],
        thin[CONV + 2],
        mixer_out_back,
        gains[1],
        gains[2],
        gains[3],
        grad_gate_up,
        down_back,
    )


def solution(mesh):
    rows, cols, one = P("fsdp", None), P(None, "fsdp"), P("fsdp")
    split = P("fsdp", "ctx", None)
    in_specs = (
        split,
        split,
        rows,
        rows,
        one,
        rows,
        rows,
        rows,
        rows,
        cols,
        one,
        rows,
        cols,
        one,
        cols,
        one,
        rows,
        one,
        one,
        one,
        rows,
        rows,
    )
    out_specs = (
        split,
        split,
        rows,
        one,
        rows,
        rows,
        rows,
        rows,
        cols,
        one,
        rows,
        cols,
        one,
        cols,
        one,
        rows,
        one,
        one,
        one,
        rows,
        rows,
    )
    return jax.shard_map(shards, mesh=mesh, in_specs=in_specs, out_specs=out_specs, check_vma=False)
```

```python
import jax
import jax.numpy as jnp
from jax import lax
from jax.experimental import pallas as pl
from jax.experimental.layout import Layout, with_layout_constraint
from jax.experimental.pallas import tpu as pltpu
from jax.sharding import PartitionSpec as P

HEADS = 25
KV_HEADS = 5
HEAD = 64
META = 128
STATE = 16
CONV = 4
DT_RANK = 100

EPS = 1e-05
NEG = -1e30
CUT = 1e30
LANES = 128
ROWS = 8
f32 = jnp.float32
bf16 = jnp.bfloat16


def matmul(left, right):
    return jnp.dot(left, right, preferred_element_type=f32)


def tmatmul(left, right):
    return lax.dot_general(left, right, (((0,), (0,)), ((), ())), preferred_element_type=f32)


def matmul_t(left, right):
    return lax.dot_general(left, right, (((1,), (1,)), ((), ())), preferred_element_type=f32)


def norm_rows(value, gain):
    scale = lax.rsqrt(jnp.mean(value * value, axis=-1, keepdims=True) + EPS)
    return (value * scale * gain, scale)


def norm_back(value, scale, gain, upstream):
    tilted = upstream * gain
    mixing = jnp.mean(tilted * value, axis=-1, keepdims=True)
    return (
        scale * tilted - value * scale * scale * scale * mixing,
        jnp.sum(upstream * value * scale, axis=0),
    )


def doc_number(positions, bounds):
    return jnp.sum((positions[:, None] >= bounds[None, :]).astype(jnp.int32), axis=1)


def padded(array, axis, size):
    widths = [(0, 0)] * array.ndim
    widths[axis] = (0, size - array.shape[axis])
    return jnp.pad(array, widths)


def shifted(block, axis, distance):
    devices = range(lax.axis_size(axis))
    route = [(i - distance, i) for i in devices if i - distance in devices]
    return lax.ppermute(block, axis, route)


def gathered(array, axis):
    return lax.all_gather(array, axis, axis=0)


def exchanged(array):
    return lax.all_to_all(array, "fsdp", 0, 0)


def scattered(array):
    return lax.psum_scatter(array.astype(bf16), "fsdp", scatter_dimension=0, tiled=False).astype(
        f32
    )


AT = pl.DeviceIdType.MESH
ANY = pl.BlockSpec(memory_space=pl.ANY)
INSIDE = pl.BlockSpec(memory_space=pltpu.VMEM)

def greet(axis, peers):
    barrier = pltpu.get_barrier_semaphore()
    for peer in peers:
        pl.semaphore_signal(barrier, inc=1, device_id={axis: peer}, device_id_type=AT)
    pl.semaphore_wait(barrier, len(peers))

def sender(axis, src, dst, send, recv, peer):
    return pltpu.make_async_remote_copy(src_ref=src, dst_ref=dst, send_sem=send, recv_sem=recv, device_id={axis: peer}, device_id_type=AT)

def comm_call(body, name, number, ins, shape, out_spec, scratch, time=25):
    return pl.pallas_call(body, name=name, out_shape=shape, in_specs=[spec for spec, _ in ins], out_specs=out_spec, scratch_shapes=scratch,
        cost_estimate=lasting(time), compiler_params=pltpu.CompilerParams(collective_id=number, has_side_effects=True, vmem_limit_bytes=40*2**20))(*[array for _, array in ins])

def pair_gather(array, number, swaps=()):
    devices = lax.axis_size("fsdp")
    pairs = devices // 2
    many = len(swaps)

    def body(*refs):
        mine, moved = refs[0], refs[1 : many + 1]
        out, landed = refs[many + 1], refs[many + 2 : 2 * many + 2]
        own, sent, got, passed, taken, moved_sent, moved_got = refs[2 * many + 2 :]
        me = lax.axis_index("fsdp")
        pair, core = me // 2, lax.rem(me, 2)
        mate = me + 1 - 2 * core
        peers = [2 * lax.rem(pair + k, pairs) + core for k in range(1, pairs)]
        others = [lax.rem(me + k, devices) for k in range(1, devices)]
        greet("fsdp", others if many else [mate, *peers])
        first = [
            sender("fsdp", mine, out.at[me], sent.at[k], got.at[k], peer)
            for k, peer in enumerate([mate, *peers])
        ]
        for copy in first[1:]:
            copy.start()
        first[0].start()
        extra = [
            sender(
                "fsdp",
                src.at[peer],
                dst.at[me],
                moved_sent.at[m, k],
                moved_got.at[m, k],
                peer,
            )
            for m, (src, dst) in enumerate(zip(moved, landed))
            for k, peer in enumerate(others)
        ]
        for copy in extra:
            copy.start()
        local = [pltpu.make_async_copy(mine, out.at[me], own.at[0])]
        for m, (src, dst) in enumerate(zip(moved, landed)):
            local.append(pltpu.make_async_copy(src.at[me], dst.at[me], own.at[m + 1]))
        for copy in local:
            copy.start()
        second = []
        for k in range(1, pairs):
            slot = 2 * lax.rem(pair + pairs - k, pairs) + core
            first[k].wait_recv()
            copy = sender(
                "fsdp", out.at[slot], out.at[slot], passed.at[k - 1], taken.at[k - 1], mate
            )
            copy.start()
            second.append(copy)
        first[0].wait_recv()
        for copy in first:
            copy.wait_send()
        for copy in second + extra + local:
            copy.wait()

    dma = pltpu.SemaphoreType.DMA
    shapes = [jax.ShapeDtypeStruct((devices,) + array.shape, array.dtype)]
    shapes += [jax.ShapeDtypeStruct(swap.shape, swap.dtype) for swap in swaps]
    result = comm_call(
        body,
        "pair_gather",
        number,
        [(ANY, array)] + [(ANY, swap) for swap in swaps],
        shapes,
        [ANY] * (many + 1),
        [dma((many + 1,)), dma((pairs,)), dma((pairs,)), dma((pairs - 1,)), dma((pairs - 1,))]
        + [dma((max(many, 1), devices - 1))] * 2,
    )
    return result if many else result[0]


def direct_many(arrays, modes, axis, number):
    devices = lax.axis_size(axis)
    many = len(arrays)

    def body(*refs):
        mine, out, (own, sent, got) = refs[:many], refs[many : 2 * many], refs[2 * many :]
        me = lax.axis_index(axis)
        peers = [lax.rem(me + k, devices) for k in range(1, devices)]
        greet(axis, peers)
        copies = []
        for m, (src, dst, mode) in enumerate(zip(mine, out, modes)):
            for k, peer in enumerate(peers):
                part = src if mode == "gather" else src.at[peer]
                copies.append(sender(axis, part, dst.at[me], sent.at[m, k], got.at[m, k], peer))
        for copy in copies:
            copy.start()
        for m, (src, dst, mode) in enumerate(zip(mine, out, modes)):
            part = src if mode == "gather" else src.at[me]
            copies.append(pltpu.make_async_copy(part, dst.at[me], own.at[m]))
            copies[-1].start()
        for copy in copies:
            copy.wait()

    dma = pltpu.SemaphoreType.DMA
    shapes = [
        jax.ShapeDtypeStruct(
            (devices,) + array.shape if mode == "gather" else array.shape, array.dtype
        )
        for array, mode in zip(arrays, modes)
    ]
    return comm_call(
        body,
        "direct_many",
        number,
        [(ANY, array) for array in arrays],
        shapes,
        [ANY] * many,
        [dma((many,)), dma((many, devices - 1)), dma((many, devices - 1))],
    )


def split_columns(weight, cols, wide, seqs):
    rows = weight.shape[0]
    kinds = weight.shape[1] // (cols * seqs)

    def body(mine, out):
        for m in range(kinds):
            for f in range(seqs):
                first = (m * seqs + f) * cols
                out[f, :, m * wide : m * wide + cols] = mine[:, first : first + cols]
                if wide > cols:
                    blank = jnp.zeros((rows, wide - cols), bf16)
                    out[f, :, m * wide + cols : (m + 1) * wide] = blank

    return pl.pallas_call(
        body,
        name="split_columns",
        out_shape=jax.ShapeDtypeStruct((seqs, rows, kinds * wide), bf16),
        in_specs=[INSIDE],
        out_specs=INSIDE,
        compiler_params=pltpu.CompilerParams(vmem_limit_bytes=40 * 2**20),
    )(weight)


def join_columns(array, kinds):
    seqs, rows, _ = array.shape

    def body(mine, *outs):
        for out, parts in zip(outs, kinds):
            for m, (first, cols) in enumerate(parts):
                for f in range(seqs):
                    place = (m * seqs + f) * cols
                    out[:, place : place + cols] = mine[f, :, first : first + cols].astype(f32)

    return pl.pallas_call(
        body,
        name="join_columns",
        out_shape=[
            jax.ShapeDtypeStruct((rows, seqs * sum(cols for _, cols in parts)), f32)
            for parts in kinds
        ],
        in_specs=[INSIDE],
        out_specs=[INSIDE] * len(kinds),
        compiler_params=pltpu.CompilerParams(vmem_limit_bytes=48 * 2**20),
    )(array)


def pair_scatter(array, number):
    devices = array.shape[0]; pairs = devices // 2; shape = array.shape[1:]
    def body(mine, out, near, summed, far, sent, got, passed, taken):
        me = lax.axis_index("fsdp"); pair = me // 2; core = lax.rem(me, 2); mate = me + 1 - 2 * core
        places = [lax.rem(pair + k, pairs) for k in range(1, pairs + 1)]
        greet("fsdp", [mate, *[2 * q + core for q in places[:-1]]])
        first = [sender("fsdp", mine.at[2 * q + 1 - core], near.at[k], sent.at[k], got.at[k], mate) for k, q in enumerate(places)]
        for copy in first: copy.start()
        second = []
        for k, q in enumerate(places):
            first[k].wait_recv()
            total = mine[2 * q + core].astype(f32) + near[k].astype(f32)
            if k < pairs - 1:
                summed[k] = total.astype(bf16)
                copy = sender("fsdp", summed.at[k], far.at[k], passed.at[k], taken.at[k], 2 * q + core)
                copy.start(); second.append(copy)
            else:
                out[...] = total
        for copy in second:
            copy.wait_recv()
        total = out[...]
        for k in range(pairs - 1): total = total + far[k].astype(f32)
        out[...] = total
        for copy in first: copy.wait_send()
        for copy in second: copy.wait_send()
    return comm_call(body, "pair_scatter", number, [(INSIDE, array)], jax.ShapeDtypeStruct(shape, f32), INSIDE,
        [pltpu.VMEM((pairs,) + shape, bf16), pltpu.VMEM((pairs-1,) + shape, bf16), pltpu.VMEM((pairs-1,) + shape, bf16),
         pltpu.SemaphoreType.DMA((pairs,)), pltpu.SemaphoreType.DMA((pairs,)), pltpu.SemaphoreType.DMA((pairs-1,)), pltpu.SemaphoreType.DMA((pairs-1,))])

def direct_sum(array, number):
    devices = array.shape[0]; shape = array.shape[1:]
    def body(mine, out, near, sent, got, passed, taken):
        me = lax.axis_index("fsdp")
        peers = [lax.rem(me + k, devices) for k in range(1, devices)]
        greet("fsdp", peers)
        first = [sender("fsdp", mine.at[peer], near.at[k], sent.at[k], got.at[k], peer) for k, peer in enumerate(peers)]
        for copy in first: copy.start()
        total = mine[me].astype(f32)
        for k in range(devices - 1):
            first[k].wait_recv()
            total = total + near[k].astype(f32)
        out[me] = total.astype(bf16)
        second = [sender("fsdp", out.at[me], out.at[me], passed.at[k], taken.at[k], peer) for k, peer in enumerate(peers)]
        for copy in second: copy.start()
        for copy in second: copy.wait()
        for copy in first: copy.wait_send()
    return comm_call(body, "direct_sum", number, [(INSIDE, array)], jax.ShapeDtypeStruct(array.shape, bf16), INSIDE,
        [pltpu.VMEM((devices-1,) + shape, bf16)] + [pltpu.SemaphoreType.DMA((devices-1,))] * 4)

def finish(part, smalls, number):
    devices = lax.axis_size("fsdp")
    line = lax.axis_size("ctx")
    total = part.shape[0]
    half, sub = total // 2, total // devices

    few = len(smalls)

    def body(part, *refs):
        small, (part_out, *small_out) = refs[:few], refs[few : 2 * few + 1]
        near, mid, done, own, sent, got, back_sent, back_got, out_sent, out_got, *rest = refs[2 * few + 1 :]
        small_sent, small_got = rest
        me, place = lax.axis_index("fsdp"), lax.axis_index("ctx")
        barrier = pltpu.get_barrier_semaphore()
        peers = [lax.rem(me + k, devices) for k in range(1, devices)]
        for peer in peers:
            pl.semaphore_signal(barrier, inc=1, device_id={"fsdp": peer}, device_id_type=AT)
        mates = [lax.rem(place + k, line) for k in range(1, line)]
        for mate in mates:
            pl.semaphore_signal(barrier, inc=1, device_id={"ctx": mate}, device_id_type=AT)
        pl.semaphore_wait(barrier, devices + line - 2)
        extra = []
        for m, (src, dst) in enumerate(zip(small, small_out)):
            for k, mate in enumerate(mates):
                sems = small_sent.at[m, k], small_got.at[m, k]
                extra.append(sender("ctx", src, dst.at[place], *sems, mate))
            extra.append(pltpu.make_async_copy(src, dst.at[place], own.at[sub + m]))
        for copy in extra:
            copy.start()

        def moves(way, i):
            slot = i + way * half
            onward = place + 1 - 2 * way
            back = place - 1 + 2 * way
            begin = sender("ctx", part.at[slot], near.at[slot], sent.at[slot], got.at[slot], onward)
            relay = sender("ctx", mid.at[slot], near.at[slot], sent.at[slot], got.at[slot], onward)
            spread = sender("ctx", done.at[slot], done.at[slot], back_sent.at[slot], back_got.at[slot], back)
            return slot, begin, relay, spread

        def ends(way):
            return (0, line - 1) if way == 0 else (line - 1, 0)

        def turn(s, _):
            for way in range(2):
                first, last = ends(way)
                hops = place if way == 0 else line - 1 - place

                def inward(i):
                    slot, begin, relay, spread = moves(way, i)

                    @pl.when(place == first)
                    def _():
                        begin.start()

                    @pl.when(place != first)
                    def _():
                        relay.wait_recv()

                        @pl.when(place != last)
                        def _():
                            mid[slot] = (part[slot].astype(f32) + near[slot].astype(f32)).astype(bf16)
                            relay.start()

                        @pl.when(place == last)
                        def _():
                            done[slot] = (part[slot].astype(f32) + near[slot].astype(f32)).astype(bf16)

                def outward(i):
                    slot, begin, relay, spread = moves(way, i)

                    @pl.when(place != last)
                    def _():
                        spread.wait_recv()

                    @pl.when(place != first)
                    def _():
                        spread.start()

                    owner, rank = slot // sub, lax.rem(slot, sub)
                    here = me * sub + rank

                    @pl.when(me != owner)
                    def _():
                        sender("fsdp", done.at[slot], part_out.at[here], out_sent.at[slot], out_got.at[here], owner).start()

                    @pl.when(me == owner)
                    def _():
                        pltpu.make_async_copy(done.at[slot], part_out.at[slot], own.at[rank]).start()

                i = s - hops
                pl.when((i >= 0) & (i < half))(lambda: inward(i))
                k = s - (2 * (line - 1) - hops)
                pl.when((k >= 0) & (k < half))(lambda: outward(k))
            return 0

        lax.fori_loop(0, half + 2 * (line - 1), turn, 0)

        def drain(i, _):
            for way in range(2):
                first, last = ends(way)
                slot, begin, relay, spread = moves(way, i)

                @pl.when(place == first)
                def _():
                    begin.wait_send()

                @pl.when((place != first) & (place != last))
                def _():
                    relay.wait_send()

                @pl.when(place != first)
                def _():
                    spread.wait_send()

                owner, rank = slot // sub, lax.rem(slot, sub)
                copy = sender("fsdp", done.at[slot], part_out.at[slot], out_sent.at[slot], out_got.at[slot], owner)

                @pl.when(me != owner)
                def _():
                    copy.wait_send()
                    copy.wait_recv()

                @pl.when(me == owner)
                def _():
                    pltpu.make_async_copy(done.at[slot], part_out.at[slot], own.at[rank]).wait()
            return 0

        lax.fori_loop(0, half, drain, 0)
        for copy in extra:
            copy.wait()

    dma = pltpu.SemaphoreType.DMA
    return pl.pallas_call(
        body,
        name="finish",
        out_shape=[
            jax.ShapeDtypeStruct(part.shape, bf16),
            *[jax.ShapeDtypeStruct((line,) + small.shape, bf16) for small in smalls],
        ],
        in_specs=[INSIDE] + [ANY] * few,
        out_specs=[ANY] * (few + 1),
        scratch_shapes=[pltpu.VMEM(part.shape, bf16)] * 3
        + [dma((sub + few,))]
        + [dma((total,))] * 6
        + [dma((few, line - 1))] * 2,
        compiler_params=pltpu.CompilerParams(
            collective_id=number, has_side_effects=True, vmem_limit_bytes=50 * 2**20
        ),
        cost_estimate=pl.CostEstimate(flops=0, bytes_accessed=400 * 2**20, transcendentals=0),
    )(part, *smalls)


def columns(weight, count):
    return weight.reshape(weight.shape[0], count, -1).swapaxes(0, 1)


def by_rows(array):
    return with_layout_constraint(array, Layout((0, 1)))


def after(value, *earlier):
    zero = 0.0
    for array in earlier:
        corner = lax.slice(array, (0,) * array.ndim, (1,) * array.ndim).reshape(())
        zero = zero + jnp.minimum(jnp.abs(corner.astype(f32)), 0.0)
    return jax.tree.map(lambda part: part + zero.astype(part.dtype), value)


def relayed(value, earlier, rounds):
    corner = lax.slice(earlier, (0,) * earlier.ndim, (1,) * earlier.ndim).reshape(1, 1)
    token = jnp.broadcast_to(corner.astype(f32), (ROWS, LANES))
    devices = lax.axis_size("fsdp")
    for _ in range(rounds):
        token = lax.ppermute(token, "fsdp", [(i, i ^ 1) for i in range(devices)])
    return after(value, token)


def swapped(array):
    return array.swapaxes(0, 1)


def rates_of(rate_ref):
    return [jnp.broadcast_to(rate_ref[n : n + 1, :], (ROWS, LANES)) for n in range(STATE)]


def spread(sel_ref, picks, cuts):
    @pl.when(pl.program_id(1) == 0)
    def _():
        def turn(t, _):
            sel = sel_ref[t]
            for first, into in picks:
                for n in range(STATE):
                    lane = sel[:, first + n : first + n + 1]
                    into[t, n] = jnp.broadcast_to(lane, (ROWS, LANES))
            cuts[t] = jnp.broadcast_to(sel[:, 2 * STATE : 2 * STATE + 1], (ROWS, LANES))
            return 0

        lax.fori_loop(0, sel_ref.shape[0], turn, 0, unroll=4)


def carry_body(step_ref, conv_ref, sel_ref, rate_ref, out_ref, enters, cuts):
    rates = rates_of(rate_ref)
    spread(sel_ref, [(0, enters)], cuts)

    def turn(t, state):
        step = step_ref[t]
        push = step * conv_ref[t]
        fade = step + cuts[t]
        new = [
            jnp.exp(fade * rates[n]) * state[n] + enters[t, n] * push for n in range(STATE)
        ]
        return (*new, state[STATE] + fade)

    zero = jnp.zeros((ROWS, LANES), f32)
    state = lax.fori_loop(0, step_ref.shape[0], turn, (zero,) * (STATE + 1), unroll=8)
    for n in range(STATE + 1):
        out_ref[n] = state[n]


def scan_body(
    mine_ref,
    step_ref,
    conv_ref,
    sel_ref,
    rate_ref,
    carry_ref,
    out_ref,
    states_ref,
    enters,
    exits,
    cuts,
):
    rates = rates_of(rate_ref)
    spread(sel_ref, [(0, enters), (STATE, exits)], cuts)

    def join(j, state):
        return tuple(
            jnp.exp(rates[n] * carry_ref[j, STATE]) * state[n] + carry_ref[j, n]
            for n in range(STATE)
        )

    zero = jnp.zeros((ROWS, LANES), f32)
    state = lax.fori_loop(0, mine_ref[0], join, (zero,) * STATE)
    for n in range(STATE):
        states_ref[0, n] = state[n]

    def turn(t, state):
        step = step_ref[t]
        push = step * conv_ref[t]
        fade = step + cuts[t]
        new, total = [], zero
        for n in range(STATE):
            now = jnp.exp(fade * rates[n]) * state[n] + enters[t, n] * push
            states_ref[t + 1, n] = now
            total = total + exits[t, n] * now
            new.append(now)
        out_ref[t] = total
        return tuple(new)

    lax.fori_loop(0, step_ref.shape[0], turn, state, unroll=8)


def carry_back_body(step_ref, sel_ref, rate_ref, up_ref, out_ref, exits, cuts):
    rates = rates_of(rate_ref)
    spread(sel_ref, [(STATE, exits)], cuts)
    count = step_ref.shape[0]

    def turn(i, state):
        t = count - 1 - i
        up = up_ref[t]
        fade = step_ref[t] + cuts[t]
        return tuple(
            jnp.exp(fade * rates[n]) * (exits[t, n] * up + state[n]) for n in range(STATE)
        )

    zero = jnp.zeros((ROWS, LANES), f32)
    state = lax.fori_loop(0, count, turn, (zero,) * STATE, unroll=8)
    for n in range(STATE):
        out_ref[n] = state[n]


def scan_back_body(
    mine_ref,
    step_ref,
    conv_ref,
    sel_ref,
    rate_ref,
    up_ref,
    states_ref,
    span_ref,
    leave_ref,
    step_out,
    conv_out,
    sel_out,
    rate_out,
    enter_terms,
    exit_terms,
    enters,
    exits,
    cuts,
):
    rates = rates_of(rate_ref)
    spread(sel_ref, [(0, enters), (STATE, exits)], cuts)
    count = step_ref.shape[0]
    devices = span_ref.shape[0]
    zero = jnp.zeros((ROWS, LANES), f32)

    def join(i, state):
        j = devices - 1 - i
        return tuple(
            jnp.exp(rates[n] * span_ref[j]) * state[n] + leave_ref[j, n] for n in range(STATE)
        )

    state = lax.fori_loop(0, devices - 1 - mine_ref[0], join, (zero,) * STATE)
    state = state + (zero,) * STATE
    place = lax.broadcasted_iota(jnp.int32, (2 * LANES, LANES), 1)
    half = lax.broadcasted_iota(jnp.int32, (2 * LANES, LANES), 0) // LANES
    span = count // 2

    @pl.when(pl.program_id(1) == 0)
    def _():
        sel_out[...] = jnp.zeros_like(sel_out)

    for start in (span, 0):

        def turn(i, carried):
            t = start + span - 1 - i
            step, conv, up = step_ref[t], conv_ref[t], up_ref[t]
            push = step * conv
            fade = step + cuts[t]
            rows = pl.ds(pl.multiple_of((t - start) * ROWS, ROWS), ROWS)
            push_back, fade_back, new, rate_back = zero, zero, [], []
            for n in range(STATE):
                lanes = slice(n * LANES, (n + 1) * LANES)
                total = exits[t, n] * up + carried[n]
                exit_terms[rows, lanes] = up * states_ref[t + 1, n]
                enter_terms[rows, lanes] = total * push
                push_back = push_back + total * enters[t, n]
                earlier = jnp.exp(fade * rates[n]) * total
                slope = earlier * states_ref[t, n]
                fade_back = fade_back + slope * rates[n]
                new.append(earlier)
                rate_back.append(carried[STATE + n] + slope * step)
            step_out[t] = push_back * conv + fade_back
            conv_out[t] = push_back * step
            return (*new, *rate_back)

        state = lax.fori_loop(0, span, turn, state, unroll=4)
        total = jnp.zeros((span * ROWS, LANES), f32)
        for n in range(0, STATE, 2):
            lanes = slice(n * LANES, (n + 2) * LANES)
            pick = (place == n + half).astype(bf16)
            total = total + matmul(enter_terms[:, lanes].astype(bf16), pick)
            pick = (place == STATE + n + half).astype(bf16)
            total = total + matmul(exit_terms[:, lanes].astype(bf16), pick)
        sel_out[start : start + span] += total.reshape(span, ROWS, LANES)
    for n in range(STATE):
        rate_out[0, n : n + 1] = jnp.sum(state[STATE + n], axis=0, keepdims=True)


def lasting(time):
    return pl.CostEstimate(flops=0, bytes_accessed=int(time * 3.6e6), transcendentals=0)


def scan_specs(count, seqs, wide, devices):
    specs = dict(
        mine=pl.BlockSpec(memory_space=pltpu.SMEM),
        row=pl.BlockSpec((count, ROWS, LANES), lambda s, c: (0, s, c)),
        sel=pl.BlockSpec((count, ROWS, LANES), lambda s, c: (0, s, 0)),
        rate=pl.BlockSpec((STATE, LANES), lambda s, c: (0, c)),
        carry=pl.BlockSpec((STATE + 1, ROWS, LANES), lambda s, c: (0, s, c)),
        carries=pl.BlockSpec((devices, STATE + 1, ROWS, LANES), lambda s, c: (0, 0, s, c)),
        leave=pl.BlockSpec((STATE, ROWS, LANES), lambda s, c: (0, s, c)),
        leaves=pl.BlockSpec((devices, STATE, ROWS, LANES), lambda s, c: (0, 0, s, c)),
        span=pl.BlockSpec((devices, ROWS, LANES), lambda s, c: (0, s, c)),
        states=pl.BlockSpec((count + 1, STATE, ROWS, LANES), lambda s, c: (0, 0, s, c)),
        rates=pl.BlockSpec((1, STATE, LANES), lambda s, c: (s, 0, c)),
    )
    spreads = pltpu.VMEM((count, STATE, ROWS, LANES), f32)
    cuts = pltpu.VMEM((count, ROWS, LANES), f32)
    terms = pltpu.VMEM((count // 2 * ROWS, STATE * LANES), f32)
    specs["one"], specs["two"] = [spreads, cuts], [spreads, spreads, cuts]
    specs["four"] = [terms, terms, spreads, spreads, cuts]
    return specs, (seqs // ROWS, wide // LANES)


def scan_call(body, name, grid, ins, outs, shapes, scratch, work, args):
    return pl.pallas_call(
        body,
        name=name,
        grid=grid,
        in_specs=ins,
        out_specs=outs,
        out_shape=[jax.ShapeDtypeStruct(shape, f32) for shape in shapes],
        scratch_shapes=scratch,
        compiler_params=pltpu.CompilerParams(
            dimension_semantics=("arbitrary", "arbitrary"), vmem_limit_bytes=60 * 2**20
        ),
        cost_estimate=lasting(work),
    )(*args)


def shards(
    tokens,
    cotangent,
    doc_lengths,
    meta_tokens,
    norm_gain,
    w_query,
    w_keyval,
    w_attn_out,
    w_mixer_in,
    conv_taps,
    conv_bias,
    w_select,
    w_step,
    step_bias,
    log_rates,
    skip_gain,
    w_mixer_out,
    attn_gain,
    ssm_gain,
    ffn_norm_gain,
    w_gate_up,
    w_down,
):
    count = tokens.shape[1]
    width = tokens.shape[2]
    seqs = lax.axis_size("fsdp")
    ctx_index = lax.axis_index("ctx")
    ctx_count = lax.axis_size("ctx")
    inner = conv_bias.shape[0]
    wide = -(-inner // LANES) * LANES
    kv_width = KV_HEADS * HEAD
    groups = HEADS // KV_HEADS
    mine = jnp.reshape(ctx_index, (1,)).astype(jnp.int32)

    positions = ctx_index * count + jnp.arange(count, dtype=jnp.int32)
    last_pos = ctx_index * count + count - 1
    bounds = jnp.cumsum(doc_lengths[0])[:-1]
    docs = doc_number(positions, bounds)

    hidden_in = tokens[0].astype(f32)
    meta_rows = meta_tokens.shape[0]
    share = norm_gain.shape[0]
    extra_rows = -(-(meta_rows + 1) // 16) * 16
    few = doc_lengths[0]
    thin = jnp.concatenate(
        [
            norm_gain,
            attn_gain,
            ssm_gain,
            ffn_norm_gain,
            (few // 32).astype(bf16),
            (few % 32).astype(bf16),
        ]
    )
    extra = padded(
        jnp.concatenate([meta_tokens, padded(thin, 0, width)[None]], 0), 0, extra_rows
    )
    ff_cols = w_gate_up.shape[1] // (2 * seqs)
    conv_w = split_columns(w_mixer_in[:, : inner * seqs], inner, wide, seqs)
    gate_w = split_columns(w_mixer_in[:, inner * seqs :], inner, wide, seqs)
    everyone, conv_w = pair_gather(jnp.concatenate([tokens[0], extra], 0), 1, [conv_w])
    conv_w = conv_w.reshape(width, wide)
    tokens_all = everyone[:, :count].astype(f32).reshape(seqs * count, width)
    meta_f = meta_tokens.astype(f32)
    meta_all = everyone[:, count : count + meta_rows].astype(f32).reshape(META, width)
    thin = everyone[:, count + meta_rows]
    gains = thin[:, : 4 * share].reshape(seqs, 4, share).swapaxes(0, 1).astype(f32)
    gains = gains.reshape(4, width)
    gain_f, attn_norm_f, ssm_norm_f, ffn_gain_f = gains[0], gains[1], gains[2], gains[3]
    lengths = thin[:, 4 * share :].astype(jnp.int32)
    doc_count = doc_lengths.shape[1]
    lengths = 32 * lengths[:, :doc_count] + lengths[:, doc_count : 2 * doc_count]

    normed_all_f, _ = norm_rows(tokens_all, gain_f)
    normed = normed_all_f.astype(bf16)
    normed_own_f, scale_one = norm_rows(hidden_in, gain_f)
    normed_own = normed_own_f.astype(bf16)
    _, meta_scale = norm_rows(meta_f, gain_f)
    meta_normed = norm_rows(meta_all, gain_f)[0].astype(bf16)

    w_keyval, w_query = after((w_keyval, w_query), everyone)
    gate_w = exchanged(after(gate_w, everyone)).reshape(width, wide)
    keyval_w = lax.all_gather(w_keyval, "fsdp", axis=0, tiled=True)
    query_w = lax.all_gather(w_query, "fsdp", axis=0, tiled=True)
    ff_wide = -(-ff_cols // LANES) * LANES
    ff_w = exchanged(split_columns(w_gate_up, ff_cols, ff_wide, seqs))
    ff_w = ff_w.reshape(width, 2 * ff_wide)

    conv_in = swapped(matmul(normed, conv_w).astype(bf16).reshape(seqs, count, wide))
    gate_in = swapped(matmul(normed, gate_w).astype(bf16).reshape(seqs, count, wide))
    seq_bounds = jnp.cumsum(lengths, axis=1)[:, :-1]

    def numbers(places):
        return jnp.sum((places[:, None, None] >= seq_bounds[None]).astype(jnp.int32), axis=-1)

    seq_docs = numbers(positions)
    starts = (positions[:, None] == 0) | (seq_docs != numbers(positions - 1))
    taps_f = padded(conv_taps.astype(f32), 1, wide)
    rim = shifted(conv_in[count - (CONV - 1) :], "ctx", 1)
    extended = jnp.concatenate([rim, conv_in], 0).astype(f32)
    valid_rows = []
    for tap in range(CONV):
        earlier = positions - (CONV - 1 - tap)
        valid = (earlier[:, None] >= 0) & (numbers(earlier) == seq_docs)
        valid_rows.append(valid.astype(f32)[:, :, None])
    pre_conv = padded(conv_bias.astype(f32), 0, wide)[None, None, :]
    for tap in range(CONV):
        pre_conv = pre_conv + taps_f[tap] * extended[tap : tap + count] * valid_rows[tap]
    conv_sig = jax.nn.sigmoid(pre_conv)
    conv_out = (pre_conv * conv_sig).astype(bf16)
    conv_f = conv_out.astype(f32)
    conv_rows = conv_out.reshape(count * seqs, wide)
    select_w = padded(w_select, 0, wide)
    step_w = padded(w_step, 1, wide)
    selected = direct_sum(
        matmul(conv_rows, select_w).astype(bf16).reshape(seqs, count, -1), 3
    ).reshape(count * seqs, -1)
    step_low = selected[:, :DT_RANK]
    step_pre = matmul(step_low, step_w) + padded(step_bias.astype(f32), 0, wide)[None, :]
    step_pre = step_pre.reshape(count, seqs, wide)
    steps = jax.nn.softplus(step_pre)
    rates = -jnp.exp(padded(log_rates.astype(f32), 1, wide))
    sel = jnp.concatenate(
        [
            selected[:, DT_RANK:].astype(f32).reshape(count, seqs, 2 * STATE),
            jnp.where(starts, CUT, 0.0).astype(f32)[:, :, None],
        ],
        2,
    )
    sel = padded(sel, 2, LANES)
    spec, grid = scan_specs(count, seqs, wide, ctx_count)
    row_shape = (count, seqs, wide)
    (carry,) = scan_call(
        carry_body,
        "mamba_carry",
        grid,
        [spec["row"], spec["row"], spec["sel"], spec["rate"]],
        [spec["carry"]],
        [(STATE + 1, seqs, wide)],
        spec["one"],
        15,
        (steps, conv_f, sel, rates),
    )
    keyvals = matmul(normed_own, keyval_w).astype(bf16)
    carries, keyvals_all = direct_many(
        [carry.astype(bf16), keyvals], ["gather", "gather"], "ctx", 4
    )
    carries = carries.astype(f32)
    attn_out_w = lax.all_gather(w_attn_out, "fsdp", axis=0, tiled=True)
    out_back_all = gathered(cotangent[0], "fsdp").reshape(seqs * count, width)
    scanned, states = scan_call(
        scan_body,
        "mamba_scan",
        grid,
        [spec["mine"], spec["row"], spec["row"], spec["sel"], spec["rate"], spec["carries"]],
        [spec["row"], spec["states"]],
        [row_shape, (count + 1, STATE, seqs, wide)],
        spec["two"],
        26,
        (mine, steps, conv_f, sel, rates, carries),
    )
    skip_f = padded(skip_gain.astype(f32), 0, wide)
    ssm_out = scanned + skip_f * conv_f
    gate_f = gate_in.astype(f32)
    gate_sig = jax.nn.sigmoid(gate_f)
    gate_act = gate_f * gate_sig
    mixer_mid = swapped((ssm_out * gate_act).astype(bf16)).reshape(seqs * count, wide)
    mixer_out_w = padded(w_mixer_out, 0, wide)
    mixer_proj = pair_scatter(
        by_rows(matmul(mixer_mid, mixer_out_w).astype(bf16)).reshape(seqs, count, width), 6
    )
    queries = matmul(normed_own, query_w).astype(bf16)
    meta_kv = matmul(meta_normed, keyval_w).astype(bf16)
    query_heads = queries.reshape(count, KV_HEADS, groups, HEAD)
    piece = keyvals_all.reshape(ctx_count * count, 2 * kv_width)
    joined = jnp.concatenate([meta_kv, piece], 0)
    keys = joined[:, :kv_width].reshape(-1, KV_HEADS, HEAD)
    values = joined[:, kv_width:].reshape(-1, KV_HEADS, HEAD)
    key_pos = jnp.arange(piece.shape[0], dtype=jnp.int32)
    key_doc = doc_number(key_pos, bounds)
    shown = (key_pos[None, :] <= positions[:, None]) & (key_doc[None, :] == docs[:, None])
    shown = jnp.concatenate([jnp.full((count, META), True), shown], 1)
    scores = (
        jnp.einsum("qgha,kga->ghqk", query_heads, keys, preferred_element_type=f32) * 0.125
    )
    scores = jnp.where(shown[None, None], scores, NEG)
    top = jnp.max(scores, axis=-1, keepdims=True)
    weights = jnp.exp(scores - top)
    weights = weights / jnp.sum(weights, axis=-1, keepdims=True)
    attn_heads_f = jnp.einsum(
        "ghqk,kga->qgha", weights.astype(bf16), values, preferred_element_type=f32
    )
    attn_b = attn_heads_f.reshape(count, HEADS * HEAD).astype(bf16)
    attn_proj = matmul(attn_b, attn_out_w)
    attn_branch, attn_scale = norm_rows(attn_proj, attn_norm_f)

    ssm_branch, ssm_scale = norm_rows(mixer_proj, ssm_norm_f)
    middle = hidden_in + 0.5 * (attn_branch + ssm_branch)

    normed_two_f, scale_two = norm_rows(middle, ffn_gain_f)
    normed_two = pair_gather(normed_two_f.astype(bf16), 7).reshape(seqs * count, width)
    gate_up = matmul(normed_two, ff_w).astype(bf16)
    gate_v, up_v = gate_up[:, :ff_wide].astype(f32), gate_up[:, ff_wide:].astype(f32)
    ffn_sig = jax.nn.sigmoid(gate_v)
    hidden_ff = (gate_v * ffn_sig * up_v).astype(bf16)
    down_w = padded(w_down, 0, ff_wide)
    output = by_rows(matmul(hidden_ff, down_w).astype(bf16))

    output = exchanged(output.reshape(seqs, count, width)).astype(f32)
    block_out = (middle + jnp.sum(output, axis=0)).astype(bf16)[None]
    down_back = tmatmul(hidden_ff, out_back_all)[:ff_cols]
    hidden_back = matmul_t(out_back_all, down_w).astype(bf16).astype(f32)
    up_back = hidden_back * gate_v * ffn_sig
    gate_back = hidden_back * up_v * ffn_sig * (1.0 + gate_v * (1.0 - ffn_sig))
    gate_up_back = jnp.concatenate([gate_back.astype(bf16), up_back.astype(bf16)], 1)
    ff_w_back = tmatmul(normed_two, gate_up_back)
    normed_two_back = matmul_t(gate_up_back, ff_w).astype(bf16)
    down_back = down_back.astype(bf16)
    ff_w_back = ff_w_back.astype(bf16)
    ff_w_sum = lax.psum(ff_w_back, "ctx")
    normed_two_back = by_rows(relayed(normed_two_back, ff_w_back, 2))
    normed_two_back = pair_scatter(normed_two_back.reshape(seqs, count, width), 8)
    middle_norm_back, ffn_gain_back = norm_back(middle, scale_two, ffn_gain_f, normed_two_back)
    middle_back = cotangent[0].astype(f32) + middle_norm_back
    branch_back = 0.5 * middle_back
    ssm_proj_back, ssm_gain_back = norm_back(mixer_proj, ssm_scale, ssm_norm_f, branch_back)
    attn_proj_back, attn_gain_back = norm_back(attn_proj, attn_scale, attn_norm_f, branch_back)
    attn_own_back = attn_proj_back.astype(bf16)
    proj_back, attn_cols = pair_gather(
        jnp.concatenate([ssm_proj_back.astype(bf16), attn_own_back], 0),
        9,
        [columns(attn_b, seqs)],
    )
    attn_cols = attn_cols.reshape(seqs * count, -1)
    ssm_proj_back = proj_back[:, :count].reshape(seqs * count, width)
    attn_proj_back = proj_back[:, count:].reshape(seqs * count, width)

    mixer_out_back = tmatmul(mixer_mid, ssm_proj_back)[:inner].astype(bf16)
    attn_out_back = tmatmul(attn_cols, attn_proj_back).astype(bf16)
    mid_back = matmul_t(ssm_proj_back, mixer_out_w).astype(bf16).reshape(seqs, count, wide)
    mid_back = swapped(mid_back).astype(f32)
    ssm_back = mid_back * gate_act
    gate_in_back = mid_back * ssm_out * gate_sig * (1.0 + gate_f * (1.0 - gate_sig))
    skip_back = jnp.sum(ssm_back * conv_f, axis=(0, 1))
    (leave,) = scan_call(
        carry_back_body,
        "mamba_carry_back",
        grid,
        [spec["row"], spec["sel"], spec["rate"], spec["row"]],
        [spec["leave"]],
        [(STATE, seqs, wide)],
        spec["one"],
        15,
        (steps, sel, rates, ssm_back),
    )
    heads_back = matmul_t(attn_own_back, attn_out_w).astype(bf16)
    heads_back = heads_back.reshape(count, KV_HEADS, groups, HEAD)
    delta = jnp.sum(heads_back.astype(f32) * attn_heads_f, axis=-1)
    delta = delta.transpose(1, 2, 0)[..., None]
    weights_back = jnp.einsum("qgha,kga->ghqk", heads_back, values, preferred_element_type=f32)
    scores_back = (weights * (weights_back - delta)).astype(bf16)
    query_back = (
        jnp.einsum("ghqk,kga->qgha", scores_back, keys, preferred_element_type=f32) * 0.125
    )
    keys_back = (
        jnp.einsum("ghqk,qgha->kga", scores_back, query_heads, preferred_element_type=f32) * 0.125
    )
    values_back = jnp.einsum(
        "ghqk,qgha->kga", weights.astype(bf16), heads_back, preferred_element_type=f32
    )
    kv_back = jnp.concatenate(
        [keys_back.reshape(-1, kv_width), values_back.reshape(-1, kv_width)], 1
    )
    buffer = kv_back[META:].astype(bf16).reshape(ctx_count, count, 2 * kv_width)
    meta_kv_own = kv_back[:META].astype(bf16)
    query_back = query_back.reshape(count, HEADS * HEAD).astype(bf16)
    (leaves,) = direct_many([leave.astype(bf16)], ["gather"], "ctx", 5)
    owned = lax.all_to_all(buffer, "ctx", 0, 0)
    owned = jnp.sum(owned.astype(f32), axis=0).astype(bf16)
    kv_own = owned
    attn_normed_back = matmul_t(query_back, query_w) + matmul_t(kv_own, keyval_w)
    meta_normed_back = matmul_t(meta_kv_own, keyval_w)
    qkv_back, meta_kv_back = direct_many(
        [
            jnp.concatenate([columns(query_back, seqs), columns(kv_own, seqs)], 2),
            columns(meta_kv_own, seqs),
        ],
        ["swap"] * 2,
        "fsdp",
        12,
    )
    qkv_back = qkv_back.reshape(seqs * count, -1)
    meta_kv_back = jnp.sum(meta_kv_back.astype(f32), axis=0).astype(bf16)
    second = after((down_back, mixer_out_back, attn_out_back), ff_w_sum, qkv_back)
    token = relayed(jnp.zeros((ROWS, LANES), f32), after(second[0], *second[1:]), 2)
    second = lax.psum(second, "ctx")
    down_back, mixer_out_back, attn_out_back = [part.astype(f32) for part in second]
    leaves = after(leaves.astype(f32), token)
    steps_back, conv_back, sel_back, rates_back = scan_call(
        scan_back_body,
        "mamba_scan_back",
        grid,
        [
            spec["mine"],
            spec["row"],
            spec["row"],
            spec["sel"],
            spec["rate"],
            spec["row"],
            spec["states"],
            spec["span"],
            spec["leaves"],
        ],
        [spec["row"], spec["row"], spec["sel"], spec["rates"]],
        [row_shape, row_shape, (count, seqs, LANES), (seqs // ROWS, STATE, wide)],
        spec["four"],
        47,
        (mine, steps, conv_f, sel, rates, ssm_back, states, carries[:, STATE], leaves),
    )
    rates_log_back = jnp.sum(rates_back, axis=0) * rates
    step_pre_back = steps_back * jax.nn.sigmoid(step_pre)
    step_shift_back = jnp.sum(step_pre_back, axis=(0, 1))
    step_pre_back = step_pre_back.astype(bf16).reshape(count * seqs, wide)
    step_w_back = tmatmul(step_low, step_pre_back)
    selected_back = jnp.concatenate(
        [
            matmul_t(step_pre_back, step_w),
            sel_back[:, :, : 2 * STATE].reshape(count * seqs, 2 * STATE),
        ],
        1,
    ).astype(bf16)
    selected_back = direct_sum(selected_back.reshape(seqs, count, -1), 10)
    selected_back = selected_back.reshape(count * seqs, -1)
    select_w_back = tmatmul(selected_back, conv_rows)[:, :inner]
    conv_back = (
        conv_back
        + skip_f * ssm_back
        + matmul_t(selected_back, select_w).reshape(count, seqs, wide)
    )
    pre_back = conv_back * conv_sig * (1.0 + pre_conv * (1.0 - conv_sig))
    taps_bias_back = jnp.sum(pre_back, axis=(0, 1))
    tap_rows = []
    extended_back = jnp.zeros((count + CONV - 1, seqs, wide), f32)
    for tap in range(CONV):
        masked_back = pre_back * valid_rows[tap]
        tap_rows.append(jnp.sum(masked_back * extended[tap : tap + count], axis=(0, 1)))
        extended_back = extended_back + jnp.pad(
            taps_f[tap] * masked_back, ((tap, CONV - 1 - tap), (0, 0), (0, 0))
        )
    rim_back = shifted(extended_back[: CONV - 1].astype(bf16), "ctx", -1).astype(f32)
    conv_in_back = extended_back[CONV - 1 :] + jnp.pad(
        rim_back, ((count - (CONV - 1), 0), (0, 0), (0, 0))
    )
    conv_in_back = swapped(conv_in_back.astype(bf16)).reshape(seqs * count, wide)
    gate_in_back = swapped(gate_in_back.astype(bf16)).reshape(seqs * count, wide)

    thin = jnp.concatenate(
        [
            tap_rows[0][None],
            tap_rows[1][None],
            tap_rows[2][None],
            tap_rows[3][None],
            taps_bias_back[None],
            step_shift_back[None],
            skip_back[None],
            rates_log_back,
            step_w_back,
        ],
        0,
    )[:, :inner]
    q_cols = w_query.shape[1] // seqs
    in_cols = 2 * inner + qkv_back.shape[1]
    in_wide = -(-in_cols // LANES) * LANES
    in_back = padded(
        jnp.concatenate([conv_in_back[:, :inner], gate_in_back[:, :inner], qkv_back], 1),
        1,
        in_wide,
    )
    in_w_back = tmatmul(normed, in_back) + jnp.pad(
        tmatmul(meta_normed, meta_kv_back), ((0, 0), (2 * inner + q_cols, in_wide - in_cols))
    )
    in_w_back = in_w_back.astype(bf16)
    part = by_rows(matmul_t(conv_in_back, conv_w) + matmul_t(gate_in_back, gate_w))
    tokens_scale = lax.rsqrt(jnp.mean(tokens_all * tokens_all, axis=-1, keepdims=True) + EPS)
    meta_all_scale = lax.rsqrt(jnp.mean(meta_all * meta_all, axis=-1, keepdims=True) + EPS)
    gain_back = (
        jnp.sum(part * tokens_all * tokens_scale, axis=0)
        + jnp.sum(attn_normed_back * hidden_in * scale_one, axis=0)
        + jnp.sum(meta_normed_back * meta_all * meta_all_scale, axis=0)
    )
    gains_back = jnp.stack([gain_back, attn_gain_back, ssm_gain_back, ffn_gain_back])
    gains_back = gains_back.astype(bf16).reshape(4, seqs, share).swapaxes(0, 1)
    tail = jnp.concatenate(
        [
            meta_normed_back.astype(bf16).reshape(seqs, meta_rows, width),
            padded(gains_back.reshape(seqs, 1, 4 * share), 2, width),
        ],
        1,
    )
    totals = pair_scatter(
        jnp.concatenate(
            [
                part.astype(bf16).reshape(seqs, count, width),
                padded(tail, 1, extra_rows),
            ],
            1,
        ),
        11,
    )
    input_norm_back, _ = norm_back(
        hidden_in, scale_one, gain_f, totals[:count] + attn_normed_back
    )
    first = count
    meta_back, _ = norm_back(meta_f, meta_scale, gain_f, totals[first : first + meta_rows])
    gains_back = totals[first + meta_rows, : 4 * share]
    grad_tokens = (middle_back + input_norm_back)[None]

    small = jnp.concatenate([meta_back, padded(gains_back, 0, width)[None]], 0)
    small = padded(small.astype(bf16), 0, extra_rows)
    thin = jnp.concatenate([thin, select_w_back], 0).astype(bf16)
    thin_rows = thin.shape[0]
    thin = padded(thin, 0, -(-thin_rows // 16) * 16)
    in_w_back, small, thin = finish(in_w_back.reshape(seqs, share, in_wide), [small, thin], 13)
    thin = jnp.sum(thin.astype(f32), axis=0)
    select_first = thin_rows - select_w_back.shape[0]
    select_w_back = thin[select_first:thin_rows].T
    small = jnp.sum(small.astype(f32), axis=0)
    meta_back = small[:meta_rows]
    gains = small[meta_rows, : 4 * share].reshape(4, share)

    (grad_gate_up,) = join_columns(
        exchanged(ff_w_sum.reshape(seqs, share, 2 * ff_wide)),
        [[(0, ff_cols), (ff_wide, ff_cols)]],
    )
    first = 2 * inner
    grad_mixer_in, grad_query, grad_keyval = join_columns(
        in_w_back,
        [
            [(0, inner), (inner, inner)],
            [(first, q_cols)],
            [(first + q_cols, in_cols - first - q_cols)],
        ],
    )
    return (
        block_out,
        grad_tokens,
        meta_back,
        gains[0],
        grad_query,
        grad_keyval,
        attn_out_back,
        grad_mixer_in,
        thin[:CONV],
        thin[CONV],
        select_w_back,
        thin[CONV + 3 + STATE : CONV + 3 + STATE + DT_RANK],
        thin[CONV + 1],
        thin[CONV + 3 : CONV + 3 + STATE],
        thin[CONV + 2],
        mixer_out_back,
        gains[1],
        gains[2],
        gains[3],
        grad_gate_up,
        down_back,
    )


def solution(mesh):
    rows, cols, one = P("fsdp", None), P(None, "fsdp"), P("fsdp")
    split = P("fsdp", "ctx", None)
    in_specs = (
        split,
        split,
        rows,
        rows,
        one,
        rows,
        rows,
        rows,
        rows,
        cols,
        one,
        rows,
        cols,
        one,
        cols,
        one,
        rows,
        one,
        one,
        one,
        rows,
        rows,
    )
    out_specs = (
        split,
        split,
        rows,
        one,
        rows,
        rows,
        rows,
        rows,
        cols,
        one,
        rows,
        cols,
        one,
        cols,
        one,
        rows,
        one,
        one,
        one,
        rows,
        rows,
    )
    return jax.shard_map(shards, mesh=mesh, in_specs=in_specs, out_specs=out_specs, check_vma=False)
```

```python
import jax
import jax.numpy as jnp
from jax import lax
from jax.experimental import pallas as pl
from jax.experimental.layout import Layout, with_layout_constraint
from jax.experimental.pallas import tpu as pltpu
from jax.sharding import PartitionSpec as P

HEADS = 25
KV_HEADS = 5
HEAD = 64
META = 128
STATE = 16
CONV = 4
DT_RANK = 100

EPS = 1e-05
NEG = -1e30
CUT = 1e30
LANES = 128
ROWS = 8
f32 = jnp.float32
bf16 = jnp.bfloat16


def matmul(left, right):
    return jnp.dot(left, right, preferred_element_type=f32)


def tmatmul(left, right):
    return lax.dot_general(left, right, (((0,), (0,)), ((), ())), preferred_element_type=f32)


def matmul_t(left, right):
    return lax.dot_general(left, right, (((1,), (1,)), ((), ())), preferred_element_type=f32)


def norm_rows(value, gain):
    scale = lax.rsqrt(jnp.mean(value * value, axis=-1, keepdims=True) + EPS)
    return (value * scale * gain, scale)


def norm_back(value, scale, gain, upstream):
    tilted = upstream * gain
    mixing = jnp.mean(tilted * value, axis=-1, keepdims=True)
    return (
        scale * tilted - value * scale * scale * scale * mixing,
        jnp.sum(upstream * value * scale, axis=0),
    )


def doc_number(positions, bounds):
    return jnp.sum((positions[:, None] >= bounds[None, :]).astype(jnp.int32), axis=1)


def padded(array, axis, size):
    widths = [(0, 0)] * array.ndim
    widths[axis] = (0, size - array.shape[axis])
    return jnp.pad(array, widths)


def shifted(block, axis, distance):
    devices = range(lax.axis_size(axis))
    route = [(i - distance, i) for i in devices if i - distance in devices]
    return lax.ppermute(block, axis, route)


def gathered(array, axis):
    return lax.all_gather(array, axis, axis=0)


def exchanged(array):
    return lax.all_to_all(array, "fsdp", 0, 0)


def scattered(array):
    return lax.psum_scatter(array.astype(bf16), "fsdp", scatter_dimension=0, tiled=False).astype(
        f32
    )


AT = pl.DeviceIdType.MESH
ANY = pl.BlockSpec(memory_space=pl.ANY)
INSIDE = pl.BlockSpec(memory_space=pltpu.VMEM)

def greet(axis, peers):
    barrier = pltpu.get_barrier_semaphore()
    for peer in peers:
        pl.semaphore_signal(barrier, inc=1, device_id={axis: peer}, device_id_type=AT)
    pl.semaphore_wait(barrier, len(peers))

def sender(axis, src, dst, send, recv, peer):
    return pltpu.make_async_remote_copy(src_ref=src, dst_ref=dst, send_sem=send, recv_sem=recv, device_id={axis: peer}, device_id_type=AT)

def comm_call(body, name, number, ins, shape, out_spec, scratch, time=25):
    return pl.pallas_call(body, name=name, out_shape=shape, in_specs=[spec for spec, _ in ins], out_specs=out_spec, scratch_shapes=scratch,
        cost_estimate=lasting(time), compiler_params=pltpu.CompilerParams(collective_id=number, has_side_effects=True, vmem_limit_bytes=40*2**20))(*[array for _, array in ins])

def pair_gather(array, number, swaps=()):
    devices = lax.axis_size("fsdp")
    pairs = devices // 2
    many = len(swaps)

    def body(*refs):
        mine, moved = refs[0], refs[1 : many + 1]
        out, landed = refs[many + 1], refs[many + 2 : 2 * many + 2]
        own, sent, got, passed, taken, moved_sent, moved_got = refs[2 * many + 2 :]
        me = lax.axis_index("fsdp")
        pair, core = me // 2, lax.rem(me, 2)
        mate = me + 1 - 2 * core
        peers = [2 * lax.rem(pair + k, pairs) + core for k in range(1, pairs)]
        others = [lax.rem(me + k, devices) for k in range(1, devices)]
        greet("fsdp", others if many else [mate, *peers])
        first = [
            sender("fsdp", mine, out.at[me], sent.at[k], got.at[k], peer)
            for k, peer in enumerate([mate, *peers])
        ]
        for copy in first[1:]:
            copy.start()
        first[0].start()
        extra = [
            sender(
                "fsdp",
                src.at[peer],
                dst.at[me],
                moved_sent.at[m, k],
                moved_got.at[m, k],
                peer,
            )
            for m, (src, dst) in enumerate(zip(moved, landed))
            for k, peer in enumerate(others)
        ]
        for copy in extra:
            copy.start()
        local = [pltpu.make_async_copy(mine, out.at[me], own.at[0])]
        for m, (src, dst) in enumerate(zip(moved, landed)):
            local.append(pltpu.make_async_copy(src.at[me], dst.at[me], own.at[m + 1]))
        for copy in local:
            copy.start()
        second = []
        for k in range(1, pairs):
            slot = 2 * lax.rem(pair + pairs - k, pairs) + core
            first[k].wait_recv()
            copy = sender(
                "fsdp", out.at[slot], out.at[slot], passed.at[k - 1], taken.at[k - 1], mate
            )
            copy.start()
            second.append(copy)
        first[0].wait_recv()
        for copy in first:
            copy.wait_send()
        for copy in second + extra + local:
            copy.wait()

    dma = pltpu.SemaphoreType.DMA
    shapes = [jax.ShapeDtypeStruct((devices,) + array.shape, array.dtype)]
    shapes += [jax.ShapeDtypeStruct(swap.shape, swap.dtype) for swap in swaps]
    result = comm_call(
        body,
        "pair_gather",
        number,
        [(ANY, array)] + [(ANY, swap) for swap in swaps],
        shapes,
        [ANY] * (many + 1),
        [dma((many + 1,)), dma((pairs,)), dma((pairs,)), dma((pairs - 1,)), dma((pairs - 1,))]
        + [dma((max(many, 1), devices - 1))] * 2,
    )
    return result if many else result[0]


def direct_many(arrays, modes, axis, number):
    devices = lax.axis_size(axis)
    many = len(arrays)

    def body(*refs):
        mine, out, (own, sent, got) = refs[:many], refs[many : 2 * many], refs[2 * many :]
        me = lax.axis_index(axis)
        peers = [lax.rem(me + k, devices) for k in range(1, devices)]
        greet(axis, peers)
        copies = []
        for m, (src, dst, mode) in enumerate(zip(mine, out, modes)):
            for k, peer in enumerate(peers):
                part = src if mode == "gather" else src.at[peer]
                copies.append(sender(axis, part, dst.at[me], sent.at[m, k], got.at[m, k], peer))
        for copy in copies:
            copy.start()
        for m, (src, dst, mode) in enumerate(zip(mine, out, modes)):
            part = src if mode == "gather" else src.at[me]
            copies.append(pltpu.make_async_copy(part, dst.at[me], own.at[m]))
            copies[-1].start()
        for copy in copies:
            copy.wait()

    dma = pltpu.SemaphoreType.DMA
    shapes = [
        jax.ShapeDtypeStruct(
            (devices,) + array.shape if mode == "gather" else array.shape, array.dtype
        )
        for array, mode in zip(arrays, modes)
    ]
    return comm_call(
        body,
        "direct_many",
        number,
        [(ANY, array) for array in arrays],
        shapes,
        [ANY] * many,
        [dma((many,)), dma((many, devices - 1)), dma((many, devices - 1))],
    )


def split_columns(weight, cols, wide, seqs):
    rows = weight.shape[0]
    kinds = weight.shape[1] // (cols * seqs)

    def body(mine, out):
        for m in range(kinds):
            for f in range(seqs):
                first = (m * seqs + f) * cols
                out[f, :, m * wide : m * wide + cols] = mine[:, first : first + cols]
                if wide > cols:
                    blank = jnp.zeros((rows, wide - cols), bf16)
                    out[f, :, m * wide + cols : (m + 1) * wide] = blank

    return pl.pallas_call(
        body,
        name="split_columns",
        out_shape=jax.ShapeDtypeStruct((seqs, rows, kinds * wide), bf16),
        in_specs=[INSIDE],
        out_specs=INSIDE,
        compiler_params=pltpu.CompilerParams(vmem_limit_bytes=40 * 2**20),
    )(weight)


def join_columns(array, kinds):
    seqs, rows, _ = array.shape

    def body(mine, *outs):
        for out, parts in zip(outs, kinds):
            for m, (first, cols) in enumerate(parts):
                for f in range(seqs):
                    place = (m * seqs + f) * cols
                    out[:, place : place + cols] = mine[f, :, first : first + cols].astype(f32)

    return pl.pallas_call(
        body,
        name="join_columns",
        out_shape=[
            jax.ShapeDtypeStruct((rows, seqs * sum(cols for _, cols in parts)), f32)
            for parts in kinds
        ],
        in_specs=[INSIDE],
        out_specs=[INSIDE] * len(kinds),
        compiler_params=pltpu.CompilerParams(vmem_limit_bytes=48 * 2**20),
    )(array)


def pair_scatter(array, number):
    devices = array.shape[0]; pairs = devices // 2; shape = array.shape[1:]
    def body(mine, out, near, summed, far, sent, got, passed, taken):
        me = lax.axis_index("fsdp"); pair = me // 2; core = lax.rem(me, 2); mate = me + 1 - 2 * core
        places = [lax.rem(pair + k, pairs) for k in range(1, pairs + 1)]
        greet("fsdp", [mate, *[2 * q + core for q in places[:-1]]])
        first = [sender("fsdp", mine.at[2 * q + 1 - core], near.at[k], sent.at[k], got.at[k], mate) for k, q in enumerate(places)]
        for copy in first: copy.start()
        second = []
        for k, q in enumerate(places):
            first[k].wait_recv()
            total = mine[2 * q + core].astype(f32) + near[k].astype(f32)
            if k < pairs - 1:
                summed[k] = total.astype(bf16)
                copy = sender("fsdp", summed.at[k], far.at[k], passed.at[k], taken.at[k], 2 * q + core)
                copy.start(); second.append(copy)
            else:
                out[...] = total
        for copy in second:
            copy.wait_recv()
        total = out[...]
        for k in range(pairs - 1): total = total + far[k].astype(f32)
        out[...] = total
        for copy in first: copy.wait_send()
        for copy in second: copy.wait_send()
    return comm_call(body, "pair_scatter", number, [(INSIDE, array)], jax.ShapeDtypeStruct(shape, f32), INSIDE,
        [pltpu.VMEM((pairs,) + shape, bf16), pltpu.VMEM((pairs-1,) + shape, bf16), pltpu.VMEM((pairs-1,) + shape, bf16),
         pltpu.SemaphoreType.DMA((pairs,)), pltpu.SemaphoreType.DMA((pairs,)), pltpu.SemaphoreType.DMA((pairs-1,)), pltpu.SemaphoreType.DMA((pairs-1,))])

def direct_sum(array, number):
    devices = array.shape[0]; shape = array.shape[1:]
    def body(mine, out, near, sent, got, passed, taken):
        me = lax.axis_index("fsdp")
        peers = [lax.rem(me + k, devices) for k in range(1, devices)]
        greet("fsdp", peers)
        first = [sender("fsdp", mine.at[peer], near.at[k], sent.at[k], got.at[k], peer) for k, peer in enumerate(peers)]
        for copy in first: copy.start()
        total = mine[me].astype(f32)
        for k in range(devices - 1):
            first[k].wait_recv()
            total = total + near[k].astype(f32)
        out[me] = total.astype(bf16)
        second = [sender("fsdp", out.at[me], out.at[me], passed.at[k], taken.at[k], peer) for k, peer in enumerate(peers)]
        for copy in second: copy.start()
        for copy in second: copy.wait()
        for copy in first: copy.wait_send()
    return comm_call(body, "direct_sum", number, [(INSIDE, array)], jax.ShapeDtypeStruct(array.shape, bf16), INSIDE,
        [pltpu.VMEM((devices-1,) + shape, bf16)] + [pltpu.SemaphoreType.DMA((devices-1,))] * 4)

def finish(part, smalls, spare, number):
    devices = lax.axis_size("fsdp")
    line = lax.axis_size("ctx")
    total = part.shape[0]
    half, sub = total // 2, total // devices

    few = len(smalls)

    def body(part, *refs):
        small, (part_out, spare_out, *small_out) = refs[:few], refs[few : 2 * few + 2]
        near, mid, done, own, sent, got, back_sent, back_got, out_sent, out_got, *rest = refs[2 * few + 2 :]
        small_sent, small_got = rest
        me, place = lax.axis_index("fsdp"), lax.axis_index("ctx")
        barrier = pltpu.get_barrier_semaphore()
        peers = [lax.rem(me + k, devices) for k in range(1, devices)]
        for peer in peers:
            pl.semaphore_signal(barrier, inc=1, device_id={"fsdp": peer}, device_id_type=AT)
        mates = [lax.rem(place + k, line) for k in range(1, line)]
        for mate in mates:
            pl.semaphore_signal(barrier, inc=1, device_id={"ctx": mate}, device_id_type=AT)
        pl.semaphore_wait(barrier, devices + line - 2)
        extra = []
        for m, (src, dst) in enumerate(zip(small, small_out)):
            for k, mate in enumerate(mates):
                sems = small_sent.at[m, k], small_got.at[m, k]
                extra.append(sender("ctx", src, dst.at[place], *sems, mate))
            extra.append(pltpu.make_async_copy(src, dst.at[place], own.at[sub + m]))
        for copy in extra:
            copy.start()

        def moves(way, i):
            slot = i + way * half
            onward = place + 1 - 2 * way
            back = place - 1 + 2 * way
            begin = sender("ctx", part.at[slot], near.at[slot], sent.at[slot], got.at[slot], onward)
            relay = sender("ctx", mid.at[slot], near.at[slot], sent.at[slot], got.at[slot], onward)
            spread = sender("ctx", done.at[slot], done.at[slot], back_sent.at[slot], back_got.at[slot], back)
            return slot, begin, relay, spread

        def ends(way):
            return (0, line - 1) if way == 0 else (line - 1, 0)

        def turn(s, _):
            for way in range(2):
                first, last = ends(way)
                hops = place if way == 0 else line - 1 - place

                def inward(i):
                    slot, begin, relay, spread = moves(way, i)

                    @pl.when(place == first)
                    def _():
                        begin.start()

                    @pl.when(place != first)
                    def _():
                        relay.wait_recv()

                        @pl.when(place != last)
                        def _():
                            mid[slot] = (part[slot].astype(f32) + near[slot].astype(f32)).astype(bf16)
                            relay.start()

                        @pl.when(place == last)
                        def _():
                            done[slot] = (part[slot].astype(f32) + near[slot].astype(f32)).astype(bf16)

                def outward(i):
                    slot, begin, relay, spread = moves(way, i)

                    @pl.when(place != last)
                    def _():
                        spread.wait_recv()

                    @pl.when(place != first)
                    def _():
                        spread.start()

                    owner, rank = slot // sub, lax.rem(slot, sub)
                    here = me * sub + rank

                    @pl.when(me != owner)
                    def _():
                        sender("fsdp", done.at[slot], part_out.at[here], out_sent.at[slot], out_got.at[here], owner).start()

                    @pl.when(me == owner)
                    def _():
                        pltpu.make_async_copy(done.at[slot], part_out.at[slot], own.at[rank]).start()

                i = s - hops
                pl.when((i >= 0) & (i < half))(lambda: inward(i))
                k = s - (2 * (line - 1) - hops)
                pl.when((k >= 0) & (k < half))(lambda: outward(k))
            return 0

        lax.fori_loop(0, half + 2 * (line - 1), turn, 0)

        def drain(i, _):
            for way in range(2):
                first, last = ends(way)
                slot, begin, relay, spread = moves(way, i)

                @pl.when(place == first)
                def _():
                    begin.wait_send()

                @pl.when((place != first) & (place != last))
                def _():
                    relay.wait_send()

                @pl.when(place != first)
                def _():
                    spread.wait_send()

                owner, rank = slot // sub, lax.rem(slot, sub)
                copy = sender("fsdp", done.at[slot], part_out.at[slot], out_sent.at[slot], out_got.at[slot], owner)

                @pl.when(me != owner)
                def _():
                    copy.wait_send()
                    copy.wait_recv()

                @pl.when(me == owner)
                def _():
                    pltpu.make_async_copy(done.at[slot], part_out.at[slot], own.at[rank]).wait()
            return 0

        lax.fori_loop(0, half, drain, 0)
        spare_out[...] = done[:, :, spare:]
        for copy in extra:
            copy.wait()

    dma = pltpu.SemaphoreType.DMA
    return pl.pallas_call(
        body,
        name="finish",
        out_shape=[
            jax.ShapeDtypeStruct(part.shape, bf16),
            jax.ShapeDtypeStruct((*part.shape[:2], part.shape[2] - spare), bf16),
            *[jax.ShapeDtypeStruct((line,) + small.shape, bf16) for small in smalls],
        ],
        in_specs=[INSIDE] + [ANY] * few,
        out_specs=[ANY, INSIDE] + [ANY] * few,
        scratch_shapes=[pltpu.VMEM(part.shape, bf16)] * 3
        + [dma((sub + few,))]
        + [dma((total,))] * 6
        + [dma((few, line - 1))] * 2,
        compiler_params=pltpu.CompilerParams(
            collective_id=number, has_side_effects=True, vmem_limit_bytes=50 * 2**20
        ),
        cost_estimate=pl.CostEstimate(flops=0, bytes_accessed=400 * 2**20, transcendentals=0),
    )(part, *smalls)


def columns(weight, count):
    return weight.reshape(weight.shape[0], count, -1).swapaxes(0, 1)


def by_rows(array):
    return with_layout_constraint(array, Layout((0, 1)))


def after(value, *earlier):
    zero = 0.0
    for array in earlier:
        corner = lax.slice(array, (0,) * array.ndim, (1,) * array.ndim).reshape(())
        zero = zero + jnp.minimum(jnp.abs(corner.astype(f32)), 0.0)
    return jax.tree.map(lambda part: part + zero.astype(part.dtype), value)


def relayed(value, earlier, rounds):
    corner = lax.slice(earlier, (0,) * earlier.ndim, (1,) * earlier.ndim).reshape(1, 1)
    token = jnp.broadcast_to(corner.astype(f32), (ROWS, LANES))
    devices = lax.axis_size("fsdp")
    for _ in range(rounds):
        token = lax.ppermute(token, "fsdp", [(i, i ^ 1) for i in range(devices)])
    return after(value, token)


def swapped(array):
    return array.swapaxes(0, 1)


def rates_of(rate_ref):
    return [jnp.broadcast_to(rate_ref[n : n + 1, :], (ROWS, LANES)) for n in range(STATE)]


def spread(sel_ref, picks, cuts):
    @pl.when(pl.program_id(1) == 0)
    def _():
        def turn(t, _):
            sel = sel_ref[t]
            for first, into in picks:
                for n in range(STATE):
                    lane = sel[:, first + n : first + n + 1]
                    into[t, n] = jnp.broadcast_to(lane, (ROWS, LANES))
            cuts[t] = jnp.broadcast_to(sel[:, 2 * STATE : 2 * STATE + 1], (ROWS, LANES))
            return 0

        lax.fori_loop(0, sel_ref.shape[0], turn, 0, unroll=4)


def carry_body(step_ref, conv_ref, sel_ref, rate_ref, out_ref, enters, cuts):
    rates = rates_of(rate_ref)
    spread(sel_ref, [(0, enters)], cuts)

    def turn(t, state):
        step = step_ref[t]
        push = step * conv_ref[t]
        fade = step + cuts[t]
        new = [
            jnp.exp(fade * rates[n]) * state[n] + enters[t, n] * push for n in range(STATE)
        ]
        return (*new, state[STATE] + fade)

    zero = jnp.zeros((ROWS, LANES), f32)
    state = lax.fori_loop(0, step_ref.shape[0], turn, (zero,) * (STATE + 1), unroll=8)
    for n in range(STATE + 1):
        out_ref[n] = state[n]


def scan_body(
    mine_ref,
    step_ref,
    conv_ref,
    sel_ref,
    rate_ref,
    carry_ref,
    out_ref,
    states_ref,
    enters,
    exits,
    cuts,
):
    rates = rates_of(rate_ref)
    spread(sel_ref, [(0, enters), (STATE, exits)], cuts)

    def join(j, state):
        return tuple(
            jnp.exp(rates[n] * carry_ref[j, STATE]) * state[n] + carry_ref[j, n]
            for n in range(STATE)
        )

    zero = jnp.zeros((ROWS, LANES), f32)
    state = lax.fori_loop(0, mine_ref[0], join, (zero,) * STATE)
    for n in range(STATE):
        states_ref[0, n] = state[n]

    def turn(t, state):
        step = step_ref[t]
        push = step * conv_ref[t]
        fade = step + cuts[t]
        new, total = [], zero
        for n in range(STATE):
            now = jnp.exp(fade * rates[n]) * state[n] + enters[t, n] * push
            states_ref[t + 1, n] = now
            total = total + exits[t, n] * now
            new.append(now)
        out_ref[t] = total
        return tuple(new)

    lax.fori_loop(0, step_ref.shape[0], turn, state, unroll=8)


def carry_back_body(step_ref, sel_ref, rate_ref, up_ref, out_ref, exits, cuts):
    rates = rates_of(rate_ref)
    spread(sel_ref, [(STATE, exits)], cuts)
    count = step_ref.shape[0]

    def turn(i, state):
        t = count - 1 - i
        up = up_ref[t]
        fade = step_ref[t] + cuts[t]
        return tuple(
            jnp.exp(fade * rates[n]) * (exits[t, n] * up + state[n]) for n in range(STATE)
        )

    zero = jnp.zeros((ROWS, LANES), f32)
    state = lax.fori_loop(0, count, turn, (zero,) * STATE, unroll=8)
    for n in range(STATE):
        out_ref[n] = state[n]


def scan_back_body(
    mine_ref,
    step_ref,
    conv_ref,
    sel_ref,
    rate_ref,
    up_ref,
    states_ref,
    span_ref,
    leave_ref,
    step_out,
    conv_out,
    sel_out,
    rate_out,
    enter_terms,
    exit_terms,
    enters,
    exits,
    cuts,
):
    rates = rates_of(rate_ref)
    spread(sel_ref, [(0, enters), (STATE, exits)], cuts)
    count = step_ref.shape[0]
    devices = span_ref.shape[0]
    zero = jnp.zeros((ROWS, LANES), f32)

    def join(i, state):
        j = devices - 1 - i
        return tuple(
            jnp.exp(rates[n] * span_ref[j]) * state[n] + leave_ref[j, n] for n in range(STATE)
        )

    state = lax.fori_loop(0, devices - 1 - mine_ref[0], join, (zero,) * STATE)
    state = state + (zero,) * STATE
    place = lax.broadcasted_iota(jnp.int32, (2 * LANES, LANES), 1)
    half = lax.broadcasted_iota(jnp.int32, (2 * LANES, LANES), 0) // LANES
    span = count // 2

    @pl.when(pl.program_id(1) == 0)
    def _():
        sel_out[...] = jnp.zeros_like(sel_out)

    for start in (span, 0):

        def turn(i, carried):
            t = start + span - 1 - i
            step, conv, up = step_ref[t], conv_ref[t], up_ref[t]
            push = step * conv
            fade = step + cuts[t]
            rows = pl.ds(pl.multiple_of((t - start) * ROWS, ROWS), ROWS)
            push_back, fade_back, new, rate_back = zero, zero, [], []
            for n in range(STATE):
                lanes = slice(n * LANES, (n + 1) * LANES)
                total = exits[t, n] * up + carried[n]
                exit_terms[rows, lanes] = up * states_ref[t + 1, n]
                enter_terms[rows, lanes] = total * push
                push_back = push_back + total * enters[t, n]
                earlier = jnp.exp(fade * rates[n]) * total
                slope = earlier * states_ref[t, n]
                fade_back = fade_back + slope * rates[n]
                new.append(earlier)
                rate_back.append(carried[STATE + n] + slope * step)
            step_out[t] = push_back * conv + fade_back
            conv_out[t] = push_back * step
            return (*new, *rate_back)

        state = lax.fori_loop(0, span, turn, state, unroll=4)
        total = jnp.zeros((span * ROWS, LANES), f32)
        for n in range(0, STATE, 2):
            lanes = slice(n * LANES, (n + 2) * LANES)
            pick = (place == n + half).astype(bf16)
            total = total + matmul(enter_terms[:, lanes].astype(bf16), pick)
            pick = (place == STATE + n + half).astype(bf16)
            total = total + matmul(exit_terms[:, lanes].astype(bf16), pick)
        sel_out[start : start + span] += total.reshape(span, ROWS, LANES)
    for n in range(STATE):
        rate_out[0, n : n + 1] = jnp.sum(state[STATE + n], axis=0, keepdims=True)


def lasting(time):
    return pl.CostEstimate(flops=0, bytes_accessed=int(time * 3.6e6), transcendentals=0)


def scan_specs(count, seqs, wide, devices):
    specs = dict(
        mine=pl.BlockSpec(memory_space=pltpu.SMEM),
        row=pl.BlockSpec((count, ROWS, LANES), lambda s, c: (0, s, c)),
        sel=pl.BlockSpec((count, ROWS, LANES), lambda s, c: (0, s, 0)),
        rate=pl.BlockSpec((STATE, LANES), lambda s, c: (0, c)),
        carry=pl.BlockSpec((STATE + 1, ROWS, LANES), lambda s, c: (0, s, c)),
        carries=pl.BlockSpec((devices, STATE + 1, ROWS, LANES), lambda s, c: (0, 0, s, c)),
        leave=pl.BlockSpec((STATE, ROWS, LANES), lambda s, c: (0, s, c)),
        leaves=pl.BlockSpec((devices, STATE, ROWS, LANES), lambda s, c: (0, 0, s, c)),
        span=pl.BlockSpec((devices, ROWS, LANES), lambda s, c: (0, s, c)),
        states=pl.BlockSpec((count + 1, STATE, ROWS, LANES), lambda s, c: (0, 0, s, c)),
        rates=pl.BlockSpec((1, STATE, LANES), lambda s, c: (s, 0, c)),
    )
    spreads = pltpu.VMEM((count, STATE, ROWS, LANES), f32)
    cuts = pltpu.VMEM((count, ROWS, LANES), f32)
    terms = pltpu.VMEM((count // 2 * ROWS, STATE * LANES), f32)
    specs["one"], specs["two"] = [spreads, cuts], [spreads, spreads, cuts]
    specs["four"] = [terms, terms, spreads, spreads, cuts]
    return specs, (seqs // ROWS, wide // LANES)


def scan_call(body, name, grid, ins, outs, shapes, scratch, work, args):
    return pl.pallas_call(
        body,
        name=name,
        grid=grid,
        in_specs=ins,
        out_specs=outs,
        out_shape=[jax.ShapeDtypeStruct(shape, f32) for shape in shapes],
        scratch_shapes=scratch,
        compiler_params=pltpu.CompilerParams(
            dimension_semantics=("arbitrary", "arbitrary"), vmem_limit_bytes=60 * 2**20
        ),
        cost_estimate=lasting(work),
    )(*args)


def shards(
    tokens,
    cotangent,
    doc_lengths,
    meta_tokens,
    norm_gain,
    w_query,
    w_keyval,
    w_attn_out,
    w_mixer_in,
    conv_taps,
    conv_bias,
    w_select,
    w_step,
    step_bias,
    log_rates,
    skip_gain,
    w_mixer_out,
    attn_gain,
    ssm_gain,
    ffn_norm_gain,
    w_gate_up,
    w_down,
):
    count = tokens.shape[1]
    width = tokens.shape[2]
    seqs = lax.axis_size("fsdp")
    ctx_index = lax.axis_index("ctx")
    ctx_count = lax.axis_size("ctx")
    inner = conv_bias.shape[0]
    wide = -(-inner // LANES) * LANES
    kv_width = KV_HEADS * HEAD
    groups = HEADS // KV_HEADS
    mine = jnp.reshape(ctx_index, (1,)).astype(jnp.int32)

    positions = ctx_index * count + jnp.arange(count, dtype=jnp.int32)
    last_pos = ctx_index * count + count - 1
    bounds = jnp.cumsum(doc_lengths[0])[:-1]
    docs = doc_number(positions, bounds)

    hidden_in = tokens[0].astype(f32)
    meta_rows = meta_tokens.shape[0]
    share = norm_gain.shape[0]
    extra_rows = -(-(meta_rows + 1) // 16) * 16
    few = doc_lengths[0]
    thin = jnp.concatenate(
        [
            norm_gain,
            attn_gain,
            ssm_gain,
            ffn_norm_gain,
            (few // 32).astype(bf16),
            (few % 32).astype(bf16),
        ]
    )
    extra = padded(
        jnp.concatenate([meta_tokens, padded(thin, 0, width)[None]], 0), 0, extra_rows
    )
    ff_cols = w_gate_up.shape[1] // (2 * seqs)
    conv_w = split_columns(w_mixer_in[:, : inner * seqs], inner, wide, seqs)
    gate_w = split_columns(w_mixer_in[:, inner * seqs :], inner, wide, seqs)
    everyone, conv_w = pair_gather(jnp.concatenate([tokens[0], extra], 0), 1, [conv_w])
    conv_w = conv_w.reshape(width, wide)
    tokens_all = everyone[:, :count].astype(f32).reshape(seqs * count, width)
    meta_f = meta_tokens.astype(f32)
    meta_all = everyone[:, count : count + meta_rows].astype(f32).reshape(META, width)
    thin = everyone[:, count + meta_rows]
    gains = thin[:, : 4 * share].reshape(seqs, 4, share).swapaxes(0, 1).astype(f32)
    gains = gains.reshape(4, width)
    gain_f, attn_norm_f, ssm_norm_f, ffn_gain_f = gains[0], gains[1], gains[2], gains[3]
    lengths = thin[:, 4 * share :].astype(jnp.int32)
    doc_count = doc_lengths.shape[1]
    lengths = 32 * lengths[:, :doc_count] + lengths[:, doc_count : 2 * doc_count]

    normed_all_f, _ = norm_rows(tokens_all, gain_f)
    normed = normed_all_f.astype(bf16)
    normed_own_f, scale_one = norm_rows(hidden_in, gain_f)
    normed_own = normed_own_f.astype(bf16)
    _, meta_scale = norm_rows(meta_f, gain_f)
    meta_normed = norm_rows(meta_all, gain_f)[0].astype(bf16)

    w_keyval, w_query = after((w_keyval, w_query), everyone)
    gate_w = exchanged(after(gate_w, everyone)).reshape(width, wide)
    keyval_w = lax.all_gather(w_keyval, "fsdp", axis=0, tiled=True)
    query_w = lax.all_gather(w_query, "fsdp", axis=0, tiled=True)
    ff_wide = -(-ff_cols // LANES) * LANES
    ff_w = exchanged(split_columns(w_gate_up, ff_cols, ff_wide, seqs))
    ff_w = ff_w.reshape(width, 2 * ff_wide)

    conv_in = swapped(matmul(normed, conv_w).astype(bf16).reshape(seqs, count, wide))
    gate_in = swapped(matmul(normed, gate_w).astype(bf16).reshape(seqs, count, wide))
    seq_bounds = jnp.cumsum(lengths, axis=1)[:, :-1]

    def numbers(places):
        return jnp.sum((places[:, None, None] >= seq_bounds[None]).astype(jnp.int32), axis=-1)

    seq_docs = numbers(positions)
    starts = (positions[:, None] == 0) | (seq_docs != numbers(positions - 1))
    taps_f = padded(conv_taps.astype(f32), 1, wide)
    rim = shifted(conv_in[count - (CONV - 1) :], "ctx", 1)
    extended = jnp.concatenate([rim, conv_in], 0).astype(f32)
    valid_rows = []
    for tap in range(CONV):
        earlier = positions - (CONV - 1 - tap)
        valid = (earlier[:, None] >= 0) & (numbers(earlier) == seq_docs)
        valid_rows.append(valid.astype(f32)[:, :, None])
    pre_conv = padded(conv_bias.astype(f32), 0, wide)[None, None, :]
    for tap in range(CONV):
        pre_conv = pre_conv + taps_f[tap] * extended[tap : tap + count] * valid_rows[tap]
    conv_sig = jax.nn.sigmoid(pre_conv)
    conv_out = (pre_conv * conv_sig).astype(bf16)
    conv_f = conv_out.astype(f32)
    conv_rows = conv_out.reshape(count * seqs, wide)
    select_w = padded(w_select, 0, wide)
    step_w = padded(w_step, 1, wide)
    selected = direct_sum(
        matmul(conv_rows, select_w).astype(bf16).reshape(seqs, count, -1), 3
    ).reshape(count * seqs, -1)
    step_low = selected[:, :DT_RANK]
    step_pre = matmul(step_low, step_w) + padded(step_bias.astype(f32), 0, wide)[None, :]
    step_pre = step_pre.reshape(count, seqs, wide)
    steps = jax.nn.softplus(step_pre)
    rates = -jnp.exp(padded(log_rates.astype(f32), 1, wide))
    sel = jnp.concatenate(
        [
            selected[:, DT_RANK:].astype(f32).reshape(count, seqs, 2 * STATE),
            jnp.where(starts, CUT, 0.0).astype(f32)[:, :, None],
        ],
        2,
    )
    sel = padded(sel, 2, LANES)
    spec, grid = scan_specs(count, seqs, wide, ctx_count)
    row_shape = (count, seqs, wide)
    (carry,) = scan_call(
        carry_body,
        "mamba_carry",
        grid,
        [spec["row"], spec["row"], spec["sel"], spec["rate"]],
        [spec["carry"]],
        [(STATE + 1, seqs, wide)],
        spec["one"],
        15,
        (steps, conv_f, sel, rates),
    )
    keyvals = matmul(normed_own, keyval_w).astype(bf16)
    carries, keyvals_all = direct_many(
        [carry.astype(bf16), keyvals], ["gather", "gather"], "ctx", 4
    )
    carries = carries.astype(f32)
    attn_out_w = lax.all_gather(w_attn_out, "fsdp", axis=0, tiled=True)
    out_back_all = gathered(cotangent[0], "fsdp").reshape(seqs * count, width)
    scanned, states = scan_call(
        scan_body,
        "mamba_scan",
        grid,
        [spec["mine"], spec["row"], spec["row"], spec["sel"], spec["rate"], spec["carries"]],
        [spec["row"], spec["states"]],
        [row_shape, (count + 1, STATE, seqs, wide)],
        spec["two"],
        26,
        (mine, steps, conv_f, sel, rates, carries),
    )
    skip_f = padded(skip_gain.astype(f32), 0, wide)
    ssm_out = scanned + skip_f * conv_f
    gate_f = gate_in.astype(f32)
    gate_sig = jax.nn.sigmoid(gate_f)
    gate_act = gate_f * gate_sig
    mixer_mid = swapped((ssm_out * gate_act).astype(bf16)).reshape(seqs * count, wide)
    mixer_out_w = padded(w_mixer_out, 0, wide)
    mixer_proj = pair_scatter(
        by_rows(matmul(mixer_mid, mixer_out_w).astype(bf16)).reshape(seqs, count, width), 6
    )
    queries = matmul(normed_own, query_w).astype(bf16)
    meta_kv = matmul(meta_normed, keyval_w).astype(bf16)
    query_heads = queries.reshape(count, KV_HEADS, groups, HEAD)
    piece = keyvals_all.reshape(ctx_count * count, 2 * kv_width)
    joined = jnp.concatenate([meta_kv, piece], 0)
    keys = joined[:, :kv_width].reshape(-1, KV_HEADS, HEAD)
    values = joined[:, kv_width:].reshape(-1, KV_HEADS, HEAD)
    key_pos = jnp.arange(piece.shape[0], dtype=jnp.int32)
    key_doc = doc_number(key_pos, bounds)
    shown = (key_pos[None, :] <= positions[:, None]) & (key_doc[None, :] == docs[:, None])
    shown = jnp.concatenate([jnp.full((count, META), True), shown], 1)
    scores = (
        jnp.einsum("qgha,kga->ghqk", query_heads, keys, preferred_element_type=f32) * 0.125
    )
    scores = jnp.where(shown[None, None], scores, NEG)
    top = jnp.max(scores, axis=-1, keepdims=True)
    weights = jnp.exp(scores - top)
    weights = weights / jnp.sum(weights, axis=-1, keepdims=True)
    attn_heads_f = jnp.einsum(
        "ghqk,kga->qgha", weights.astype(bf16), values, preferred_element_type=f32
    )
    attn_b = attn_heads_f.reshape(count, HEADS * HEAD).astype(bf16)
    attn_proj = matmul(attn_b, attn_out_w)
    attn_branch, attn_scale = norm_rows(attn_proj, attn_norm_f)

    ssm_branch, ssm_scale = norm_rows(mixer_proj, ssm_norm_f)
    middle = hidden_in + 0.5 * (attn_branch + ssm_branch)

    normed_two_f, scale_two = norm_rows(middle, ffn_gain_f)
    normed_two = pair_gather(normed_two_f.astype(bf16), 7).reshape(seqs * count, width)
    gate_up = matmul(normed_two, ff_w).astype(bf16)
    gate_v, up_v = gate_up[:, :ff_wide].astype(f32), gate_up[:, ff_wide:].astype(f32)
    ffn_sig = jax.nn.sigmoid(gate_v)
    hidden_ff = (gate_v * ffn_sig * up_v).astype(bf16)
    down_w = padded(w_down, 0, ff_wide)
    output = by_rows(matmul(hidden_ff, down_w).astype(bf16))

    output = exchanged(output.reshape(seqs, count, width)).astype(f32)
    block_out = (middle + jnp.sum(output, axis=0)).astype(bf16)[None]
    down_back = tmatmul(hidden_ff, out_back_all)[:ff_cols]
    hidden_back = matmul_t(out_back_all, down_w).astype(bf16).astype(f32)
    up_back = hidden_back * gate_v * ffn_sig
    gate_back = hidden_back * up_v * ffn_sig * (1.0 + gate_v * (1.0 - ffn_sig))
    gate_up_back = jnp.concatenate([gate_back.astype(bf16), up_back.astype(bf16)], 1)
    ff_w_back = tmatmul(normed_two, gate_up_back)
    normed_two_back = matmul_t(gate_up_back, ff_w).astype(bf16)
    down_back = down_back.astype(bf16)
    ff_w_back = ff_w_back.astype(bf16)
    ff_w_sum = lax.psum(ff_w_back, "ctx")
    normed_two_back = by_rows(relayed(normed_two_back, ff_w_back, 2))
    normed_two_back = pair_scatter(normed_two_back.reshape(seqs, count, width), 8)
    middle_norm_back, ffn_gain_back = norm_back(middle, scale_two, ffn_gain_f, normed_two_back)
    middle_back = cotangent[0].astype(f32) + middle_norm_back
    branch_back = 0.5 * middle_back
    ssm_proj_back, ssm_gain_back = norm_back(mixer_proj, ssm_scale, ssm_norm_f, branch_back)
    attn_proj_back, attn_gain_back = norm_back(attn_proj, attn_scale, attn_norm_f, branch_back)
    attn_own_back = attn_proj_back.astype(bf16)
    proj_back, attn_cols = pair_gather(
        jnp.concatenate([ssm_proj_back.astype(bf16), attn_own_back], 0),
        9,
        [columns(attn_b, seqs)],
    )
    attn_cols = attn_cols.reshape(seqs * count, -1)
    ssm_proj_back = proj_back[:, :count].reshape(seqs * count, width)
    attn_proj_back = proj_back[:, count:].reshape(seqs * count, width)

    mixer_out_back = tmatmul(mixer_mid, ssm_proj_back)[:inner].astype(bf16)
    attn_out_back = tmatmul(attn_cols, attn_proj_back).astype(bf16)
    mid_back = matmul_t(ssm_proj_back, mixer_out_w).astype(bf16).reshape(seqs, count, wide)
    mid_back = swapped(mid_back).astype(f32)
    ssm_back = mid_back * gate_act
    gate_in_back = mid_back * ssm_out * gate_sig * (1.0 + gate_f * (1.0 - gate_sig))
    skip_back = jnp.sum(ssm_back * conv_f, axis=(0, 1))
    (leave,) = scan_call(
        carry_back_body,
        "mamba_carry_back",
        grid,
        [spec["row"], spec["sel"], spec["rate"], spec["row"]],
        [spec["leave"]],
        [(STATE, seqs, wide)],
        spec["one"],
        15,
        (steps, sel, rates, ssm_back),
    )
    heads_back = matmul_t(attn_own_back, attn_out_w).astype(bf16)
    heads_back = heads_back.reshape(count, KV_HEADS, groups, HEAD)
    delta = jnp.sum(heads_back.astype(f32) * attn_heads_f, axis=-1)
    delta = delta.transpose(1, 2, 0)[..., None]
    weights_back = jnp.einsum("qgha,kga->ghqk", heads_back, values, preferred_element_type=f32)
    scores_back = (weights * (weights_back - delta)).astype(bf16)
    query_back = (
        jnp.einsum("ghqk,kga->qgha", scores_back, keys, preferred_element_type=f32) * 0.125
    )
    keys_back = (
        jnp.einsum("ghqk,qgha->kga", scores_back, query_heads, preferred_element_type=f32) * 0.125
    )
    values_back = jnp.einsum(
        "ghqk,qgha->kga", weights.astype(bf16), heads_back, preferred_element_type=f32
    )
    kv_back = jnp.concatenate(
        [keys_back.reshape(-1, kv_width), values_back.reshape(-1, kv_width)], 1
    )
    buffer = kv_back[META:].astype(bf16).reshape(ctx_count, count, 2 * kv_width)
    meta_kv_own = kv_back[:META].astype(bf16)
    query_back = query_back.reshape(count, HEADS * HEAD).astype(bf16)
    (leaves,) = direct_many([leave.astype(bf16)], ["gather"], "ctx", 5)
    owned = lax.all_to_all(buffer, "ctx", 0, 0)
    owned = jnp.sum(owned.astype(f32), axis=0).astype(bf16)
    kv_own = owned
    attn_normed_back = matmul_t(query_back, query_w) + matmul_t(kv_own, keyval_w)
    meta_normed_back = matmul_t(meta_kv_own, keyval_w)
    qkv_back, meta_kv_back = direct_many(
        [
            jnp.concatenate([columns(query_back, seqs), columns(kv_own, seqs)], 2),
            columns(meta_kv_own, seqs),
        ],
        ["swap"] * 2,
        "fsdp",
        12,
    )
    qkv_back = qkv_back.reshape(seqs * count, -1)
    meta_kv_back = jnp.sum(meta_kv_back.astype(f32), axis=0).astype(bf16)
    second = after((down_back, mixer_out_back, attn_out_back), ff_w_sum, qkv_back)
    token = relayed(jnp.zeros((ROWS, LANES), f32), after(second[0], *second[1:]), 2)
    second = lax.psum(second, "ctx")
    down_back, mixer_out_back, attn_out_back = [part.astype(f32) for part in second]
    leaves = after(leaves.astype(f32), token)
    steps_back, conv_back, sel_back, rates_back = scan_call(
        scan_back_body,
        "mamba_scan_back",
        grid,
        [
            spec["mine"],
            spec["row"],
            spec["row"],
            spec["sel"],
            spec["rate"],
            spec["row"],
            spec["states"],
            spec["span"],
            spec["leaves"],
        ],
        [spec["row"], spec["row"], spec["sel"], spec["rates"]],
        [row_shape, row_shape, (count, seqs, LANES), (seqs // ROWS, STATE, wide)],
        spec["four"],
        47,
        (mine, steps, conv_f, sel, rates, ssm_back, states, carries[:, STATE], leaves),
    )
    rates_log_back = jnp.sum(rates_back, axis=0) * rates
    step_pre_back = steps_back * jax.nn.sigmoid(step_pre)
    step_shift_back = jnp.sum(step_pre_back, axis=(0, 1))
    step_pre_back = step_pre_back.astype(bf16).reshape(count * seqs, wide)
    step_w_back = tmatmul(step_low, step_pre_back)
    selected_back = jnp.concatenate(
        [
            matmul_t(step_pre_back, step_w),
            sel_back[:, :, : 2 * STATE].reshape(count * seqs, 2 * STATE),
        ],
        1,
    ).astype(bf16)
    selected_back = direct_sum(selected_back.reshape(seqs, count, -1), 10)
    selected_back = selected_back.reshape(count * seqs, -1)
    select_w_back = tmatmul(selected_back, conv_rows)[:, :inner]
    conv_back = (
        conv_back
        + skip_f * ssm_back
        + matmul_t(selected_back, select_w).reshape(count, seqs, wide)
    )
    pre_back = conv_back * conv_sig * (1.0 + pre_conv * (1.0 - conv_sig))
    taps_bias_back = jnp.sum(pre_back, axis=(0, 1))
    tap_rows = []
    extended_back = jnp.zeros((count + CONV - 1, seqs, wide), f32)
    for tap in range(CONV):
        masked_back = pre_back * valid_rows[tap]
        tap_rows.append(jnp.sum(masked_back * extended[tap : tap + count], axis=(0, 1)))
        extended_back = extended_back + jnp.pad(
            taps_f[tap] * masked_back, ((tap, CONV - 1 - tap), (0, 0), (0, 0))
        )
    rim_back = shifted(extended_back[: CONV - 1].astype(bf16), "ctx", -1).astype(f32)
    conv_in_back = extended_back[CONV - 1 :] + jnp.pad(
        rim_back, ((count - (CONV - 1), 0), (0, 0), (0, 0))
    )
    conv_in_back = swapped(conv_in_back.astype(bf16)).reshape(seqs * count, wide)
    gate_in_back = swapped(gate_in_back.astype(bf16)).reshape(seqs * count, wide)

    thin = jnp.concatenate(
        [
            tap_rows[0][None],
            tap_rows[1][None],
            tap_rows[2][None],
            tap_rows[3][None],
            taps_bias_back[None],
            step_shift_back[None],
            skip_back[None],
            rates_log_back,
            step_w_back,
        ],
        0,
    )[:, :inner]
    q_cols = w_query.shape[1] // seqs
    in_cols = 2 * inner + qkv_back.shape[1]
    thin_rows = thin.shape[0]
    few_rows = -(-(thin_rows + select_w_back.shape[0]) // LANES) * LANES
    share_cols = few_rows // (width // inner)
    in_wide = -(-(in_cols + share_cols) // LANES) * LANES
    in_back = padded(
        jnp.concatenate([conv_in_back[:, :inner], gate_in_back[:, :inner], qkv_back], 1),
        1,
        in_wide,
    )
    few = padded(jnp.concatenate([thin, select_w_back], 0), 0, few_rows).T
    few = few.reshape(inner, width // inner, share_cols).swapaxes(0, 1).reshape(width, share_cols)
    beside = jnp.concatenate([tmatmul(meta_normed, meta_kv_back), few], 1)
    in_w_back = tmatmul(normed, in_back) + jnp.pad(
        beside, ((0, 0), (2 * inner + q_cols, in_wide - in_cols - share_cols))
    )
    in_w_back = in_w_back.astype(bf16)
    part = by_rows(matmul_t(conv_in_back, conv_w) + matmul_t(gate_in_back, gate_w))
    tokens_scale = lax.rsqrt(jnp.mean(tokens_all * tokens_all, axis=-1, keepdims=True) + EPS)
    meta_all_scale = lax.rsqrt(jnp.mean(meta_all * meta_all, axis=-1, keepdims=True) + EPS)
    gain_back = (
        jnp.sum(part * tokens_all * tokens_scale, axis=0)
        + jnp.sum(attn_normed_back * hidden_in * scale_one, axis=0)
        + jnp.sum(meta_normed_back * meta_all * meta_all_scale, axis=0)
    )
    gains_back = jnp.stack([gain_back, attn_gain_back, ssm_gain_back, ffn_gain_back])
    gains_back = gains_back.astype(bf16).reshape(4, seqs, share).swapaxes(0, 1)
    tail = jnp.concatenate(
        [
            meta_normed_back.astype(bf16).reshape(seqs, meta_rows, width),
            padded(gains_back.reshape(seqs, 1, 4 * share), 2, width),
        ],
        1,
    )
    totals = pair_scatter(
        jnp.concatenate(
            [
                part.astype(bf16).reshape(seqs, count, width),
                padded(tail, 1, extra_rows),
            ],
            1,
        ),
        11,
    )
    input_norm_back, _ = norm_back(
        hidden_in, scale_one, gain_f, totals[:count] + attn_normed_back
    )
    first = count
    meta_back, _ = norm_back(meta_f, meta_scale, gain_f, totals[first : first + meta_rows])
    gains_back = totals[first + meta_rows, : 4 * share]
    grad_tokens = (middle_back + input_norm_back)[None]

    small = jnp.concatenate([meta_back, padded(gains_back, 0, width)[None]], 0)
    small = padded(small.astype(bf16), 0, extra_rows)
    spare = in_cols // LANES * LANES
    in_w_back, few, small = finish(
        in_w_back.reshape(seqs, share, in_wide), [small], spare, 13
    )
    few = few.reshape(width, in_wide - spare)[:, in_cols - spare : in_cols - spare + share_cols]
    few = few.reshape(width // inner, inner, share_cols).swapaxes(0, 1).reshape(inner, few_rows)
    few = few.astype(f32)
    select_w_back = few[:, thin_rows : thin_rows + select_w_back.shape[0]]
    thin = few[:, :thin_rows].T
    small = jnp.sum(small.astype(f32), axis=0)
    meta_back = small[:meta_rows]
    gains = small[meta_rows, : 4 * share].reshape(4, share)

    (grad_gate_up,) = join_columns(
        exchanged(ff_w_sum.reshape(seqs, share, 2 * ff_wide)),
        [[(0, ff_cols), (ff_wide, ff_cols)]],
    )
    first = 2 * inner
    grad_mixer_in, grad_query, grad_keyval = join_columns(
        in_w_back,
        [
            [(0, inner), (inner, inner)],
            [(first, q_cols)],
            [(first + q_cols, in_cols - first - q_cols)],
        ],
    )
    return (
        block_out,
        grad_tokens,
        meta_back,
        gains[0],
        grad_query,
        grad_keyval,
        attn_out_back,
        grad_mixer_in,
        thin[:CONV],
        thin[CONV],
        select_w_back,
        thin[CONV + 3 + STATE : CONV + 3 + STATE + DT_RANK],
        thin[CONV + 1],
        thin[CONV + 3 : CONV + 3 + STATE],
        thin[CONV + 2],
        mixer_out_back,
        gains[1],
        gains[2],
        gains[3],
        grad_gate_up,
        down_back,
    )


def solution(mesh):
    rows, cols, one = P("fsdp", None), P(None, "fsdp"), P("fsdp")
    split = P("fsdp", "ctx", None)
    in_specs = (
        split,
        split,
        rows,
        rows,
        one,
        rows,
        rows,
        rows,
        rows,
        cols,
        one,
        rows,
        cols,
        one,
        cols,
        one,
        rows,
        one,
        one,
        one,
        rows,
        rows,
    )
    out_specs = (
        split,
        split,
        rows,
        one,
        rows,
        rows,
        rows,
        rows,
        cols,
        one,
        rows,
        cols,
        one,
        cols,
        one,
        rows,
        one,
        one,
        one,
        rows,
        rows,
    )
    return jax.shard_map(shards, mesh=mesh, in_specs=in_specs, out_specs=out_specs, check_vma=False)
```

```python
import jax
import jax.numpy as jnp
from jax import lax
from jax.experimental import pallas as pl
from jax.experimental.layout import Layout, with_layout_constraint
from jax.experimental.pallas import tpu as pltpu
from jax.sharding import PartitionSpec as P

HEADS = 25
KV_HEADS = 5
HEAD = 64
META = 128
STATE = 16
CONV = 4
DT_RANK = 100

EPS = 1e-05
NEG = -1e30
CUT = 1e30
LANES = 128
ROWS = 8
f32 = jnp.float32
bf16 = jnp.bfloat16


def matmul(left, right):
    return jnp.dot(left, right, preferred_element_type=f32)


def tmatmul(left, right):
    return lax.dot_general(left, right, (((0,), (0,)), ((), ())), preferred_element_type=f32)


def matmul_t(left, right):
    return lax.dot_general(left, right, (((1,), (1,)), ((), ())), preferred_element_type=f32)


def norm_rows(value, gain):
    scale = lax.rsqrt(jnp.mean(value * value, axis=-1, keepdims=True) + EPS)
    return (value * scale * gain, scale)


def norm_back(value, scale, gain, upstream):
    tilted = upstream * gain
    mixing = jnp.mean(tilted * value, axis=-1, keepdims=True)
    return (
        scale * tilted - value * scale * scale * scale * mixing,
        jnp.sum(upstream * value * scale, axis=0),
    )


def doc_number(positions, bounds):
    return jnp.sum((positions[:, None] >= bounds[None, :]).astype(jnp.int32), axis=1)


def padded(array, axis, size):
    widths = [(0, 0)] * array.ndim
    widths[axis] = (0, size - array.shape[axis])
    return jnp.pad(array, widths)


def shifted(block, axis, distance):
    devices = range(lax.axis_size(axis))
    route = [(i - distance, i) for i in devices if i - distance in devices]
    return lax.ppermute(block, axis, route)


def gathered(array, axis):
    return lax.all_gather(array, axis, axis=0)


def exchanged(array):
    return lax.all_to_all(array, "fsdp", 0, 0)


def scattered(array):
    return lax.psum_scatter(array.astype(bf16), "fsdp", scatter_dimension=0, tiled=False).astype(
        f32
    )


AT = pl.DeviceIdType.MESH
ANY = pl.BlockSpec(memory_space=pl.ANY)
INSIDE = pl.BlockSpec(memory_space=pltpu.VMEM)

def greet(axis, peers):
    barrier = pltpu.get_barrier_semaphore()
    for peer in peers:
        pl.semaphore_signal(barrier, inc=1, device_id={axis: peer}, device_id_type=AT)
    pl.semaphore_wait(barrier, len(peers))

def sender(axis, src, dst, send, recv, peer):
    return pltpu.make_async_remote_copy(src_ref=src, dst_ref=dst, send_sem=send, recv_sem=recv, device_id={axis: peer}, device_id_type=AT)

def comm_call(body, name, number, ins, shape, out_spec, scratch, time=25):
    return pl.pallas_call(body, name=name, out_shape=shape, in_specs=[spec for spec, _ in ins], out_specs=out_spec, scratch_shapes=scratch,
        cost_estimate=lasting(time), compiler_params=pltpu.CompilerParams(collective_id=number, has_side_effects=True, vmem_limit_bytes=40*2**20))(*[array for _, array in ins])

def pair_gather(array, number, swaps=()):
    devices = lax.axis_size("fsdp")
    pairs = devices // 2
    many = len(swaps)

    def body(*refs):
        mine, moved = refs[0], refs[1 : many + 1]
        out, landed = refs[many + 1], refs[many + 2 : 2 * many + 2]
        own, sent, got, passed, taken, moved_sent, moved_got = refs[2 * many + 2 :]
        me = lax.axis_index("fsdp")
        pair, core = me // 2, lax.rem(me, 2)
        mate = me + 1 - 2 * core
        peers = [2 * lax.rem(pair + k, pairs) + core for k in range(1, pairs)]
        others = [lax.rem(me + k, devices) for k in range(1, devices)]
        greet("fsdp", others if many else [mate, *peers])
        first = [
            sender("fsdp", mine, out.at[me], sent.at[k], got.at[k], peer)
            for k, peer in enumerate([mate, *peers])
        ]
        for copy in first[1:]:
            copy.start()
        first[0].start()
        extra = [
            sender(
                "fsdp",
                src.at[peer],
                dst.at[me],
                moved_sent.at[m, k],
                moved_got.at[m, k],
                peer,
            )
            for m, (src, dst) in enumerate(zip(moved, landed))
            for k, peer in enumerate(others)
        ]
        for copy in extra:
            copy.start()
        local = [pltpu.make_async_copy(mine, out.at[me], own.at[0])]
        for m, (src, dst) in enumerate(zip(moved, landed)):
            local.append(pltpu.make_async_copy(src.at[me], dst.at[me], own.at[m + 1]))
        for copy in local:
            copy.start()
        second = []
        for k in range(1, pairs):
            slot = 2 * lax.rem(pair + pairs - k, pairs) + core
            first[k].wait_recv()
            copy = sender(
                "fsdp", out.at[slot], out.at[slot], passed.at[k - 1], taken.at[k - 1], mate
            )
            copy.start()
            second.append(copy)
        first[0].wait_recv()
        for copy in first:
            copy.wait_send()
        for copy in second + extra + local:
            copy.wait()

    dma = pltpu.SemaphoreType.DMA
    shapes = [jax.ShapeDtypeStruct((devices,) + array.shape, array.dtype)]
    shapes += [jax.ShapeDtypeStruct(swap.shape, swap.dtype) for swap in swaps]
    result = comm_call(
        body,
        "pair_gather",
        number,
        [(ANY, array)] + [(ANY, swap) for swap in swaps],
        shapes,
        [ANY] * (many + 1),
        [dma((many + 1,)), dma((pairs,)), dma((pairs,)), dma((pairs - 1,)), dma((pairs - 1,))]
        + [dma((max(many, 1), devices - 1))] * 2,
    )
    return result if many else result[0]


def direct_many(arrays, modes, axis, number):
    devices = lax.axis_size(axis)
    many = len(arrays)

    def body(*refs):
        mine, out, (own, sent, got) = refs[:many], refs[many : 2 * many], refs[2 * many :]
        me = lax.axis_index(axis)
        peers = [lax.rem(me + k, devices) for k in range(1, devices)]
        greet(axis, peers)
        copies = []
        for m, (src, dst, mode) in enumerate(zip(mine, out, modes)):
            for k, peer in enumerate(peers):
                part = src if mode == "gather" else src.at[peer]
                copies.append(sender(axis, part, dst.at[me], sent.at[m, k], got.at[m, k], peer))
        for copy in copies:
            copy.start()
        for m, (src, dst, mode) in enumerate(zip(mine, out, modes)):
            part = src if mode == "gather" else src.at[me]
            copies.append(pltpu.make_async_copy(part, dst.at[me], own.at[m]))
            copies[-1].start()
        for copy in copies:
            copy.wait()

    dma = pltpu.SemaphoreType.DMA
    shapes = [
        jax.ShapeDtypeStruct(
            (devices,) + array.shape if mode == "gather" else array.shape, array.dtype
        )
        for array, mode in zip(arrays, modes)
    ]
    return comm_call(
        body,
        "direct_many",
        number,
        [(ANY, array) for array in arrays],
        shapes,
        [ANY] * many,
        [dma((many,)), dma((many, devices - 1)), dma((many, devices - 1))],
    )


def split_columns(weight, cols, wide, seqs):
    rows = weight.shape[0]
    kinds = weight.shape[1] // (cols * seqs)

    def body(mine, out):
        for m in range(kinds):
            for f in range(seqs):
                first = (m * seqs + f) * cols
                out[f, :, m * wide : m * wide + cols] = mine[:, first : first + cols]
                if wide > cols:
                    blank = jnp.zeros((rows, wide - cols), bf16)
                    out[f, :, m * wide + cols : (m + 1) * wide] = blank

    return pl.pallas_call(
        body,
        name="split_columns",
        out_shape=jax.ShapeDtypeStruct((seqs, rows, kinds * wide), bf16),
        in_specs=[INSIDE],
        out_specs=INSIDE,
        compiler_params=pltpu.CompilerParams(vmem_limit_bytes=40 * 2**20),
    )(weight)


def join_columns(array, kinds):
    seqs, rows, _ = array.shape

    def body(mine, *outs):
        for out, parts in zip(outs, kinds):
            for m, (first, cols) in enumerate(parts):
                for f in range(seqs):
                    place = (m * seqs + f) * cols
                    out[:, place : place + cols] = mine[f, :, first : first + cols].astype(f32)

    return pl.pallas_call(
        body,
        name="join_columns",
        out_shape=[
            jax.ShapeDtypeStruct((rows, seqs * sum(cols for _, cols in parts)), f32)
            for parts in kinds
        ],
        in_specs=[INSIDE],
        out_specs=[INSIDE] * len(kinds),
        compiler_params=pltpu.CompilerParams(vmem_limit_bytes=48 * 2**20),
    )(array)


def pair_scatter(array, number):
    devices = array.shape[0]; pairs = devices // 2; shape = array.shape[1:]
    def body(mine, out, near, summed, far, sent, got, passed, taken):
        me = lax.axis_index("fsdp"); pair = me // 2; core = lax.rem(me, 2); mate = me + 1 - 2 * core
        places = [lax.rem(pair + k, pairs) for k in range(1, pairs + 1)]
        greet("fsdp", [mate, *[2 * q + core for q in places[:-1]]])
        first = [sender("fsdp", mine.at[2 * q + 1 - core], near.at[k], sent.at[k], got.at[k], mate) for k, q in enumerate(places)]
        for copy in first: copy.start()
        second = []
        for k, q in enumerate(places):
            first[k].wait_recv()
            total = mine[2 * q + core].astype(f32) + near[k].astype(f32)
            if k < pairs - 1:
                summed[k] = total.astype(bf16)
                copy = sender("fsdp", summed.at[k], far.at[k], passed.at[k], taken.at[k], 2 * q + core)
                copy.start(); second.append(copy)
            else:
                out[...] = total
        for copy in second:
            copy.wait_recv()
        total = out[...]
        for k in range(pairs - 1): total = total + far[k].astype(f32)
        out[...] = total
        for copy in first: copy.wait_send()
        for copy in second: copy.wait_send()
    return comm_call(body, "pair_scatter", number, [(INSIDE, array)], jax.ShapeDtypeStruct(shape, f32), INSIDE,
        [pltpu.VMEM((pairs,) + shape, bf16), pltpu.VMEM((pairs-1,) + shape, bf16), pltpu.VMEM((pairs-1,) + shape, bf16),
         pltpu.SemaphoreType.DMA((pairs,)), pltpu.SemaphoreType.DMA((pairs,)), pltpu.SemaphoreType.DMA((pairs-1,)), pltpu.SemaphoreType.DMA((pairs-1,))])

def direct_sum(array, number):
    devices = array.shape[0]; shape = array.shape[1:]
    def body(mine, out, near, sent, got, passed, taken):
        me = lax.axis_index("fsdp")
        peers = [lax.rem(me + k, devices) for k in range(1, devices)]
        greet("fsdp", peers)
        first = [sender("fsdp", mine.at[peer], near.at[k], sent.at[k], got.at[k], peer) for k, peer in enumerate(peers)]
        for copy in first: copy.start()
        total = mine[me].astype(f32)
        for k in range(devices - 1):
            first[k].wait_recv()
            total = total + near[k].astype(f32)
        out[me] = total.astype(bf16)
        second = [sender("fsdp", out.at[me], out.at[me], passed.at[k], taken.at[k], peer) for k, peer in enumerate(peers)]
        for copy in second: copy.start()
        for copy in second: copy.wait()
        for copy in first: copy.wait_send()
    return comm_call(body, "direct_sum", number, [(INSIDE, array)], jax.ShapeDtypeStruct(array.shape, bf16), INSIDE,
        [pltpu.VMEM((devices-1,) + shape, bf16)] + [pltpu.SemaphoreType.DMA((devices-1,))] * 4)

def finish(part, smalls, spare, number):
    devices = lax.axis_size("fsdp")
    line = lax.axis_size("ctx")
    total = part.shape[0]
    half, sub = total // 2, total // devices

    few = len(smalls)

    def body(part, *refs):
        small, (part_out, spare_out, *small_out) = refs[:few], refs[few : 2 * few + 2]
        near, mid, done, own, sent, got, back_sent, back_got, out_sent, out_got, *rest = refs[2 * few + 2 :]
        small_sent, small_got = rest
        me, place = lax.axis_index("fsdp"), lax.axis_index("ctx")
        barrier = pltpu.get_barrier_semaphore()
        peers = [lax.rem(me + k, devices) for k in range(1, devices)]
        for peer in peers:
            pl.semaphore_signal(barrier, inc=1, device_id={"fsdp": peer}, device_id_type=AT)
        mates = [lax.rem(place + k, line) for k in range(1, line)]
        for mate in mates:
            pl.semaphore_signal(barrier, inc=1, device_id={"ctx": mate}, device_id_type=AT)
        pl.semaphore_wait(barrier, devices + line - 2)
        extra = []
        for m, (src, dst) in enumerate(zip(small, small_out)):
            for k, mate in enumerate(mates):
                sems = small_sent.at[m, k], small_got.at[m, k]
                extra.append(sender("ctx", src, dst.at[place], *sems, mate))
            extra.append(pltpu.make_async_copy(src, dst.at[place], own.at[sub + m]))
        for copy in extra:
            copy.start()

        def moves(way, i):
            slot = i + way * half
            onward = place + 1 - 2 * way
            back = place - 1 + 2 * way
            begin = sender("ctx", part.at[slot], near.at[slot], sent.at[slot], got.at[slot], onward)
            relay = sender("ctx", mid.at[slot], near.at[slot], sent.at[slot], got.at[slot], onward)
            spread = sender("ctx", done.at[slot], done.at[slot], back_sent.at[slot], back_got.at[slot], back)
            return slot, begin, relay, spread

        def ends(way):
            return (0, line - 1) if way == 0 else (line - 1, 0)

        def turn(s, _):
            for way in range(2):
                first, last = ends(way)
                hops = place if way == 0 else line - 1 - place

                def inward(i):
                    slot, begin, relay, spread = moves(way, i)

                    @pl.when(place == first)
                    def _():
                        begin.start()

                    @pl.when(place != first)
                    def _():
                        relay.wait_recv()

                        @pl.when(place != last)
                        def _():
                            mid[slot] = (part[slot].astype(f32) + near[slot].astype(f32)).astype(bf16)
                            relay.start()

                        @pl.when(place == last)
                        def _():
                            done[slot] = (part[slot].astype(f32) + near[slot].astype(f32)).astype(bf16)

                def outward(i):
                    slot, begin, relay, spread = moves(way, i)

                    @pl.when(place != last)
                    def _():
                        spread.wait_recv()

                    @pl.when(place != first)
                    def _():
                        spread.start()

                    owner, rank = slot // sub, lax.rem(slot, sub)
                    here = me * sub + rank

                    @pl.when(me != owner)
                    def _():
                        sender("fsdp", done.at[slot], part_out.at[here], out_sent.at[slot], out_got.at[here], owner).start()

                    @pl.when(me == owner)
                    def _():
                        pltpu.make_async_copy(done.at[slot], part_out.at[slot], own.at[rank]).start()

                i = s - hops
                pl.when((i >= 0) & (i < half))(lambda: inward(i))
                k = s - (2 * (line - 1) - hops)
                pl.when((k >= 0) & (k < half))(lambda: outward(k))
            return 0

        lax.fori_loop(0, half + 2 * (line - 1), turn, 0)

        def drain(i, _):
            for way in range(2):
                first, last = ends(way)
                slot, begin, relay, spread = moves(way, i)

                @pl.when(place == first)
                def _():
                    begin.wait_send()

                @pl.when((place != first) & (place != last))
                def _():
                    relay.wait_send()

                @pl.when(place != first)
                def _():
                    spread.wait_send()

                owner, rank = slot // sub, lax.rem(slot, sub)
                copy = sender("fsdp", done.at[slot], part_out.at[slot], out_sent.at[slot], out_got.at[slot], owner)

                @pl.when(me != owner)
                def _():
                    copy.wait_send()
                    copy.wait_recv()

                @pl.when(me == owner)
                def _():
                    pltpu.make_async_copy(done.at[slot], part_out.at[slot], own.at[rank]).wait()
            return 0

        lax.fori_loop(0, half, drain, 0)
        spare_out[...] = done[:, :, spare:]
        for copy in extra:
            copy.wait()

    dma = pltpu.SemaphoreType.DMA
    return pl.pallas_call(
        body,
        name="finish",
        out_shape=[
            jax.ShapeDtypeStruct(part.shape, bf16),
            jax.ShapeDtypeStruct((*part.shape[:2], part.shape[2] - spare), bf16),
            *[jax.ShapeDtypeStruct((line,) + small.shape, bf16) for small in smalls],
        ],
        in_specs=[INSIDE] + [ANY] * few,
        out_specs=[ANY, INSIDE] + [ANY] * few,
        scratch_shapes=[pltpu.VMEM(part.shape, bf16)] * 3
        + [dma((sub + few,))]
        + [dma((total,))] * 6
        + [dma((few, line - 1))] * 2,
        compiler_params=pltpu.CompilerParams(
            collective_id=number, has_side_effects=True, vmem_limit_bytes=50 * 2**20
        ),
        cost_estimate=pl.CostEstimate(flops=0, bytes_accessed=400 * 2**20, transcendentals=0),
    )(part, *smalls)


def columns(weight, count):
    return weight.reshape(weight.shape[0], count, -1).swapaxes(0, 1)


def by_rows(array):
    return with_layout_constraint(array, Layout((0, 1)))


def after(value, *earlier):
    zero = 0.0
    for array in earlier:
        corner = lax.slice(array, (0,) * array.ndim, (1,) * array.ndim).reshape(())
        zero = zero + jnp.minimum(jnp.abs(corner.astype(f32)), 0.0)
    return jax.tree.map(lambda part: part + zero.astype(part.dtype), value)


def relayed(value, earlier, rounds):
    corner = lax.slice(earlier, (0,) * earlier.ndim, (1,) * earlier.ndim).reshape(1, 1)
    token = jnp.broadcast_to(corner.astype(f32), (ROWS, LANES))
    devices = lax.axis_size("fsdp")
    for _ in range(rounds):
        token = lax.ppermute(token, "fsdp", [(i, i ^ 1) for i in range(devices)])
    return after(value, token)


def swapped(array):
    return array.swapaxes(0, 1)


def rates_of(rate_ref):
    return [jnp.broadcast_to(rate_ref[n : n + 1, :], (ROWS, LANES)) for n in range(STATE)]


def spread(sel_ref, picks, cuts):
    @pl.when(pl.program_id(1) == 0)
    def _():
        def turn(t, _):
            sel = sel_ref[t]
            for first, into in picks:
                for n in range(STATE):
                    lane = sel[:, first + n : first + n + 1]
                    into[t, n] = jnp.broadcast_to(lane, (ROWS, LANES))
            cuts[t] = jnp.broadcast_to(sel[:, 2 * STATE : 2 * STATE + 1], (ROWS, LANES))
            return 0

        lax.fori_loop(0, sel_ref.shape[0], turn, 0, unroll=16)


def carry_body(step_ref, conv_ref, sel_ref, rate_ref, out_ref, enters, cuts):
    rates = rates_of(rate_ref)
    spread(sel_ref, [(0, enters)], cuts)

    def turn(t, state):
        step = step_ref[t]
        push = step * conv_ref[t]
        fade = step + cuts[t]
        new = [
            jnp.exp(fade * rates[n]) * state[n] + enters[t, n] * push for n in range(STATE)
        ]
        return (*new, state[STATE] + fade)

    zero = jnp.zeros((ROWS, LANES), f32)
    state = lax.fori_loop(0, step_ref.shape[0], turn, (zero,) * (STATE + 1), unroll=8)
    for n in range(STATE + 1):
        out_ref[n] = state[n]


def scan_body(
    mine_ref,
    step_ref,
    conv_ref,
    sel_ref,
    rate_ref,
    carry_ref,
    out_ref,
    states_ref,
    enters,
    exits,
    cuts,
):
    rates = rates_of(rate_ref)
    spread(sel_ref, [(0, enters), (STATE, exits)], cuts)

    def join(j, state):
        return tuple(
            jnp.exp(rates[n] * carry_ref[j, STATE]) * state[n] + carry_ref[j, n]
            for n in range(STATE)
        )

    zero = jnp.zeros((ROWS, LANES), f32)
    state = lax.fori_loop(0, mine_ref[0], join, (zero,) * STATE)
    for n in range(STATE):
        states_ref[0, n] = state[n]

    def turn(t, state):
        step = step_ref[t]
        push = step * conv_ref[t]
        fade = step + cuts[t]
        new, total = [], zero
        for n in range(STATE):
            now = jnp.exp(fade * rates[n]) * state[n] + enters[t, n] * push
            states_ref[t + 1, n] = now
            total = total + exits[t, n] * now
            new.append(now)
        out_ref[t] = total
        return tuple(new)

    lax.fori_loop(0, step_ref.shape[0], turn, state, unroll=8)


def carry_back_body(step_ref, sel_ref, rate_ref, up_ref, out_ref, exits, cuts):
    rates = rates_of(rate_ref)
    spread(sel_ref, [(STATE, exits)], cuts)
    count = step_ref.shape[0]

    def turn(i, state):
        t = count - 1 - i
        up = up_ref[t]
        fade = step_ref[t] + cuts[t]
        return tuple(
            jnp.exp(fade * rates[n]) * (exits[t, n] * up + state[n]) for n in range(STATE)
        )

    zero = jnp.zeros((ROWS, LANES), f32)
    state = lax.fori_loop(0, count, turn, (zero,) * STATE, unroll=8)
    for n in range(STATE):
        out_ref[n] = state[n]


def scan_back_body(
    mine_ref,
    step_ref,
    conv_ref,
    sel_ref,
    rate_ref,
    up_ref,
    states_ref,
    span_ref,
    leave_ref,
    step_out,
    conv_out,
    sel_out,
    rate_out,
    enter_terms,
    exit_terms,
    enters,
    exits,
    cuts,
):
    rates = rates_of(rate_ref)
    spread(sel_ref, [(0, enters), (STATE, exits)], cuts)
    count = step_ref.shape[0]
    devices = span_ref.shape[0]
    zero = jnp.zeros((ROWS, LANES), f32)

    def join(i, state):
        j = devices - 1 - i
        return tuple(
            jnp.exp(rates[n] * span_ref[j]) * state[n] + leave_ref[j, n] for n in range(STATE)
        )

    state = lax.fori_loop(0, devices - 1 - mine_ref[0], join, (zero,) * STATE)
    state = state + (zero,) * STATE
    place = lax.broadcasted_iota(jnp.int32, (2 * LANES, LANES), 1)
    half = lax.broadcasted_iota(jnp.int32, (2 * LANES, LANES), 0) // LANES
    span = count // 2

    @pl.when(pl.program_id(1) == 0)
    def _():
        sel_out[...] = jnp.zeros_like(sel_out)

    for start in (span, 0):

        def turn(i, carried):
            t = start + span - 1 - i
            step, conv, up = step_ref[t], conv_ref[t], up_ref[t]
            push = step * conv
            fade = step + cuts[t]
            rows = pl.ds(pl.multiple_of((t - start) * ROWS, ROWS), ROWS)
            push_back, fade_back, new, rate_back = zero, zero, [], []
            for n in range(STATE):
                lanes = slice(n * LANES, (n + 1) * LANES)
                total = exits[t, n] * up + carried[n]
                exit_terms[rows, lanes] = up * states_ref[t + 1, n]
                enter_terms[rows, lanes] = total * push
                push_back = push_back + total * enters[t, n]
                earlier = jnp.exp(fade * rates[n]) * total
                slope = earlier * states_ref[t, n]
                fade_back = fade_back + slope * rates[n]
                new.append(earlier)
                rate_back.append(carried[STATE + n] + slope * step)
            step_out[t] = push_back * conv + fade_back
            conv_out[t] = push_back * step
            return (*new, *rate_back)

        state = lax.fori_loop(0, span, turn, state, unroll=4)
        total = jnp.zeros((span * ROWS, LANES), f32)
        for n in range(0, STATE, 2):
            lanes = slice(n * LANES, (n + 2) * LANES)
            pick = (place == n + half).astype(bf16)
            total = total + matmul(enter_terms[:, lanes].astype(bf16), pick)
            pick = (place == STATE + n + half).astype(bf16)
            total = total + matmul(exit_terms[:, lanes].astype(bf16), pick)
        sel_out[start : start + span] += total.reshape(span, ROWS, LANES)
    for n in range(STATE):
        rate_out[0, n : n + 1] = jnp.sum(state[STATE + n], axis=0, keepdims=True)


def lasting(time):
    return pl.CostEstimate(flops=0, bytes_accessed=int(time * 3.6e6), transcendentals=0)


def scan_specs(count, seqs, wide, devices):
    specs = dict(
        mine=pl.BlockSpec(memory_space=pltpu.SMEM),
        row=pl.BlockSpec((count, ROWS, LANES), lambda s, c: (0, s, c)),
        sel=pl.BlockSpec((count, ROWS, LANES), lambda s, c: (0, s, 0)),
        rate=pl.BlockSpec((STATE, LANES), lambda s, c: (0, c)),
        carry=pl.BlockSpec((STATE + 1, ROWS, LANES), lambda s, c: (0, s, c)),
        carries=pl.BlockSpec((devices, STATE + 1, ROWS, LANES), lambda s, c: (0, 0, s, c)),
        leave=pl.BlockSpec((STATE, ROWS, LANES), lambda s, c: (0, s, c)),
        leaves=pl.BlockSpec((devices, STATE, ROWS, LANES), lambda s, c: (0, 0, s, c)),
        span=pl.BlockSpec((devices, ROWS, LANES), lambda s, c: (0, s, c)),
        states=pl.BlockSpec((count + 1, STATE, ROWS, LANES), lambda s, c: (0, 0, s, c)),
        rates=pl.BlockSpec((1, STATE, LANES), lambda s, c: (s, 0, c)),
    )
    spreads = pltpu.VMEM((count, STATE, ROWS, LANES), f32)
    cuts = pltpu.VMEM((count, ROWS, LANES), f32)
    terms = pltpu.VMEM((count // 2 * ROWS, STATE * LANES), f32)
    specs["one"], specs["two"] = [spreads, cuts], [spreads, spreads, cuts]
    specs["four"] = [terms, terms, spreads, spreads, cuts]
    return specs, (seqs // ROWS, wide // LANES)


def scan_call(body, name, grid, ins, outs, shapes, scratch, work, args):
    return pl.pallas_call(
        body,
        name=name,
        grid=grid,
        in_specs=ins,
        out_specs=outs,
        out_shape=[jax.ShapeDtypeStruct(shape, f32) for shape in shapes],
        scratch_shapes=scratch,
        compiler_params=pltpu.CompilerParams(
            dimension_semantics=("arbitrary", "arbitrary"), vmem_limit_bytes=60 * 2**20
        ),
        cost_estimate=lasting(work),
    )(*args)


def shards(
    tokens,
    cotangent,
    doc_lengths,
    meta_tokens,
    norm_gain,
    w_query,
    w_keyval,
    w_attn_out,
    w_mixer_in,
    conv_taps,
    conv_bias,
    w_select,
    w_step,
    step_bias,
    log_rates,
    skip_gain,
    w_mixer_out,
    attn_gain,
    ssm_gain,
    ffn_norm_gain,
    w_gate_up,
    w_down,
):
    count = tokens.shape[1]
    width = tokens.shape[2]
    seqs = lax.axis_size("fsdp")
    ctx_index = lax.axis_index("ctx")
    ctx_count = lax.axis_size("ctx")
    inner = conv_bias.shape[0]
    wide = -(-inner // LANES) * LANES
    kv_width = KV_HEADS * HEAD
    groups = HEADS // KV_HEADS
    mine = jnp.reshape(ctx_index, (1,)).astype(jnp.int32)

    positions = ctx_index * count + jnp.arange(count, dtype=jnp.int32)
    last_pos = ctx_index * count + count - 1
    bounds = jnp.cumsum(doc_lengths[0])[:-1]
    docs = doc_number(positions, bounds)

    hidden_in = tokens[0].astype(f32)
    meta_rows = meta_tokens.shape[0]
    share = norm_gain.shape[0]
    extra_rows = -(-(meta_rows + 1) // 16) * 16
    few = doc_lengths[0]
    thin = jnp.concatenate(
        [
            norm_gain,
            attn_gain,
            ssm_gain,
            ffn_norm_gain,
            (few // 32).astype(bf16),
            (few % 32).astype(bf16),
        ]
    )
    extra = padded(
        jnp.concatenate([meta_tokens, padded(thin, 0, width)[None]], 0), 0, extra_rows
    )
    ff_cols = w_gate_up.shape[1] // (2 * seqs)
    conv_w = split_columns(w_mixer_in[:, : inner * seqs], inner, wide, seqs)
    gate_w = split_columns(w_mixer_in[:, inner * seqs :], inner, wide, seqs)
    everyone, conv_w = pair_gather(jnp.concatenate([tokens[0], extra], 0), 1, [conv_w])
    conv_w = conv_w.reshape(width, wide)
    tokens_all = everyone[:, :count].astype(f32).reshape(seqs * count, width)
    meta_f = meta_tokens.astype(f32)
    meta_all = everyone[:, count : count + meta_rows].astype(f32).reshape(META, width)
    thin = everyone[:, count + meta_rows]
    gains = thin[:, : 4 * share].reshape(seqs, 4, share).swapaxes(0, 1).astype(f32)
    gains = gains.reshape(4, width)
    gain_f, attn_norm_f, ssm_norm_f, ffn_gain_f = gains[0], gains[1], gains[2], gains[3]
    lengths = thin[:, 4 * share :].astype(jnp.int32)
    doc_count = doc_lengths.shape[1]
    lengths = 32 * lengths[:, :doc_count] + lengths[:, doc_count : 2 * doc_count]

    normed_all_f, _ = norm_rows(tokens_all, gain_f)
    normed = normed_all_f.astype(bf16)
    normed_own_f, scale_one = norm_rows(hidden_in, gain_f)
    normed_own = normed_own_f.astype(bf16)
    _, meta_scale = norm_rows(meta_f, gain_f)
    meta_normed = norm_rows(meta_all, gain_f)[0].astype(bf16)

    w_keyval, w_query = after((w_keyval, w_query), everyone)
    gate_w = exchanged(after(gate_w, everyone)).reshape(width, wide)
    keyval_w = lax.all_gather(w_keyval, "fsdp", axis=0, tiled=True)
    query_w = lax.all_gather(w_query, "fsdp", axis=0, tiled=True)
    ff_wide = -(-ff_cols // LANES) * LANES
    ff_w = exchanged(split_columns(w_gate_up, ff_cols, ff_wide, seqs))
    ff_w = ff_w.reshape(width, 2 * ff_wide)

    conv_in = swapped(matmul(normed, conv_w).astype(bf16).reshape(seqs, count, wide))
    gate_in = swapped(matmul(normed, gate_w).astype(bf16).reshape(seqs, count, wide))
    seq_bounds = jnp.cumsum(lengths, axis=1)[:, :-1]

    def numbers(places):
        return jnp.sum((places[:, None, None] >= seq_bounds[None]).astype(jnp.int32), axis=-1)

    seq_docs = numbers(positions)
    starts = (positions[:, None] == 0) | (seq_docs != numbers(positions - 1))
    taps_f = padded(conv_taps.astype(f32), 1, wide)
    rim = shifted(conv_in[count - (CONV - 1) :], "ctx", 1)
    extended = jnp.concatenate([rim, conv_in], 0).astype(f32)
    valid_rows = []
    for tap in range(CONV):
        earlier = positions - (CONV - 1 - tap)
        valid = (earlier[:, None] >= 0) & (numbers(earlier) == seq_docs)
        valid_rows.append(valid.astype(f32)[:, :, None])
    pre_conv = padded(conv_bias.astype(f32), 0, wide)[None, None, :]
    for tap in range(CONV):
        pre_conv = pre_conv + taps_f[tap] * extended[tap : tap + count] * valid_rows[tap]
    conv_sig = jax.nn.sigmoid(pre_conv)
    conv_out = (pre_conv * conv_sig).astype(bf16)
    conv_f = conv_out.astype(f32)
    conv_rows = conv_out.reshape(count * seqs, wide)
    select_w = padded(w_select, 0, wide)
    step_w = padded(w_step, 1, wide)
    selected = direct_sum(
        matmul(conv_rows, select_w).astype(bf16).reshape(seqs, count, -1), 3
    ).reshape(count * seqs, -1)
    step_low = selected[:, :DT_RANK]
    step_pre = matmul(step_low, step_w) + padded(step_bias.astype(f32), 0, wide)[None, :]
    step_pre = step_pre.reshape(count, seqs, wide)
    steps = jax.nn.softplus(step_pre)
    rates = -jnp.exp(padded(log_rates.astype(f32), 1, wide))
    sel = jnp.concatenate(
        [
            selected[:, DT_RANK:].astype(f32).reshape(count, seqs, 2 * STATE),
            jnp.where(starts, CUT, 0.0).astype(f32)[:, :, None],
        ],
        2,
    )
    sel = padded(sel, 2, LANES)
    spec, grid = scan_specs(count, seqs, wide, ctx_count)
    row_shape = (count, seqs, wide)
    (carry,) = scan_call(
        carry_body,
        "mamba_carry",
        grid,
        [spec["row"], spec["row"], spec["sel"], spec["rate"]],
        [spec["carry"]],
        [(STATE + 1, seqs, wide)],
        spec["one"],
        15,
        (steps, conv_f, sel, rates),
    )
    keyvals = matmul(normed_own, keyval_w).astype(bf16)
    carries, keyvals_all = direct_many(
        [carry.astype(bf16), keyvals], ["gather", "gather"], "ctx", 4
    )
    carries = carries.astype(f32)
    attn_out_w = lax.all_gather(w_attn_out, "fsdp", axis=0, tiled=True)
    out_back_all = gathered(cotangent[0], "fsdp").reshape(seqs * count, width)
    scanned, states = scan_call(
        scan_body,
        "mamba_scan",
        grid,
        [spec["mine"], spec["row"], spec["row"], spec["sel"], spec["rate"], spec["carries"]],
        [spec["row"], spec["states"]],
        [row_shape, (count + 1, STATE, seqs, wide)],
        spec["two"],
        26,
        (mine, steps, conv_f, sel, rates, carries),
    )
    skip_f = padded(skip_gain.astype(f32), 0, wide)
    ssm_out = scanned + skip_f * conv_f
    gate_f = gate_in.astype(f32)
    gate_sig = jax.nn.sigmoid(gate_f)
    gate_act = gate_f * gate_sig
    mixer_mid = swapped((ssm_out * gate_act).astype(bf16)).reshape(seqs * count, wide)
    mixer_out_w = padded(w_mixer_out, 0, wide)
    mixer_proj = pair_scatter(
        by_rows(matmul(mixer_mid, mixer_out_w).astype(bf16)).reshape(seqs, count, width), 6
    )
    queries = matmul(normed_own, query_w).astype(bf16)
    meta_kv = matmul(meta_normed, keyval_w).astype(bf16)
    query_heads = queries.reshape(count, KV_HEADS, groups, HEAD)
    piece = keyvals_all.reshape(ctx_count * count, 2 * kv_width)
    joined = jnp.concatenate([meta_kv, piece], 0)
    keys = joined[:, :kv_width].reshape(-1, KV_HEADS, HEAD)
    values = joined[:, kv_width:].reshape(-1, KV_HEADS, HEAD)
    key_pos = jnp.arange(piece.shape[0], dtype=jnp.int32)
    key_doc = doc_number(key_pos, bounds)
    shown = (key_pos[None, :] <= positions[:, None]) & (key_doc[None, :] == docs[:, None])
    shown = jnp.concatenate([jnp.full((count, META), True), shown], 1)
    scores = (
        jnp.einsum("qgha,kga->ghqk", query_heads, keys, preferred_element_type=f32) * 0.125
    )
    scores = jnp.where(shown[None, None], scores, NEG)
    top = jnp.max(scores, axis=-1, keepdims=True)
    weights = jnp.exp(scores - top)
    weights = weights / jnp.sum(weights, axis=-1, keepdims=True)
    attn_heads_f = jnp.einsum(
        "ghqk,kga->qgha", weights.astype(bf16), values, preferred_element_type=f32
    )
    attn_b = attn_heads_f.reshape(count, HEADS * HEAD).astype(bf16)
    attn_proj = matmul(attn_b, attn_out_w)
    attn_branch, attn_scale = norm_rows(attn_proj, attn_norm_f)

    ssm_branch, ssm_scale = norm_rows(mixer_proj, ssm_norm_f)
    middle = hidden_in + 0.5 * (attn_branch + ssm_branch)

    normed_two_f, scale_two = norm_rows(middle, ffn_gain_f)
    normed_two = pair_gather(normed_two_f.astype(bf16), 7).reshape(seqs * count, width)
    gate_up = matmul(normed_two, ff_w).astype(bf16)
    gate_v, up_v = gate_up[:, :ff_wide].astype(f32), gate_up[:, ff_wide:].astype(f32)
    ffn_sig = jax.nn.sigmoid(gate_v)
    hidden_ff = (gate_v * ffn_sig * up_v).astype(bf16)
    down_w = padded(w_down, 0, ff_wide)
    output = by_rows(matmul(hidden_ff, down_w).astype(bf16))

    output = exchanged(output.reshape(seqs, count, width)).astype(f32)
    block_out = (middle + jnp.sum(output, axis=0)).astype(bf16)[None]
    down_back = tmatmul(hidden_ff, out_back_all)[:ff_cols]
    hidden_back = matmul_t(out_back_all, down_w).astype(bf16).astype(f32)
    up_back = hidden_back * gate_v * ffn_sig
    gate_back = hidden_back * up_v * ffn_sig * (1.0 + gate_v * (1.0 - ffn_sig))
    gate_up_back = jnp.concatenate([gate_back.astype(bf16), up_back.astype(bf16)], 1)
    ff_w_back = tmatmul(normed_two, gate_up_back)
    normed_two_back = matmul_t(gate_up_back, ff_w).astype(bf16)
    down_back = down_back.astype(bf16)
    ff_w_back = ff_w_back.astype(bf16)
    ff_w_sum = lax.psum(ff_w_back, "ctx")
    normed_two_back = by_rows(relayed(normed_two_back, ff_w_back, 2))
    normed_two_back = pair_scatter(normed_two_back.reshape(seqs, count, width), 8)
    middle_norm_back, ffn_gain_back = norm_back(middle, scale_two, ffn_gain_f, normed_two_back)
    middle_back = cotangent[0].astype(f32) + middle_norm_back
    branch_back = 0.5 * middle_back
    ssm_proj_back, ssm_gain_back = norm_back(mixer_proj, ssm_scale, ssm_norm_f, branch_back)
    attn_proj_back, attn_gain_back = norm_back(attn_proj, attn_scale, attn_norm_f, branch_back)
    attn_own_back = attn_proj_back.astype(bf16)
    proj_back, attn_cols = pair_gather(
        jnp.concatenate([ssm_proj_back.astype(bf16), attn_own_back], 0),
        9,
        [columns(attn_b, seqs)],
    )
    attn_cols = attn_cols.reshape(seqs * count, -1)
    ssm_proj_back = proj_back[:, :count].reshape(seqs * count, width)
    attn_proj_back = proj_back[:, count:].reshape(seqs * count, width)

    mixer_out_back = tmatmul(mixer_mid, ssm_proj_back)[:inner].astype(bf16)
    attn_out_back = tmatmul(attn_cols, attn_proj_back).astype(bf16)
    mid_back = matmul_t(ssm_proj_back, mixer_out_w).astype(bf16).reshape(seqs, count, wide)
    mid_back = swapped(mid_back).astype(f32)
    ssm_back = mid_back * gate_act
    gate_in_back = mid_back * ssm_out * gate_sig * (1.0 + gate_f * (1.0 - gate_sig))
    skip_back = jnp.sum(ssm_back * conv_f, axis=(0, 1))
    (leave,) = scan_call(
        carry_back_body,
        "mamba_carry_back",
        grid,
        [spec["row"], spec["sel"], spec["rate"], spec["row"]],
        [spec["leave"]],
        [(STATE, seqs, wide)],
        spec["one"],
        15,
        (steps, sel, rates, ssm_back),
    )
    heads_back = matmul_t(attn_own_back, attn_out_w).astype(bf16)
    heads_back = heads_back.reshape(count, KV_HEADS, groups, HEAD)
    delta = jnp.sum(heads_back.astype(f32) * attn_heads_f, axis=-1)
    delta = delta.transpose(1, 2, 0)[..., None]
    weights_back = jnp.einsum("qgha,kga->ghqk", heads_back, values, preferred_element_type=f32)
    scores_back = (weights * (weights_back - delta)).astype(bf16)
    query_back = (
        jnp.einsum("ghqk,kga->qgha", scores_back, keys, preferred_element_type=f32) * 0.125
    )
    keys_back = (
        jnp.einsum("ghqk,qgha->kga", scores_back, query_heads, preferred_element_type=f32) * 0.125
    )
    values_back = jnp.einsum(
        "ghqk,qgha->kga", weights.astype(bf16), heads_back, preferred_element_type=f32
    )
    kv_back = jnp.concatenate(
        [keys_back.reshape(-1, kv_width), values_back.reshape(-1, kv_width)], 1
    )
    buffer = kv_back[META:].astype(bf16).reshape(ctx_count, count, 2 * kv_width)
    meta_kv_own = kv_back[:META].astype(bf16)
    query_back = query_back.reshape(count, HEADS * HEAD).astype(bf16)
    (leaves,) = direct_many([leave.astype(bf16)], ["gather"], "ctx", 5)
    owned = lax.all_to_all(buffer, "ctx", 0, 0)
    owned = jnp.sum(owned.astype(f32), axis=0).astype(bf16)
    kv_own = owned
    attn_normed_back = matmul_t(query_back, query_w) + matmul_t(kv_own, keyval_w)
    meta_normed_back = matmul_t(meta_kv_own, keyval_w)
    qkv_back, meta_kv_back = direct_many(
        [
            jnp.concatenate([columns(query_back, seqs), columns(kv_own, seqs)], 2),
            columns(meta_kv_own, seqs),
        ],
        ["swap"] * 2,
        "fsdp",
        12,
    )
    qkv_back = qkv_back.reshape(seqs * count, -1)
    meta_kv_back = jnp.sum(meta_kv_back.astype(f32), axis=0).astype(bf16)
    second = after((down_back, mixer_out_back, attn_out_back), ff_w_sum, qkv_back)
    token = relayed(jnp.zeros((ROWS, LANES), f32), after(second[0], *second[1:]), 1)
    second = lax.psum(second, "ctx")
    down_back, mixer_out_back, attn_out_back = [part.astype(f32) for part in second]
    leaves = after(leaves.astype(f32), token)
    steps_back, conv_back, sel_back, rates_back = scan_call(
        scan_back_body,
        "mamba_scan_back",
        grid,
        [
            spec["mine"],
            spec["row"],
            spec["row"],
            spec["sel"],
            spec["rate"],
            spec["row"],
            spec["states"],
            spec["span"],
            spec["leaves"],
        ],
        [spec["row"], spec["row"], spec["sel"], spec["rates"]],
        [row_shape, row_shape, (count, seqs, LANES), (seqs // ROWS, STATE, wide)],
        spec["four"],
        47,
        (mine, steps, conv_f, sel, rates, ssm_back, states, carries[:, STATE], leaves),
    )
    rates_log_back = jnp.sum(rates_back, axis=0) * rates
    step_pre_back = steps_back * jax.nn.sigmoid(step_pre)
    step_shift_back = jnp.sum(step_pre_back, axis=(0, 1))
    step_pre_back = step_pre_back.astype(bf16).reshape(count * seqs, wide)
    step_w_back = tmatmul(step_low, step_pre_back)
    selected_back = jnp.concatenate(
        [
            matmul_t(step_pre_back, step_w),
            sel_back[:, :, : 2 * STATE].reshape(count * seqs, 2 * STATE),
        ],
        1,
    ).astype(bf16)
    selected_back = direct_sum(selected_back.reshape(seqs, count, -1), 10)
    selected_back = selected_back.reshape(count * seqs, -1)
    select_w_back = tmatmul(selected_back, conv_rows)[:, :inner]
    conv_back = (
        conv_back
        + skip_f * ssm_back
        + matmul_t(selected_back, select_w).reshape(count, seqs, wide)
    )
    pre_back = conv_back * conv_sig * (1.0 + pre_conv * (1.0 - conv_sig))
    taps_bias_back = jnp.sum(pre_back, axis=(0, 1))
    tap_rows = []
    extended_back = jnp.zeros((count + CONV - 1, seqs, wide), f32)
    for tap in range(CONV):
        masked_back = pre_back * valid_rows[tap]
        tap_rows.append(jnp.sum(masked_back * extended[tap : tap + count], axis=(0, 1)))
        extended_back = extended_back + jnp.pad(
            taps_f[tap] * masked_back, ((tap, CONV - 1 - tap), (0, 0), (0, 0))
        )
    rim_back = shifted(extended_back[: CONV - 1].astype(bf16), "ctx", -1).astype(f32)
    conv_in_back = extended_back[CONV - 1 :] + jnp.pad(
        rim_back, ((count - (CONV - 1), 0), (0, 0), (0, 0))
    )
    conv_in_back = swapped(conv_in_back.astype(bf16)).reshape(seqs * count, wide)
    gate_in_back = swapped(gate_in_back.astype(bf16)).reshape(seqs * count, wide)

    thin = jnp.concatenate(
        [
            tap_rows[0][None],
            tap_rows[1][None],
            tap_rows[2][None],
            tap_rows[3][None],
            taps_bias_back[None],
            step_shift_back[None],
            skip_back[None],
            rates_log_back,
            step_w_back,
        ],
        0,
    )[:, :inner]
    q_cols = w_query.shape[1] // seqs
    in_cols = 2 * inner + qkv_back.shape[1]
    thin_rows = thin.shape[0]
    few_rows = -(-(thin_rows + select_w_back.shape[0]) // LANES) * LANES
    share_cols = few_rows // (width // inner)
    in_wide = -(-(in_cols + share_cols) // LANES) * LANES
    in_back = padded(
        jnp.concatenate([conv_in_back[:, :inner], gate_in_back[:, :inner], qkv_back], 1),
        1,
        in_wide,
    )
    few = padded(jnp.concatenate([thin, select_w_back], 0), 0, few_rows).T
    few = few.reshape(inner, width // inner, share_cols).swapaxes(0, 1).reshape(width, share_cols)
    beside = jnp.concatenate([tmatmul(meta_normed, meta_kv_back), few], 1)
    in_w_back = tmatmul(normed, in_back) + jnp.pad(
        beside, ((0, 0), (2 * inner + q_cols, in_wide - in_cols - share_cols))
    )
    in_w_back = in_w_back.astype(bf16)
    part = by_rows(matmul_t(conv_in_back, conv_w) + matmul_t(gate_in_back, gate_w))
    tokens_scale = lax.rsqrt(jnp.mean(tokens_all * tokens_all, axis=-1, keepdims=True) + EPS)
    meta_all_scale = lax.rsqrt(jnp.mean(meta_all * meta_all, axis=-1, keepdims=True) + EPS)
    gain_back = (
        jnp.sum(part * tokens_all * tokens_scale, axis=0)
        + jnp.sum(attn_normed_back * hidden_in * scale_one, axis=0)
        + jnp.sum(meta_normed_back * meta_all * meta_all_scale, axis=0)
    )
    gains_back = jnp.stack([gain_back, attn_gain_back, ssm_gain_back, ffn_gain_back])
    gains_back = gains_back.astype(bf16).reshape(4, seqs, share).swapaxes(0, 1)
    tail = jnp.concatenate(
        [
            meta_normed_back.astype(bf16).reshape(seqs, meta_rows, width),
            padded(gains_back.reshape(seqs, 1, 4 * share), 2, width),
        ],
        1,
    )
    totals = pair_scatter(
        jnp.concatenate(
            [
                part.astype(bf16).reshape(seqs, count, width),
                padded(tail, 1, extra_rows),
            ],
            1,
        ),
        11,
    )
    input_norm_back, _ = norm_back(
        hidden_in, scale_one, gain_f, totals[:count] + attn_normed_back
    )
    first = count
    meta_back, _ = norm_back(meta_f, meta_scale, gain_f, totals[first : first + meta_rows])
    gains_back = totals[first + meta_rows, : 4 * share]
    grad_tokens = (middle_back + input_norm_back)[None]

    small = jnp.concatenate([meta_back, padded(gains_back, 0, width)[None]], 0)
    small = padded(small.astype(bf16), 0, extra_rows)
    spare = in_cols // LANES * LANES
    in_w_back, few, small = finish(
        in_w_back.reshape(seqs, share, in_wide), [small], spare, 13
    )
    few = few.reshape(width, in_wide - spare)[:, in_cols - spare : in_cols - spare + share_cols]
    few = few.reshape(width // inner, inner, share_cols).swapaxes(0, 1).reshape(inner, few_rows)
    few = few.astype(f32)
    select_w_back = few[:, thin_rows : thin_rows + select_w_back.shape[0]]
    thin = few[:, :thin_rows].T
    small = jnp.sum(small.astype(f32), axis=0)
    meta_back = small[:meta_rows]
    gains = small[meta_rows, : 4 * share].reshape(4, share)

    (grad_gate_up,) = join_columns(
        exchanged(ff_w_sum.reshape(seqs, share, 2 * ff_wide)),
        [[(0, ff_cols), (ff_wide, ff_cols)]],
    )
    first = 2 * inner
    grad_mixer_in, grad_query, grad_keyval = join_columns(
        in_w_back,
        [
            [(0, inner), (inner, inner)],
            [(first, q_cols)],
            [(first + q_cols, in_cols - first - q_cols)],
        ],
    )
    return (
        block_out,
        grad_tokens,
        meta_back,
        gains[0],
        grad_query,
        grad_keyval,
        attn_out_back,
        grad_mixer_in,
        thin[:CONV],
        thin[CONV],
        select_w_back,
        thin[CONV + 3 + STATE : CONV + 3 + STATE + DT_RANK],
        thin[CONV + 1],
        thin[CONV + 3 : CONV + 3 + STATE],
        thin[CONV + 2],
        mixer_out_back,
        gains[1],
        gains[2],
        gains[3],
        grad_gate_up,
        down_back,
    )


def solution(mesh):
    rows, cols, one = P("fsdp", None), P(None, "fsdp"), P("fsdp")
    split = P("fsdp", "ctx", None)
    in_specs = (
        split,
        split,
        rows,
        rows,
        one,
        rows,
        rows,
        rows,
        rows,
        cols,
        one,
        rows,
        cols,
        one,
        cols,
        one,
        rows,
        one,
        one,
        one,
        rows,
        rows,
    )
    out_specs = (
        split,
        split,
        rows,
        one,
        rows,
        rows,
        rows,
        rows,
        cols,
        one,
        rows,
        cols,
        one,
        cols,
        one,
        rows,
        one,
        one,
        one,
        rows,
        rows,
    )
    return jax.shard_map(shards, mesh=mesh, in_specs=in_specs, out_specs=out_specs, check_vma=False)
```
